256 devices in a mesh: blk: 64 (over z, y, x_hi), rep: 4 (over x_lo, core).
Axes of the slice: x: 4 (x_hi: 2, x_lo: 2; x = x_hi * 2 + x_lo), y: 4, z: 8, core: 2. Of those that a mesh axis runs over, the one named last changes fastest.
Arguments:
- entities: float32 [131072, 256], P('blk'), may hold values from -3 to 3
- entity_acc: float32 [131072], P('blk'), may hold values from 0.001 to 1
- relations: float32 [2048, 256], replicated, may hold values from -6 to 6
- relation_acc: float32 [2048], replicated, may hold values from 0.1 to 10
- src_ids: int32 [64, 4096], P('blk', 'rep'), may hold values from 0 to 2047
- rel_ids: int32 [64, 4096], P('blk', 'rep'), may hold values from 0 to 2047
- dst_ids: int32 [64, 4096], P('blk', 'rep'), may hold values from 0 to 2047
- neg_ids: int32 [64, 16384], P('blk', 'rep'), may hold values from 0 to 2047
- counts: int32 [64, 4], P('blk', 'rep'), may hold values from 512 to 1024, as said below
Outputs:
- new_entities: float32 [131072, 256], P('blk')
- new_entity_acc: float32 [131072], P('blk')
- new_relations: float32 [2048, 256], replicated
- new_relation_acc: float32 [2048], replicated
The draws below stay inside these ranges and needn't reach their ends.
Inputs may be any that keep to these rules, and one draw needn't show every extreme that they name: `counts`: every count lies between 512 and 1024; some bucket and replica row is full in every draw, at a place drawn from the seed.
All inputs are finite; a program needn't handle non-finite values.
Results may differ from the reference program's by a relative error of at most 0.0011.
Values may be sent and summed in bfloat16 or wider, within the bound.
No kernel may reach another device: no remote copies, remote signals or barrier semaphores. Data moves between devices by JAX's collectives and lax.ppermute only.
A program may use at most 64 MiB of HBM per device.

```python
import math
import jax
import jax.numpy as jnp
import numpy as np
from jax import lax

D = 256
ENT_DEV = 2048
E_DEV = 1024
GROUP = 256
NEG = 1024
NREL = 2048
NPART = 64
NENT = 131072
GROUPS = 4
N_REP = 4


def draw_counts(key, part):
    key = jax.random.fold_in(key, 7)
    first, second = jax.random.split(key)
    values = jax.random.randint(first, (NPART * N_REP,), E_DEV // 2, E_DEV + 1, dtype=jnp.int32)
    chosen = jax.random.randint(second, (), 0, NPART * N_REP, dtype=jnp.int32)
    values = jnp.where(jnp.arange(NPART * N_REP, dtype=jnp.int32) == chosen, E_DEV, values)
    return values.reshape(NPART, N_REP)


def plant(drawn, own_key, low, high):
    index_at = [jax.random.randint(jax.random.fold_in(own_key, axis), (), 0, length) for axis, length in enumerate(drawn.shape)]
    main_axis = drawn.shape.index(max(drawn.shape))
    next_to = index_at[:main_axis] + [(index_at[main_axis] + 1) % drawn.shape[main_axis]] + index_at[main_axis + 1:]
    return drawn.at[tuple(index_at)].set(low).at[tuple(next_to)].set(high)


def block_scale(own_key, shape, cuts, least, high):
    factor_of = 1.0
    for position, shards_of in cuts:
        heights = jax.random.uniform(jax.random.fold_in(jax.random.fold_in(own_key, 6), position), (shards_of,), jnp.float32, least / len(cuts), high / len(cuts))
        factor_of = factor_of * jnp.repeat(jnp.exp(heights), shape[position] // shards_of).reshape((-1,) + (1,) * (len(shape) - 1 - position))
    return factor_of


def cumulative_ranks(amount, slope):
    loads = [(1 << 20) // math.isqrt(standing ** slope) + 1 for standing in range(1, amount + 1)]
    scale = 1 + sum(loads) // (1 << 30)
    return np.cumsum(np.array([max(1, weight // scale) for weight in loads]))


def skewed_ids(stream_key, dims, count, skew):
    table = cumulative_ranks(count, skew)
    lot = jax.random.randint(jax.random.fold_in(stream_key, 1), dims, 0, int(table[count - 1]))
    grade = jnp.searchsorted(jnp.asarray(table, jnp.int32), lot, side="right")
    return jax.random.permutation(jax.random.fold_in(stream_key, 2), count)[grade].astype(jnp.int32)


def normal_values(rng, shape, deviation, most, cuts=(), held_as=jnp.bfloat16):
    array = deviation * jax.random.normal(rng, shape, jnp.float32)
    if cuts:
        array = array * block_scale(rng, shape, cuts, -0.22, 0.18)
    return jnp.clip(array, -most, most).astype(held_as)


def setup_inputs(seed: int = 0) -> dict:
    arg_keys = jax.random.split(jax.random.key(seed), 10)
    entities = normal_values(arg_keys[0], (NENT, D), 0.5, 3.0, ((0, 64),), jnp.float32)
    entity_acc = jnp.clip(jnp.exp(math.log(1.0) - 6.9077552 * jax.random.uniform(arg_keys[1], (NENT,), jnp.float32) ** block_scale(arg_keys[1], (NENT,), ((0, 64),), -0.2, 0.2)), 0.001, 1.0)
    relations = normal_values(arg_keys[2], (NREL, D), 1.0, 6.0, (), jnp.float32)
    relation_acc = jnp.clip(jnp.exp(jax.random.uniform(arg_keys[3], (NREL,), jnp.float32, math.log(0.1), math.log(10.0))), 0.1, 10.0)
    src_ids = plant(skewed_ids(arg_keys[4], (NPART, N_REP * E_DEV), ENT_DEV, 2), jax.random.fold_in(arg_keys[4], 3), 0, ENT_DEV - 1).astype(jnp.int32)
    rel_ids = plant(skewed_ids(arg_keys[5], (NPART, N_REP * E_DEV), NREL, 2), jax.random.fold_in(arg_keys[5], 3), 0, NREL - 1).astype(jnp.int32)
    dst_ids = plant(skewed_ids(arg_keys[6], (NPART, N_REP * E_DEV), ENT_DEV, 2), jax.random.fold_in(arg_keys[6], 3), 0, ENT_DEV - 1).astype(jnp.int32)
    neg_ids = plant(jax.random.randint(arg_keys[7], (NPART, N_REP * GROUPS * NEG), 0, ENT_DEV), jax.random.fold_in(arg_keys[7], 1), 0, ENT_DEV - 1).astype(jnp.int32)
    counts = draw_counts(jax.random.fold_in(arg_keys[9], 71), 0)
    return {"entities": entities, "entity_acc": entity_acc, "relations": relations, "relation_acc": relation_acc, "src_ids": src_ids, "rel_ids": rel_ids, "dst_ids": dst_ids, "neg_ids": neg_ids, "counts": counts}


entity_rate = 0.1
relation_rate = 0.1

def complex_mul(left, right):
    half = left.shape[1] // 2
    left_real, left_imag = (left[:, :half], left[:, half:])
    right_real, right_imag = (right[:, :half], right[:, half:])
    return jnp.concatenate([left_real * right_real - left_imag * right_imag, left_real * right_imag + left_imag * right_real], axis=1)

def conj_mul(grad, other):
    half = grad.shape[1] // 2
    grad_real, grad_imag = (grad[:, :half], grad[:, half:])
    other_real, other_imag = (other[:, :half], other[:, half:])
    return jnp.concatenate([grad_real * other_real + grad_imag * other_imag, -grad_real * other_imag + grad_imag * other_real], axis=1)

def bucket_terms(src_rows, dst_rows, relations, src_index, rel_index, dst_index, neg_index, edge_count):
    edges = src_index.shape[0]
    width = src_rows.shape[1]
    groups = edges // GROUP
    heads = jnp.take(src_rows, src_index, axis=0).astype(jnp.float32)
    tails = jnp.take(dst_rows, dst_index, axis=0).astype(jnp.float32)
    rel_rows = jnp.take(relations, rel_index, axis=0)
    product = complex_mul(heads, rel_rows)
    live_mask = (jnp.arange(edges, dtype=jnp.int32) < edge_count).astype(jnp.float32)
    positive = lax.optimization_barrier(jnp.sum(product * tails, axis=1))
    pos_coef = -live_mask * jax.nn.sigmoid(-positive)
    product_low = lax.optimization_barrier(product.astype(jnp.bfloat16))
    product_low = product_low.astype(jnp.float32).reshape(groups, GROUP, width)
    negatives = jnp.take(dst_rows, neg_index, axis=0).astype(jnp.float32).reshape(groups, NEG, width)
    neg_scores = jnp.einsum('cid,cnd->cin', product_low, negatives)
    neg_coef = live_mask.reshape(groups, GROUP, 1) * jax.nn.sigmoid(neg_scores) / NEG
    neg_coef = lax.optimization_barrier(neg_coef.astype(jnp.bfloat16)).astype(jnp.float32)
    grad_product = pos_coef[:, None] * tails + jnp.einsum('cin,cnd->cid', neg_coef, negatives).reshape(edges, width)
    grad_neg = jnp.einsum('cin,cid->cnd', neg_coef, product_low).reshape(groups * NEG, width)
    rows = src_rows.shape[0]
    dst_grad = jnp.zeros((rows, width), jnp.float32).at[dst_index].add(pos_coef[:, None] * product)
    dst_grad = dst_grad.at[neg_index].add(grad_neg)
    src_grad = jnp.zeros((rows, width), jnp.float32).at[src_index].add(conj_mul(grad_product, rel_rows))
    rel_grad = jnp.zeros((relations.shape[0], width), jnp.float32).at[rel_index].add(conj_mul(grad_product, heads))
    return (src_grad, dst_grad, rel_grad)

def adagrad_rows(rows, accum, grad, rate):
    new_accum = accum + lax.optimization_barrier(jnp.mean(grad * grad, axis=1))
    return (rows - rate * grad / jnp.sqrt(new_accum)[:, None], new_accum)

def reference(entities, entity_acc, relations, relation_acc, src_ids, rel_ids, dst_ids, neg_ids, counts):
    parts = counts.shape[0]
    reps = counts.shape[1]
    rows = entities.shape[0] // parts
    width = entities.shape[1]
    edges = src_ids.shape[1] // reps
    neg_width = neg_ids.shape[1] // reps
    low = entities.astype(jnp.bfloat16)

    def step(carry, bucket):
        ent_grad, rel_total = carry
        part_index = (bucket // reps).astype(jnp.int32)
        rep_index = (bucket % reps).astype(jnp.int32)
        next_index = ((part_index + 1) % parts).astype(jnp.int32)
        zero = jnp.zeros((), jnp.int32)
        src_rows = lax.dynamic_slice_in_dim(low, part_index * rows, rows, 0)
        dst_rows = lax.dynamic_slice_in_dim(low, next_index * rows, rows, 0)
        src_index = lax.dynamic_slice(src_ids, (part_index, rep_index * edges), (1, edges))[0]
        rel_index = lax.dynamic_slice(rel_ids, (part_index, rep_index * edges), (1, edges))[0]
        dst_index = lax.dynamic_slice(dst_ids, (part_index, rep_index * edges), (1, edges))[0]
        neg_index = lax.dynamic_slice(neg_ids, (part_index, rep_index * neg_width), (1, neg_width))[0]
        edge_count = lax.dynamic_slice(counts, (part_index, rep_index), (1, 1))[0, 0]
        src_grad, dst_grad, rel_grad = bucket_terms(src_rows, dst_rows, relations, src_index, rel_index, dst_index, neg_index, edge_count)
        current = lax.dynamic_slice(ent_grad, (part_index * rows, zero), (rows, width))
        ent_grad = lax.dynamic_update_slice(ent_grad, current + src_grad, (part_index * rows, zero))
        current = lax.dynamic_slice(ent_grad, (next_index * rows, zero), (rows, width))
        ent_grad = lax.dynamic_update_slice(ent_grad, current + dst_grad, (next_index * rows, zero))
        return ((ent_grad, rel_total + rel_grad), None)
    start = (jnp.zeros(entities.shape, jnp.float32), jnp.zeros(relations.shape, jnp.float32))
    (ent_grad, rel_total), _ = lax.scan(step, start, jnp.arange(parts * reps, dtype=jnp.int32))
    new_entities, new_entity_acc = adagrad_rows(entities, entity_acc, ent_grad, entity_rate)
    new_relations, new_relation_acc = adagrad_rows(relations, relation_acc, rel_total, relation_rate)
    return (new_entities, new_entity_acc, new_relations, new_relation_acc)
```

```python
import functools

import jax
import jax.numpy as jnp
from jax import lax
from jax.experimental import pallas as pl
from jax.experimental.pallas import tpu as pltpu
from jax.sharding import PartitionSpec as P

F32 = jnp.float32
BF16 = jnp.bfloat16
D = 256
H = 128
ENT = 2048
EDGES = 1024
GROUP = 256
NEG = 1024
NREL = 2048
RATE = 0.1
AXES = ("blk", "rep")
VMEM_LIMIT = 48 * 1024 * 1024
CHUNK = 256


def vmem():
    return pl.BlockSpec(memory_space=pltpu.VMEM)


def smem():
    return pl.BlockSpec(memory_space=pltpu.SMEM)


def call(kernel, out_shape, n_smem, n_vmem, scratch=(), flops=0, bytes_accessed=0):
    return pl.pallas_call(
        kernel,
        out_shape=out_shape,
        in_specs=[smem()] * n_smem + [vmem()] * n_vmem,
        out_specs=jax.tree.map(lambda _: vmem(), out_shape),
        scratch_shapes=list(scratch),
        cost_estimate=pl.CostEstimate(
            flops=flops, bytes_accessed=bytes_accessed, transcendentals=0
        ),
        compiler_params=pltpu.CompilerParams(vmem_limit_bytes=VMEM_LIMIT),
    )


def columns(row):
    n = row.shape[1]
    parts = [
        jnp.transpose(jnp.broadcast_to(row[:, i : i + H], (H, H))) for i in range(0, n, H)
    ]
    return parts[0] if len(parts) == 1 else jnp.concatenate(parts, axis=0)


def one_hot_rows(col, n, base=0):
    e = col.shape[0]
    lane = lax.broadcasted_iota(jnp.int32, (e, H), 1)
    parts = [jnp.where(col == lane + (base + j), 1.0, 0.0).astype(BF16) for j in range(0, n, H)]
    return jnp.concatenate(parts, axis=1)


def one_hot_cols(row, n, base):
    e = row.shape[1]
    sub = lax.broadcasted_iota(jnp.int32, (n, e), 0) + base
    return jnp.where(jnp.broadcast_to(row, (n, e)) == sub, 1.0, 0.0).astype(BF16)


def dot(a, b):
    return jnp.dot(a, b, preferred_element_type=F32)


def dot_nt(a, b):
    return lax.dot_general(a, b, (((1,), (1,)), ((), ())), preferred_element_type=F32)


def gather_kernel(ids_ref, negs_ref, low_ref, rel_ref, head_ref, relrow_ref, prod_ref, cnt_ref, hi_ref, mid_ref, lo_ref):
    for r in range(0, NREL, 256):
        x = rel_ref[r : r + 256, :]
        for ref in (hi_ref, mid_ref, lo_ref):
            part = x.astype(BF16)
            ref[r : r + 256, :] = part
            x = x - part.astype(F32)

    def group(g, _):
        rows = pl.ds(pl.multiple_of(g * GROUP, GROUP), GROUP)
        src = columns(ids_ref[0:1, rows])
        heads = dot(one_hot_rows(src, ENT), low_ref[...])
        pick = one_hot_rows(columns(ids_ref[1:2, rows]), NREL)
        rel = dot(pick, hi_ref[...]) + dot(pick, mid_ref[...]) + dot(pick, lo_ref[...])
        hr, hi, rr, ri = heads[:, :H], heads[:, H:], rel[:, :H], rel[:, H:]
        head_ref[rows, :] = heads.astype(BF16)
        relrow_ref[rows, :] = rel
        prod_ref[rows, :H] = hr * rr - hi * ri
        prod_ref[rows, H:] = hr * ri + hi * rr
        negs = negs_ref[pl.ds(g, 1), :]
        high = one_hot_cols(lax.shift_right_logical(negs, 7), ENT // H, 0)
        low = one_hot_cols(lax.bitwise_and(negs, H - 1), H, 0)
        cnt_ref[g] = dot_nt(high, low) * (1.0 / NEG)
        return 0

    lax.fori_loop(0, EDGES // GROUP, group, 0)


def score_kernel(
    count_ref,
    ids_ref,
    near_ref,
    far_ref,
    head_ref,
    relrow_ref,
    prod_ref,
    cnt_ref,
    keep_ref,
    send_ref,
    cc_ref,
    plt_ref,
    pd_ref,
    gh_ref,
    gr_ref,
):
    half = ENT // 2
    count = count_ref[0, 0]

    def group(g, _):
        rows = pl.ds(pl.multiple_of(g * GROUP, GROUP), GROUP)
        dst = columns(ids_ref[2:3, rows])
        tails = dot(one_hot_rows(dst, half), near_ref[...]) + dot(
            one_hot_rows(dst, half, half), far_ref[...]
        )
        prod = prod_ref[rows, :]
        edge = lax.broadcasted_iota(jnp.int32, (GROUP, 1), 0) + g * GROUP
        live = jnp.where(edge < count, 1.0, 0.0).astype(F32)
        positive = jnp.sum(prod * tails, axis=1, keepdims=True)
        pos = -live * jax.nn.sigmoid(-positive)
        low = prod.astype(BF16)
        for j, table in ((0, near_ref), (1, far_ref)):
            scores = dot_nt(low, table[...])
            for i in range(half // H):
                w = cnt_ref[g, pl.ds(j * (half // H) + i, 1), :]
                part = scores[:, i * H : (i + 1) * H]
                cc_ref[rows, j * half + i * H : j * half + (i + 1) * H] = (
                    jax.nn.sigmoid(part) * w
                ).astype(BF16)
        neg = dot(cc_ref[rows, :half], near_ref[...]) + dot(cc_ref[rows, half:], far_ref[...])
        grad = pos * tails + live * neg
        rel = relrow_ref[rows, :]
        head = head_ref[rows, :].astype(F32)
        gr, gi = grad[:, :H], grad[:, H:]
        for out, other in ((gh_ref, rel), (gr_ref, head)):
            a, b = other[:, :H], other[:, H:]
            out[rows, :H] = (gr * a + gi * b).astype(BF16)
            out[rows, H:] = (gi * a - gr * b).astype(BF16)
        pd_ref[rows, :] = (pos * prod).astype(BF16)
        plt_ref[:, rows] = jnp.transpose(live * prod).astype(BF16)
        return 0

    lax.fori_loop(0, EDGES // GROUP, group, 0)

    def scatter(i, _):
        rows = pl.ds(pl.multiple_of(i * CHUNK, CHUNK), CHUNK)
        keep_ref[rows, :] = dot(one_hot_cols(ids_ref[3:4, :], CHUNK, i * CHUNK), gr_ref[...])
        send_ref[rows, :] = dot(
            one_hot_cols(ids_ref[3:4, :], CHUNK, half + i * CHUNK), gr_ref[...]
        ).astype(BF16)
        return 0

    lax.fori_loop(0, half // CHUNK, scatter, 0)


def scatter_kernel(
    place_ref,
    ids_ref,
    cc_ref,
    plt_ref,
    pd_ref,
    gh_ref,
    src_keep_ref,
    src_send_ref,
    dst_keep_ref,
    dst_send_ref,
):
    half = ENT // 2
    xl = place_ref[0]

    def scatter(i, _):
        rows = pl.ds(pl.multiple_of(i * CHUNK, CHUNK), CHUNK)
        to = lax.bitwise_xor(i, xl * (half // 2 // CHUNK))
        out = pl.ds(pl.multiple_of(to * CHUNK, CHUNK), CHUNK)
        for base, src_ref, dst_ref in (
            (0, src_keep_ref, dst_keep_ref),
            (half, src_send_ref, dst_send_ref),
        ):
            src = dot(one_hot_cols(ids_ref[4:5, :], CHUNK, base + i * CHUNK), gh_ref[...])
            src_ref[rows, :] = src.astype(src_ref.dtype)
            cols = pl.ds(pl.multiple_of(base + i * CHUNK, CHUNK), CHUNK)
            drawn = jnp.transpose(dot(plt_ref[...], cc_ref[:, cols]))
            dst = dot(one_hot_cols(ids_ref[2:3, :], CHUNK, base + i * CHUNK), pd_ref[...])
            dst_ref[out, :] = (drawn + dst).astype(dst_ref.dtype)
        return 0

    lax.fori_loop(0, half // CHUNK, scatter, 0)


def add_split_kernel(n_in, n_out, *refs):
    ins, outs = refs[:n_in], refs[n_in:]
    size = outs[0].shape[0]
    step = min(size, 64)
    for k, out in enumerate(outs):
        for r in range(0, size, step):
            total = ins[0][k * size + r : k * size + r + step, :].astype(F32)
            for ref in ins[1:]:
                total = total + ref[k * size + r : k * size + r + step, :].astype(F32)
            out[r : r + step, :] = total.astype(out.dtype)


def add_split(parts, n_out, own=BF16, sent=BF16):
    rows = parts[0].shape[0] // n_out
    shapes = [jax.ShapeDtypeStruct((rows, D), sent if k else own) for k in range(n_out)]
    return call(
        functools.partial(add_split_kernel, len(parts), n_out),
        shapes,
        0,
        len(parts),
        flops=len(parts) * n_out * rows * D,
        bytes_accessed=3 * len(parts) * n_out * rows * D,
    )(*parts)


def split3(x):
    hi = x.astype(BF16).astype(F32)
    mid = (x - hi).astype(BF16).astype(F32)
    return hi, mid, x - hi - mid


def sum_with_means_kernel(place_ref, *refs):
    parts, out_ref = refs[:-1], refs[-1]
    rows = parts[0].shape[0]
    step = min(rows, H)
    means = []
    for r in range(0, rows, step):
        terms = [ref[r : r + step, :].astype(F32) for ref in parts]
        if len(terms) == 8:
            z = place_ref[0]
            for bit in (1, 2, 4):
                flip = lax.bitwise_and(z, bit) != 0
                terms = [jnp.where(flip, terms[k ^ bit], terms[k]) for k in range(8)]
        total = terms[0]
        for term in terms[1:]:
            total = total + term
        out_ref[r : r + step, :] = total.astype(BF16)
        mean = jnp.sum(total * total, axis=1, keepdims=True) * (1.0 / D)
        mean = jnp.broadcast_to(mean, (step, H))
        if step < H:
            mean = jnp.concatenate([mean] * (H // step), axis=0)
        means.append(jnp.transpose(mean)[0:1, :])
    pad = jnp.zeros((8 - len(means), H), F32)
    hi, mid, lo = (jnp.concatenate([part, pad], axis=0) for part in split3(jnp.concatenate(means, axis=0)))
    top = jnp.concatenate([hi, mid], axis=1)
    bottom = jnp.concatenate([lo, jnp.zeros_like(lo)], axis=1)
    out_ref[rows : rows + 16, :] = jnp.concatenate([top, bottom], axis=0).astype(BF16)


def sum_with_means(parts, place=None):
    rows = parts[0].shape[0]
    place = jnp.zeros((1,), jnp.int32) if place is None else place.reshape(1)
    return call(
        sum_with_means_kernel,
        jax.ShapeDtypeStruct((rows + 16, D), BF16),
        1,
        len(parts),
        flops=len(parts) * rows * D,
        bytes_accessed=3 * len(parts) * rows * D,
    )(place, *parts)


def means_of(piece, start, row):
    tile = piece[pl.ds(pl.multiple_of(start, 16), 16), :].astype(F32)
    return tile[row : row + 1, :H] + tile[row : row + 1, H:] + tile[8 + row : 9 + row, :H]


def update_kernel(n_pieces, sub, place_ref, rows_ref, acc_ref, *refs):
    pieces, new_ref, new_acc_ref = refs[:n_pieces], refs[n_pieces], refs[n_pieces + 1]
    size = rows_ref.shape[0]
    i = pl.program_id(0)
    want = lax.bitwise_xor(i, place_ref[0])
    lane = lax.broadcasted_iota(jnp.int32, (1, H), 1)
    for k, piece in enumerate(pieces):

        @pl.when(want == k)
        def _(piece=piece):
            for r in range(0, size, H):
                if sub >= H:
                    g = piece[r : r + H, :].astype(F32)
                    mean = means_of(piece, size, r // H)
                else:
                    starts = [
                        lax.bitwise_xor(c // sub, place_ref[1]) * (sub + 16)
                        for c in range(r, r + H, sub)
                    ]
                    g = jnp.concatenate(
                        [
                            piece[pl.ds(pl.multiple_of(start, 16), sub), :].astype(F32)
                            for start in starts
                        ],
                        axis=0,
                    )
                    first, second = (means_of(piece, start + sub, 0) for start in starts)
                    mean = jnp.where(lane < sub, first, second)
                at = pl.ds(i * (size // H) + r // H, 1)
                acc = acc_ref[at, :] + mean
                new_acc_ref[at, :] = acc
                scale = jnp.transpose(jnp.broadcast_to(RATE / jnp.sqrt(acc), (H, H)))
                new_ref[r : r + H, :H] = rows_ref[r : r + H, :H] - g[:, :H] * scale
                new_ref[r : r + H, H:] = rows_ref[r : r + H, H:] - g[:, H:] * scale


def update(rows, acc, pieces, place, size, sub):
    n = rows.shape[0]
    whole = lambda i: (0, 0)
    new, new_acc = pl.pallas_call(
        functools.partial(update_kernel, len(pieces), sub),
        grid=(n // size,),
        out_shape=[
            jax.ShapeDtypeStruct((n, D), F32),
            jax.ShapeDtypeStruct((n // H, H), F32),
        ],
        in_specs=[
            smem(),
            pl.BlockSpec((size, D), lambda i: (i, 0)),
            pl.BlockSpec((n // H, H), whole),
        ]
        + [pl.BlockSpec(piece.shape, whole) for piece in pieces],
        out_specs=[
            pl.BlockSpec((size, D), lambda i: (i, 0)),
            pl.BlockSpec((n // H, H), whole),
        ],
        cost_estimate=pl.CostEstimate(flops=8 * n * D, bytes_accessed=10 * n * D, transcendentals=n),
        compiler_params=pltpu.CompilerParams(vmem_limit_bytes=VMEM_LIMIT),
    )(place, rows, acc.reshape(n // H, H), *pieces)
    return new, new_acc.reshape(n)


def swap(x, mask):
    return lax.ppermute(x, AXES, [(i, i ^ mask) for i in range(256)])


def shift(x, distance, mask):
    route = [(((i // 4 - distance) % 64) * 4 + ((i % 4) ^ mask), i) for i in range(256)]
    return lax.ppermute(x, AXES, route)


CORE, XL = 1, 2
X_MASKS = (2, 4, 6)
Y_MASKS = (8, 16, 24)
Z_MASKS = tuple(range(32, 256, 32))


def shards(
    entities, entity_acc, relations, relation_acc, src_ids, rel_ids, dst_ids, neg_ids, counts
):
    blk, rep = lax.axis_index("blk"), lax.axis_index("rep")
    core, xl = rep % 2, rep // 2
    x = (blk % 2) * 2 + xl
    y = (blk // 2) % 4

    low = entities.astype(BF16)
    half = lax.dynamic_slice_in_dim(entities, core * (ENT // 2), ENT // 2, 0).astype(BF16)
    near = shift(half, -1, XL)
    far = swap(near, CORE)

    ids = jnp.concatenate(
        [
            src_ids,
            rel_ids,
            dst_ids ^ (core * 1024),
            rel_ids ^ (core * 1024 + x * 256 + y * 64),
            src_ids ^ (core * 1024 + xl * 512),
            jnp.zeros((3, EDGES), jnp.int32),
        ],
        axis=0,
    )
    negs = (neg_ids ^ (core * 1024)).reshape(4, NEG)
    head, rel_rows, prod, cnt = call(
        gather_kernel,
        [
            jax.ShapeDtypeStruct((EDGES, D), BF16),
            jax.ShapeDtypeStruct((EDGES, D), F32),
            jax.ShapeDtypeStruct((EDGES, D), F32),
            jax.ShapeDtypeStruct((4, ENT // H, H), F32),
        ],
        0,
        4,
        [pltpu.VMEM((NREL, D), BF16)] * 3,
        flops=4 * 2 * EDGES * ENT * D,
        bytes_accessed=1 << 22,
    )(ids, negs, low, relations)

    kept = jax.ShapeDtypeStruct((ENT // 2, D), F32)
    sent = jax.ShapeDtypeStruct((ENT // 2, D), BF16)
    rel_keep, rel_send, cc, plt, pd, gh = call(
        score_kernel,
        [
            kept,
            sent,
            jax.ShapeDtypeStruct((EDGES, ENT), BF16),
            jax.ShapeDtypeStruct((D, EDGES), BF16),
            jax.ShapeDtypeStruct((EDGES, D), BF16),
            jax.ShapeDtypeStruct((EDGES, D), BF16),
        ],
        1,
        7,
        [pltpu.VMEM((EDGES, D), BF16)],
        flops=4 * 2 * EDGES * ENT * D,
        bytes_accessed=1 << 23,
    )(counts, ids, near, far, head, rel_rows, prod, cnt)
    src_keep, src_send, dst_keep, dst_send = call(
        scatter_kernel,
        [kept, sent, kept, sent],
        1,
        5,
        flops=3 * 2 * EDGES * ENT * D,
        bytes_accessed=1 << 23,
    )(xl.reshape(1), ids, cc, plt, pd, gh)

    rel_recv = swap(rel_send, CORE)
    parts = add_split([rel_keep, rel_recv], 4, own=F32)
    recv = [swap(part, mask) for part, mask in zip(parts[1:], X_MASKS)]
    src_recv = swap(src_send, CORE)
    dst_recv = swap(dst_send, CORE)
    src_own, src_away = add_split([src_keep, src_recv], 2, own=F32)
    dst_own, dst_away = add_split([dst_keep, dst_recv], 2)

    parts = add_split([parts[0], *recv], 4, own=F32)
    recv = [swap(part, mask) for part, mask in zip(parts[1:], Y_MASKS)]
    (mine,) = add_split([parts[0], *recv], 1)

    src_other = swap(src_away, XL)
    dst_first = shift(dst_own, 1, 0)
    dst_second = shift(dst_away, 1, XL)

    others = [swap(mine, mask) for mask in Z_MASKS]
    ent_own = sum_with_means([src_own, src_other, dst_first, dst_second])
    ent_xl = swap(ent_own, XL)
    ent_core = [swap(ent_own, CORE), swap(ent_xl, CORE)]
    place = jnp.stack([core * 2 + xl, jnp.zeros_like(core)])
    new_entities, new_entity_acc = update(
        entities, entity_acc, [ent_own, ent_xl, *ent_core], place, 512, 512
    )

    z = blk // 8
    total = sum_with_means([mine, *others], z)
    recv = [swap(total, mask) for mask in Y_MASKS]
    quarter = jnp.concatenate([total, *recv], axis=0)
    pieces = [quarter, *[swap(quarter, mask) for mask in X_MASKS]]
    pieces = pieces + [swap(piece, CORE) for piece in pieces]
    place = jnp.stack([core * 4 + x, y])
    new_relations, new_relation_acc = update(relations, relation_acc, pieces, place, 256, 64)
    return (new_entities, new_entity_acc, new_relations, new_relation_acc)


def solution(mesh):
    in_specs = (
        P("blk", None),
        P("blk"),
        P(),
        P(),
        P("blk", "rep"),
        P("blk", "rep"),
        P("blk", "rep"),
        P("blk", "rep"),
        P("blk", "rep"),
    )
    out_specs = (P("blk", None), P("blk"), P(), P())
    return jax.shard_map(shards, mesh=mesh, in_specs=in_specs, out_specs=out_specs, check_vma=False)
```

```python
import functools

import jax
import jax.numpy as jnp
from jax import lax
from jax.experimental import pallas as pl
from jax.experimental.pallas import tpu as pltpu
from jax.sharding import PartitionSpec as P

F32 = jnp.float32
BF16 = jnp.bfloat16
D = 256
H = 128
ENT = 2048
EDGES = 1024
GROUP = 256
NEG = 1024
NREL = 2048
RATE = 0.1
AXES = ("blk", "rep")
VMEM_LIMIT = 48 * 1024 * 1024
CHUNK = 256


def vmem():
    return pl.BlockSpec(memory_space=pltpu.VMEM)


def smem():
    return pl.BlockSpec(memory_space=pltpu.SMEM)


def call(kernel, out_shape, n_smem, n_vmem, scratch=(), flops=0, bytes_accessed=0):
    return pl.pallas_call(
        kernel,
        out_shape=out_shape,
        in_specs=[smem()] * n_smem + [vmem()] * n_vmem,
        out_specs=jax.tree.map(lambda _: vmem(), out_shape),
        scratch_shapes=list(scratch),
        cost_estimate=pl.CostEstimate(
            flops=flops, bytes_accessed=bytes_accessed, transcendentals=0
        ),
        compiler_params=pltpu.CompilerParams(vmem_limit_bytes=VMEM_LIMIT),
    )


def columns(row):
    n = row.shape[1]
    parts = [
        jnp.transpose(jnp.broadcast_to(row[:, i : i + H], (H, H))) for i in range(0, n, H)
    ]
    return parts[0] if len(parts) == 1 else jnp.concatenate(parts, axis=0)


def one_hot_rows(col, n, base=0):
    e = col.shape[0]
    lane = lax.broadcasted_iota(jnp.int32, (e, H), 1)
    parts = [jnp.where(col == lane + (base + j), 1.0, 0.0).astype(BF16) for j in range(0, n, H)]
    return jnp.concatenate(parts, axis=1)


def one_hot_cols(row, n, base):
    e = row.shape[1]
    sub = lax.broadcasted_iota(jnp.int32, (n, e), 0) + base
    return jnp.where(jnp.broadcast_to(row, (n, e)) == sub, 1.0, 0.0).astype(BF16)


def dot(a, b):
    return jnp.dot(a, b, preferred_element_type=F32)


def dot_nt(a, b):
    return lax.dot_general(a, b, (((1,), (1,)), ((), ())), preferred_element_type=F32)


def gather_kernel(ids_ref, negs_ref, low_ref, rel_ref, head_ref, relrow_ref, prod_ref, cnt_ref, hi_ref, mid_ref, lo_ref):
    for r in range(0, NREL, 256):
        x = rel_ref[r : r + 256, :]
        for ref in (hi_ref, mid_ref, lo_ref):
            part = x.astype(BF16)
            ref[r : r + 256, :] = part
            x = x - part.astype(F32)

    def group(g, _):
        rows = pl.ds(pl.multiple_of(g * GROUP, GROUP), GROUP)
        src = columns(ids_ref[0:1, rows])
        heads = dot(one_hot_rows(src, ENT), low_ref[...])
        pick = one_hot_rows(columns(ids_ref[1:2, rows]), NREL)
        rel = dot(pick, hi_ref[...]) + dot(pick, mid_ref[...]) + dot(pick, lo_ref[...])
        hr, hi, rr, ri = heads[:, :H], heads[:, H:], rel[:, :H], rel[:, H:]
        head_ref[rows, :] = heads.astype(BF16)
        relrow_ref[rows, :] = rel
        prod_ref[rows, :H] = hr * rr - hi * ri
        prod_ref[rows, H:] = hr * ri + hi * rr
        negs = negs_ref[pl.ds(g, 1), :]
        high = one_hot_cols(lax.shift_right_logical(negs, 7), ENT // H, 0)
        low = one_hot_cols(lax.bitwise_and(negs, H - 1), H, 0)
        cnt_ref[g] = dot_nt(high, low) * (1.0 / NEG)
        return 0

    lax.fori_loop(0, EDGES // GROUP, group, 0)


def score_kernel(
    count_ref,
    ids_ref,
    near_ref,
    far_ref,
    head_ref,
    relrow_ref,
    prod_ref,
    cnt_ref,
    keep_ref,
    send_ref,
    cc_ref,
    plt_ref,
    pd_ref,
    gh_ref,
    gr_ref,
):
    half = ENT // 2
    count = count_ref[0, 0]

    def group(g, _):
        rows = pl.ds(pl.multiple_of(g * GROUP, GROUP), GROUP)
        dst = columns(ids_ref[2:3, rows])
        tails = dot(one_hot_rows(dst, half), near_ref[...]) + dot(
            one_hot_rows(dst, half, half), far_ref[...]
        )
        prod = prod_ref[rows, :]
        edge = lax.broadcasted_iota(jnp.int32, (GROUP, 1), 0) + g * GROUP
        live = jnp.where(edge < count, 1.0, 0.0).astype(F32)
        positive = jnp.sum(prod * tails, axis=1, keepdims=True)
        pos = -live * jax.nn.sigmoid(-positive)
        low = prod.astype(BF16)
        for j, table in ((0, near_ref), (1, far_ref)):
            scores = dot_nt(low, table[...])
            for i in range(half // H):
                w = cnt_ref[g, pl.ds(j * (half // H) + i, 1), :]
                part = scores[:, i * H : (i + 1) * H]
                cc_ref[rows, j * half + i * H : j * half + (i + 1) * H] = (
                    jax.nn.sigmoid(part) * w
                ).astype(BF16)
        neg = dot(cc_ref[rows, :half], near_ref[...]) + dot(cc_ref[rows, half:], far_ref[...])
        grad = pos * tails + live * neg
        rel = relrow_ref[rows, :]
        head = head_ref[rows, :].astype(F32)
        gr, gi = grad[:, :H], grad[:, H:]
        for out, other in ((gh_ref, rel), (gr_ref, head)):
            a, b = other[:, :H], other[:, H:]
            out[rows, :H] = (gr * a + gi * b).astype(BF16)
            out[rows, H:] = (gi * a - gr * b).astype(BF16)
        pd_ref[rows, :] = (pos * prod).astype(BF16)
        plt_ref[:, rows] = jnp.transpose(live * prod).astype(BF16)
        return 0

    lax.fori_loop(0, EDGES // GROUP, group, 0)

    def scatter(i, _):
        rows = pl.ds(pl.multiple_of(i * CHUNK, CHUNK), CHUNK)
        keep_ref[rows, :] = dot(one_hot_cols(ids_ref[3:4, :], CHUNK, i * CHUNK), gr_ref[...])
        send_ref[rows, :] = dot(
            one_hot_cols(ids_ref[3:4, :], CHUNK, half + i * CHUNK), gr_ref[...]
        ).astype(BF16)
        return 0

    lax.fori_loop(0, half // CHUNK, scatter, 0)


def scatter_kernel(
    place_ref,
    ids_ref,
    cc_ref,
    plt_ref,
    pd_ref,
    gh_ref,
    src_keep_ref,
    src_send_ref,
    dst_keep_ref,
    dst_send_ref,
):
    half = ENT // 2
    xl = place_ref[0]

    def scatter(i, _):
        rows = pl.ds(pl.multiple_of(i * CHUNK, CHUNK), CHUNK)
        to = lax.bitwise_xor(i, xl * (half // 2 // CHUNK))
        out = pl.ds(pl.multiple_of(to * CHUNK, CHUNK), CHUNK)
        for base, src_ref, dst_ref in (
            (0, src_keep_ref, dst_keep_ref),
            (half, src_send_ref, dst_send_ref),
        ):
            src = dot(one_hot_cols(ids_ref[4:5, :], CHUNK, base + i * CHUNK), gh_ref[...])
            src_ref[rows, :] = src.astype(src_ref.dtype)
            cols = pl.ds(pl.multiple_of(base + i * CHUNK, CHUNK), CHUNK)
            drawn = jnp.transpose(dot(plt_ref[...], cc_ref[:, cols]))
            dst = dot(one_hot_cols(ids_ref[2:3, :], CHUNK, base + i * CHUNK), pd_ref[...])
            dst_ref[out, :] = (drawn + dst).astype(dst_ref.dtype)
        return 0

    lax.fori_loop(0, half // CHUNK, scatter, 0)


def add_split_kernel(n_in, n_out, *refs):
    ins, outs = refs[:n_in], refs[n_in:]
    size = outs[0].shape[0]
    step = min(size, 64)
    for k, out in enumerate(outs):
        for r in range(0, size, step):
            total = ins[0][k * size + r : k * size + r + step, :].astype(F32)
            for ref in ins[1:]:
                total = total + ref[k * size + r : k * size + r + step, :].astype(F32)
            out[r : r + step, :] = total.astype(out.dtype)


def add_split(parts, n_out, own=BF16, sent=BF16):
    rows = parts[0].shape[0] // n_out
    shapes = [jax.ShapeDtypeStruct((rows, D), sent if k else own) for k in range(n_out)]
    return call(
        functools.partial(add_split_kernel, len(parts), n_out),
        shapes,
        0,
        len(parts),
        flops=len(parts) * n_out * rows * D,
        bytes_accessed=3 * len(parts) * n_out * rows * D,
    )(*parts)


def split3(x):
    hi = x.astype(BF16).astype(F32)
    mid = (x - hi).astype(BF16).astype(F32)
    return hi, mid, x - hi - mid


def sum_with_means_kernel(*refs):
    parts, out_ref = refs[:-1], refs[-1]
    rows = parts[0].shape[0]
    means = []
    for r in range(0, rows, H):
        total = parts[0][r : r + H, :].astype(F32)
        for ref in parts[1:]:
            total = total + ref[r : r + H, :].astype(F32)
        out_ref[r : r + H, :] = total.astype(BF16)
        mean = jnp.sum(total * total, axis=1, keepdims=True) * (1.0 / D)
        means.append(jnp.transpose(jnp.broadcast_to(mean, (H, H)))[0:1, :])
    means.append(jnp.zeros((8 - len(means), H), F32))
    hi, mid, lo = split3(jnp.concatenate(means, axis=0))
    top = jnp.concatenate([hi, mid], axis=1)
    bottom = jnp.concatenate([lo, jnp.zeros_like(lo)], axis=1)
    out_ref[rows : rows + 16, :] = jnp.concatenate([top, bottom], axis=0).astype(BF16)


def sum_with_means(parts):
    rows = parts[0].shape[0]
    return call(
        sum_with_means_kernel,
        jax.ShapeDtypeStruct((rows + 16, D), BF16),
        0,
        len(parts),
        flops=len(parts) * rows * D,
        bytes_accessed=3 * len(parts) * rows * D,
    )(*parts)


def means_of(piece, start, row):
    tile = piece[start : start + 16, :].astype(F32)
    return tile[row : row + 1, :H] + tile[row : row + 1, H:] + tile[8 + row : 9 + row, :H]


def update_kernel(n_pieces, place_ref, rows_ref, acc_ref, *refs):
    pieces, new_ref, new_acc_ref = refs[:n_pieces], refs[n_pieces], refs[n_pieces + 1]
    size = rows_ref.shape[0]
    i = pl.program_id(0)
    want = lax.bitwise_xor(i, place_ref[0])
    for k, piece in enumerate(pieces):

        @pl.when(want == k)
        def _(piece=piece):
            for r in range(0, size, H):
                g = piece[r : r + H, :].astype(F32)
                at = pl.ds(i * (size // H) + r // H, 1)
                acc = acc_ref[at, :] + means_of(piece, size, r // H)
                new_acc_ref[at, :] = acc
                scale = jnp.transpose(jnp.broadcast_to(RATE / jnp.sqrt(acc), (H, H)))
                new_ref[r : r + H, :H] = rows_ref[r : r + H, :H] - g[:, :H] * scale
                new_ref[r : r + H, H:] = rows_ref[r : r + H, H:] - g[:, H:] * scale


def update(rows, acc, pieces, place):
    n = rows.shape[0]
    size = n // len(pieces)
    whole = lambda i: (0, 0)
    new, new_acc = pl.pallas_call(
        functools.partial(update_kernel, len(pieces)),
        grid=(n // size,),
        out_shape=[
            jax.ShapeDtypeStruct((n, D), F32),
            jax.ShapeDtypeStruct((n // H, H), F32),
        ],
        in_specs=[
            smem(),
            pl.BlockSpec((size, D), lambda i: (i, 0)),
            pl.BlockSpec((n // H, H), whole),
        ]
        + [pl.BlockSpec(piece.shape, whole) for piece in pieces],
        out_specs=[
            pl.BlockSpec((size, D), lambda i: (i, 0)),
            pl.BlockSpec((n // H, H), whole),
        ],
        cost_estimate=pl.CostEstimate(flops=8 * n * D, bytes_accessed=10 * n * D, transcendentals=n),
        compiler_params=pltpu.CompilerParams(vmem_limit_bytes=VMEM_LIMIT),
    )(place, rows, acc.reshape(n // H, H), *pieces)
    return new, new_acc.reshape(n)


def sum_rows_kernel(parts_ref, out_ref):
    total = parts_ref[0].astype(F32)
    for k in range(1, parts_ref.shape[0]):
        total = total + parts_ref[k].astype(F32)
    out_ref[...] = jnp.broadcast_to(total, out_ref.shape)


def sum_rows(parts):
    return call(
        sum_rows_kernel,
        jax.ShapeDtypeStruct(parts.shape, F32),
        0,
        1,
        flops=parts.size,
        bytes_accessed=6 * parts.size,
    )(parts)


def spread(parts):
    groups = [[2 * k + hi for k in range(32)] for hi in range(2)]
    return lax.all_to_all(parts, "blk", 0, 0, axis_index_groups=groups, tiled=True)


def swap(x, mask):
    return lax.ppermute(x, AXES, [(i, i ^ mask) for i in range(256)])


def shift(x, distance, mask):
    route = [(((i // 4 - distance) % 64) * 4 + ((i % 4) ^ mask), i) for i in range(256)]
    return lax.ppermute(x, AXES, route)


CORE, XL = 1, 2
X_MASKS = (2, 4, 6)


def shards(
    entities, entity_acc, relations, relation_acc, src_ids, rel_ids, dst_ids, neg_ids, counts
):
    blk, rep = lax.axis_index("blk"), lax.axis_index("rep")
    core, xl = rep % 2, rep // 2
    x = (blk % 2) * 2 + xl

    low = entities.astype(BF16)
    half = lax.dynamic_slice_in_dim(entities, core * (ENT // 2), ENT // 2, 0).astype(BF16)
    near = shift(half, -1, XL)

    ids = jnp.concatenate(
        [
            src_ids,
            rel_ids,
            dst_ids ^ (core * 1024),
            rel_ids ^ (core * 1024 + x * 256),
            src_ids ^ (core * 1024 + xl * 512),
            jnp.zeros((3, EDGES), jnp.int32),
        ],
        axis=0,
    )
    negs = (neg_ids ^ (core * 1024)).reshape(4, NEG)
    head, rel_rows, prod, cnt = call(
        gather_kernel,
        [
            jax.ShapeDtypeStruct((EDGES, D), BF16),
            jax.ShapeDtypeStruct((EDGES, D), F32),
            jax.ShapeDtypeStruct((EDGES, D), F32),
            jax.ShapeDtypeStruct((4, ENT // H, H), F32),
        ],
        0,
        4,
        [pltpu.VMEM((NREL, D), BF16)] * 3,
        flops=4 * 2 * EDGES * ENT * D,
        bytes_accessed=1 << 22,
    )(ids, negs, low, relations)

    near, head = lax.optimization_barrier((near, head))
    far = swap(near, CORE)
    kept = jax.ShapeDtypeStruct((ENT // 2, D), F32)
    sent = jax.ShapeDtypeStruct((ENT // 2, D), BF16)
    rel_keep, rel_send, cc, plt, pd, gh = call(
        score_kernel,
        [
            kept,
            sent,
            jax.ShapeDtypeStruct((EDGES, ENT), BF16),
            jax.ShapeDtypeStruct((D, EDGES), BF16),
            jax.ShapeDtypeStruct((EDGES, D), BF16),
            jax.ShapeDtypeStruct((EDGES, D), BF16),
        ],
        1,
        7,
        [pltpu.VMEM((EDGES, D), BF16)],
        flops=4 * 2 * EDGES * ENT * D,
        bytes_accessed=1 << 23,
    )(counts, ids, near, far, head, rel_rows, prod, cnt)
    rel_recv = swap(rel_send, CORE)
    parts = add_split([rel_keep, rel_recv], 4, own=F32)
    parts, cc = lax.optimization_barrier((parts, cc))
    recv = [swap(part, mask) for part, mask in zip(parts[1:], X_MASKS)]

    src_keep, src_send, dst_keep, dst_send = call(
        scatter_kernel,
        [kept, sent, kept, sent],
        1,
        5,
        flops=3 * 2 * EDGES * ENT * D,
        bytes_accessed=1 << 23,
    )(xl.reshape(1), ids, cc, plt, pd, gh)
    recv, src_send, dst_send = lax.optimization_barrier((recv, src_send, dst_send))
    src_recv = swap(src_send, CORE)
    dst_recv = swap(dst_send, CORE)
    src_own, src_away = add_split([src_keep, src_recv], 2, own=F32)
    dst_own, dst_away = add_split([dst_keep, dst_recv], 2)
    (mine,) = add_split([parts[0], *recv], 1)
    mine, src_away, dst_own, dst_away = lax.optimization_barrier(
        (mine, src_away, dst_own, dst_away)
    )
    src_other = swap(src_away, XL)
    dst_first = shift(dst_own, 1, 0)
    dst_second = shift(dst_away, 1, XL)

    landed = spread(mine.reshape(32, 8, D))
    ent_own = sum_with_means([src_own, src_other, dst_first, dst_second])
    summed = sum_rows(landed)
    summed, ent_own = lax.optimization_barrier((summed, ent_own))
    ent_xl = swap(ent_own, XL)
    total = spread(summed).reshape(256, D)
    quarter = sum_with_means([total])
    recv = [swap(quarter, mask) for mask in X_MASKS]

    ent_core = [swap(ent_own, CORE), swap(ent_xl, CORE)]
    place = (core * 2 + xl).reshape(1)
    new_entities, new_entity_acc = update(
        entities, entity_acc, [ent_own, ent_xl, *ent_core], place
    )

    pieces = [quarter, *recv]
    pieces = pieces + [swap(piece, CORE) for piece in pieces]
    place = (core * 4 + x).reshape(1)
    new_relations, new_relation_acc = update(relations, relation_acc, pieces, place)
    return (new_entities, new_entity_acc, new_relations, new_relation_acc)


def solution(mesh):
    in_specs = (
        P("blk", None),
        P("blk"),
        P(),
        P(),
        P("blk", "rep"),
        P("blk", "rep"),
        P("blk", "rep"),
        P("blk", "rep"),
        P("blk", "rep"),
    )
    out_specs = (P("blk", None), P("blk"), P(), P())
    return jax.shard_map(shards, mesh=mesh, in_specs=in_specs, out_specs=out_specs, check_vma=False)
```

```python
import functools

import jax
import jax.numpy as jnp
from jax import lax
from jax.experimental import pallas as pl
from jax.experimental.pallas import tpu as pltpu
from jax.sharding import PartitionSpec as P

F32 = jnp.float32
BF16 = jnp.bfloat16
D = 256
H = 128
ENT = 2048
EDGES = 1024
GROUP = 256
NEG = 1024
NREL = 2048
RATE = 0.1
AXES = ("blk", "rep")
VMEM_LIMIT = 48 * 1024 * 1024
CHUNK = 256


def vmem():
    return pl.BlockSpec(memory_space=pltpu.VMEM)


def smem():
    return pl.BlockSpec(memory_space=pltpu.SMEM)


def call(kernel, out_shape, n_smem, n_vmem, scratch=(), flops=0, bytes_accessed=0):
    return pl.pallas_call(
        kernel,
        out_shape=out_shape,
        in_specs=[smem()] * n_smem + [vmem()] * n_vmem,
        out_specs=jax.tree.map(lambda _: vmem(), out_shape),
        scratch_shapes=list(scratch),
        cost_estimate=pl.CostEstimate(
            flops=flops, bytes_accessed=bytes_accessed, transcendentals=0
        ),
        compiler_params=pltpu.CompilerParams(vmem_limit_bytes=VMEM_LIMIT),
    )


def columns(row):
    n = row.shape[1]
    parts = [
        jnp.transpose(jnp.broadcast_to(row[:, i : i + H], (H, H))) for i in range(0, n, H)
    ]
    return parts[0] if len(parts) == 1 else jnp.concatenate(parts, axis=0)


def one_hot_rows(col, n, base=0):
    e = col.shape[0]
    lane = lax.broadcasted_iota(jnp.int32, (e, H), 1)
    parts = [jnp.where(col == lane + (base + j), 1.0, 0.0).astype(BF16) for j in range(0, n, H)]
    return jnp.concatenate(parts, axis=1)


def one_hot_cols(row, n, base):
    e = row.shape[1]
    sub = lax.broadcasted_iota(jnp.int32, (n, e), 0) + base
    return jnp.where(jnp.broadcast_to(row, (n, e)) == sub, 1.0, 0.0).astype(BF16)


def dot(a, b):
    return jnp.dot(a, b, preferred_element_type=F32)


def dot_nt(a, b):
    return lax.dot_general(a, b, (((1,), (1,)), ((), ())), preferred_element_type=F32)


def gather_kernel(ids_ref, negs_ref, low_ref, rel_ref, head_ref, relrow_ref, prod_ref, cnt_ref, hi_ref, mid_ref, lo_ref):
    for r in range(0, NREL, 256):
        x = rel_ref[r : r + 256, :]
        for ref in (hi_ref, mid_ref, lo_ref):
            part = x.astype(BF16)
            ref[r : r + 256, :] = part
            x = x - part.astype(F32)

    def group(g, _):
        rows = pl.ds(pl.multiple_of(g * GROUP, GROUP), GROUP)
        src = columns(ids_ref[0:1, rows])
        heads = dot(one_hot_rows(src, ENT), low_ref[...])
        pick = one_hot_rows(columns(ids_ref[1:2, rows]), NREL)
        rel = dot(pick, hi_ref[...]) + dot(pick, mid_ref[...]) + dot(pick, lo_ref[...])
        hr, hi, rr, ri = heads[:, :H], heads[:, H:], rel[:, :H], rel[:, H:]
        head_ref[rows, :] = heads.astype(BF16)
        relrow_ref[rows, :] = rel
        prod_ref[rows, :H] = hr * rr - hi * ri
        prod_ref[rows, H:] = hr * ri + hi * rr
        negs = negs_ref[pl.ds(g, 1), :]
        high = one_hot_cols(lax.shift_right_logical(negs, 7), ENT // H, 0)
        low = one_hot_cols(lax.bitwise_and(negs, H - 1), H, 0)
        cnt_ref[g] = dot_nt(high, low) * (1.0 / NEG)
        return 0

    lax.fori_loop(0, EDGES // GROUP, group, 0)


def score_kernel(
    count_ref,
    ids_ref,
    near_ref,
    far_ref,
    head_ref,
    relrow_ref,
    prod_ref,
    cnt_ref,
    keep_ref,
    send_ref,
    cc_ref,
    plt_ref,
    pd_ref,
    gh_ref,
    gr_ref,
):
    half = ENT // 2
    count = count_ref[0, 0]

    def group(g, _):
        rows = pl.ds(pl.multiple_of(g * GROUP, GROUP), GROUP)
        dst = columns(ids_ref[2:3, rows])
        tails = dot(one_hot_rows(dst, half), near_ref[...]) + dot(
            one_hot_rows(dst, half, half), far_ref[...]
        )
        prod = prod_ref[rows, :]
        edge = lax.broadcasted_iota(jnp.int32, (GROUP, 1), 0) + g * GROUP
        live = jnp.where(edge < count, 1.0, 0.0).astype(F32)
        positive = jnp.sum(prod * tails, axis=1, keepdims=True)
        pos = -live * jax.nn.sigmoid(-positive)
        low = prod.astype(BF16)
        for j, table in ((0, near_ref), (1, far_ref)):
            scores = dot_nt(low, table[...])
            for i in range(half // H):
                w = cnt_ref[g, pl.ds(j * (half // H) + i, 1), :]
                part = scores[:, i * H : (i + 1) * H]
                cc_ref[rows, j * half + i * H : j * half + (i + 1) * H] = (
                    jax.nn.sigmoid(part) * w
                ).astype(BF16)
        neg = dot(cc_ref[rows, :half], near_ref[...]) + dot(cc_ref[rows, half:], far_ref[...])
        grad = pos * tails + live * neg
        rel = relrow_ref[rows, :]
        head = head_ref[rows, :].astype(F32)
        gr, gi = grad[:, :H], grad[:, H:]
        for out, other in ((gh_ref, rel), (gr_ref, head)):
            a, b = other[:, :H], other[:, H:]
            out[rows, :H] = (gr * a + gi * b).astype(BF16)
            out[rows, H:] = (gi * a - gr * b).astype(BF16)
        pd_ref[rows, :] = (pos * prod).astype(BF16)
        plt_ref[:, rows] = jnp.transpose(live * prod).astype(BF16)
        return 0

    lax.fori_loop(0, EDGES // GROUP, group, 0)

    def scatter(i, _):
        rows = pl.ds(pl.multiple_of(i * CHUNK, CHUNK), CHUNK)
        keep_ref[rows, :] = dot(one_hot_cols(ids_ref[3:4, :], CHUNK, i * CHUNK), gr_ref[...])
        send_ref[rows, :] = dot(
            one_hot_cols(ids_ref[3:4, :], CHUNK, half + i * CHUNK), gr_ref[...]
        ).astype(BF16)
        return 0

    lax.fori_loop(0, half // CHUNK, scatter, 0)


def scatter_kernel(
    place_ref,
    ids_ref,
    cc_ref,
    plt_ref,
    pd_ref,
    gh_ref,
    src_keep_ref,
    src_send_ref,
    dst_keep_ref,
    dst_send_ref,
):
    half = ENT // 2
    xl = place_ref[0]

    def scatter(i, _):
        rows = pl.ds(pl.multiple_of(i * CHUNK, CHUNK), CHUNK)
        to = lax.bitwise_xor(i, xl * (half // 2 // CHUNK))
        out = pl.ds(pl.multiple_of(to * CHUNK, CHUNK), CHUNK)
        for base, src_ref, dst_ref in (
            (0, src_keep_ref, dst_keep_ref),
            (half, src_send_ref, dst_send_ref),
        ):
            src = dot(one_hot_cols(ids_ref[4:5, :], CHUNK, base + i * CHUNK), gh_ref[...])
            src_ref[rows, :] = src.astype(src_ref.dtype)
            cols = pl.ds(pl.multiple_of(base + i * CHUNK, CHUNK), CHUNK)
            drawn = jnp.transpose(dot(plt_ref[...], cc_ref[:, cols]))
            dst = dot(one_hot_cols(ids_ref[2:3, :], CHUNK, base + i * CHUNK), pd_ref[...])
            dst_ref[out, :] = (drawn + dst).astype(dst_ref.dtype)
        return 0

    lax.fori_loop(0, half // CHUNK, scatter, 0)


def add_split_kernel(n_in, n_out, *refs):
    ins, outs = refs[:n_in], refs[n_in:]
    size = outs[0].shape[0]
    step = min(size, 64)
    for k, out in enumerate(outs):
        for r in range(0, size, step):
            total = ins[0][k * size + r : k * size + r + step, :].astype(F32)
            for ref in ins[1:]:
                total = total + ref[k * size + r : k * size + r + step, :].astype(F32)
            out[r : r + step, :] = total.astype(out.dtype)


def add_split(parts, n_out, own=BF16, sent=BF16):
    rows = parts[0].shape[0] // n_out
    shapes = [jax.ShapeDtypeStruct((rows, D), sent if k else own) for k in range(n_out)]
    return call(
        functools.partial(add_split_kernel, len(parts), n_out),
        shapes,
        0,
        len(parts),
        flops=len(parts) * n_out * rows * D,
        bytes_accessed=3 * len(parts) * n_out * rows * D,
    )(*parts)


def split3(x):
    hi = x.astype(BF16).astype(F32)
    mid = (x - hi).astype(BF16).astype(F32)
    return hi, mid, x - hi - mid


def sum_with_means_kernel(*refs):
    parts, out_ref = refs[:-1], refs[-1]
    rows = parts[0].shape[0]
    means = []
    for r in range(0, rows, H):
        total = parts[0][r : r + H, :].astype(F32)
        for ref in parts[1:]:
            total = total + ref[r : r + H, :].astype(F32)
        out_ref[r : r + H, :] = total.astype(BF16)
        mean = jnp.sum(total * total, axis=1, keepdims=True) * (1.0 / D)
        means.append(jnp.transpose(jnp.broadcast_to(mean, (H, H)))[0:1, :])
    means.append(jnp.zeros((8 - len(means), H), F32))
    hi, mid, lo = split3(jnp.concatenate(means, axis=0))
    top = jnp.concatenate([hi, mid], axis=1)
    bottom = jnp.concatenate([lo, jnp.zeros_like(lo)], axis=1)
    out_ref[rows : rows + 16, :] = jnp.concatenate([top, bottom], axis=0).astype(BF16)


def sum_with_means(parts):
    rows = parts[0].shape[0]
    return call(
        sum_with_means_kernel,
        jax.ShapeDtypeStruct((rows + 16, D), BF16),
        0,
        len(parts),
        flops=len(parts) * rows * D,
        bytes_accessed=3 * len(parts) * rows * D,
    )(*parts)


def means_of(piece, start, row):
    tile = piece[start : start + 16, :].astype(F32)
    return tile[row : row + 1, :H] + tile[row : row + 1, H:] + tile[8 + row : 9 + row, :H]


def update_kernel(n_pieces, place_ref, rows_ref, acc_ref, *refs):
    pieces, new_ref, new_acc_ref = refs[:n_pieces], refs[n_pieces], refs[n_pieces + 1]
    size = rows_ref.shape[0]
    i = pl.program_id(0)
    want = lax.bitwise_xor(i, place_ref[0])
    for k, piece in enumerate(pieces):

        @pl.when(want == k)
        def _(piece=piece):
            for r in range(0, size, H):
                g = piece[r : r + H, :].astype(F32)
                at = pl.ds(i * (size // H) + r // H, 1)
                acc = acc_ref[at, :] + means_of(piece, size, r // H)
                new_acc_ref[at, :] = acc
                scale = jnp.transpose(jnp.broadcast_to(RATE / jnp.sqrt(acc), (H, H)))
                new_ref[r : r + H, :H] = rows_ref[r : r + H, :H] - g[:, :H] * scale
                new_ref[r : r + H, H:] = rows_ref[r : r + H, H:] - g[:, H:] * scale


def update(rows, acc, pieces, place):
    n = rows.shape[0]
    size = n // len(pieces)
    whole = lambda i: (0, 0)
    new, new_acc = pl.pallas_call(
        functools.partial(update_kernel, len(pieces)),
        grid=(n // size,),
        out_shape=[
            jax.ShapeDtypeStruct((n, D), F32),
            jax.ShapeDtypeStruct((n // H, H), F32),
        ],
        in_specs=[
            smem(),
            pl.BlockSpec((size, D), lambda i: (i, 0)),
            pl.BlockSpec((n // H, H), whole),
        ]
        + [pl.BlockSpec(piece.shape, whole) for piece in pieces],
        out_specs=[
            pl.BlockSpec((size, D), lambda i: (i, 0)),
            pl.BlockSpec((n // H, H), whole),
        ],
        cost_estimate=pl.CostEstimate(flops=8 * n * D, bytes_accessed=10 * n * D, transcendentals=n),
        compiler_params=pltpu.CompilerParams(vmem_limit_bytes=VMEM_LIMIT),
    )(place, rows, acc.reshape(n // H, H), *pieces)
    return new, new_acc.reshape(n)


def sum_rows_kernel(parts_ref, out_ref):
    total = parts_ref[0].astype(F32)
    for k in range(1, parts_ref.shape[0]):
        total = total + parts_ref[k].astype(F32)
    out_ref[...] = jnp.broadcast_to(total, out_ref.shape)


def sum_rows(parts):
    return call(
        sum_rows_kernel,
        jax.ShapeDtypeStruct(parts.shape, F32),
        0,
        1,
        flops=parts.size,
        bytes_accessed=6 * parts.size,
    )(parts)


def spread(parts):
    groups = [[2 * k + hi for k in range(32)] for hi in range(2)]
    return lax.all_to_all(parts, "blk", 0, 0, axis_index_groups=groups, tiled=True)


def swap(x, mask):
    return lax.ppermute(x, AXES, [(i, i ^ mask) for i in range(256)])


def shift(x, distance, mask):
    route = [(((i // 4 - distance) % 64) * 4 + ((i % 4) ^ mask), i) for i in range(256)]
    return lax.ppermute(x, AXES, route)


CORE, XL = 1, 2
X_MASKS = (2, 4, 6)


def shards(
    entities, entity_acc, relations, relation_acc, src_ids, rel_ids, dst_ids, neg_ids, counts
):
    blk, rep = lax.axis_index("blk"), lax.axis_index("rep")
    core, xl = rep % 2, rep // 2
    x = (blk % 2) * 2 + xl

    low = entities.astype(BF16)
    half = lax.dynamic_slice_in_dim(entities, core * (ENT // 2), ENT // 2, 0).astype(BF16)
    near = shift(half, -1, XL)

    ids = jnp.concatenate(
        [
            src_ids,
            rel_ids,
            dst_ids ^ (core * 1024),
            rel_ids ^ (core * 1024 + x * 256),
            src_ids ^ (core * 1024 + xl * 512),
            jnp.zeros((3, EDGES), jnp.int32),
        ],
        axis=0,
    )
    negs = (neg_ids ^ (core * 1024)).reshape(4, NEG)
    head, rel_rows, prod, cnt = call(
        gather_kernel,
        [
            jax.ShapeDtypeStruct((EDGES, D), BF16),
            jax.ShapeDtypeStruct((EDGES, D), F32),
            jax.ShapeDtypeStruct((EDGES, D), F32),
            jax.ShapeDtypeStruct((4, ENT // H, H), F32),
        ],
        0,
        4,
        [pltpu.VMEM((NREL, D), BF16)] * 3,
        flops=4 * 2 * EDGES * ENT * D,
        bytes_accessed=1 << 22,
    )(ids, negs, low, relations)

    near, head = lax.optimization_barrier((near, head))
    far = swap(near, CORE)
    kept = jax.ShapeDtypeStruct((ENT // 2, D), F32)
    sent = jax.ShapeDtypeStruct((ENT // 2, D), BF16)
    rel_keep, rel_send, cc, plt, pd, gh = call(
        score_kernel,
        [
            kept,
            sent,
            jax.ShapeDtypeStruct((EDGES, ENT), BF16),
            jax.ShapeDtypeStruct((D, EDGES), BF16),
            jax.ShapeDtypeStruct((EDGES, D), BF16),
            jax.ShapeDtypeStruct((EDGES, D), BF16),
        ],
        1,
        7,
        [pltpu.VMEM((EDGES, D), BF16)],
        flops=4 * 2 * EDGES * ENT * D,
        bytes_accessed=1 << 23,
    )(counts, ids, near, far, head, rel_rows, prod, cnt)
    rel_recv = swap(rel_send, CORE)
    parts = add_split([rel_keep, rel_recv], 4, own=F32)
    parts, cc = lax.optimization_barrier((parts, cc))
    recv = [swap(part, mask) for part, mask in zip(parts[1:], X_MASKS)]

    src_keep, src_send, dst_keep, dst_send = call(
        scatter_kernel,
        [kept, sent, kept, sent],
        1,
        5,
        flops=3 * 2 * EDGES * ENT * D,
        bytes_accessed=1 << 23,
    )(xl.reshape(1), ids, cc, plt, pd, gh)
    recv, src_send, dst_send = lax.optimization_barrier((recv, src_send, dst_send))
    src_recv = swap(src_send, CORE)
    dst_recv = swap(dst_send, CORE)
    src_own, src_away = add_split([src_keep, src_recv], 2, own=F32)
    dst_own, dst_away = add_split([dst_keep, dst_recv], 2)
    (mine,) = add_split([parts[0], *recv], 1)
    src_other = swap(src_away, XL)
    dst_first = shift(dst_own, 1, 0)
    dst_second = shift(dst_away, 1, XL)

    landed = spread(mine.reshape(32, 8, D))
    landed, src_other, dst_first, dst_second = lax.optimization_barrier(
        (landed, src_other, dst_first, dst_second)
    )
    summed = sum_rows(landed)
    ent_own = sum_with_means([src_own, src_other, dst_first, dst_second])
    ent_xl = swap(ent_own, XL)
    ent_core = [swap(ent_own, CORE), swap(ent_xl, CORE)]
    place = (core * 2 + xl).reshape(1)
    new_entities, new_entity_acc = update(
        entities, entity_acc, [ent_own, ent_xl, *ent_core], place
    )
    total, new_entity_acc = lax.optimization_barrier((spread(summed), new_entity_acc))
    quarter = sum_with_means([total.reshape(256, D)])
    recv = [swap(quarter, mask) for mask in X_MASKS]

    pieces = [quarter, *recv]
    pieces = pieces + [swap(piece, CORE) for piece in pieces]
    place = (core * 4 + x).reshape(1)
    new_relations, new_relation_acc = update(relations, relation_acc, pieces, place)
    return (new_entities, new_entity_acc, new_relations, new_relation_acc)


def solution(mesh):
    in_specs = (
        P("blk", None),
        P("blk"),
        P(),
        P(),
        P("blk", "rep"),
        P("blk", "rep"),
        P("blk", "rep"),
        P("blk", "rep"),
        P("blk", "rep"),
    )
    out_specs = (P("blk", None), P("blk"), P(), P())
    return jax.shard_map(shards, mesh=mesh, in_specs=in_specs, out_specs=out_specs, check_vma=False)
```

```python
import functools

import jax
import jax.numpy as jnp
from jax import lax
from jax.experimental import pallas as pl
from jax.experimental.pallas import tpu as pltpu
from jax.sharding import PartitionSpec as P

F32 = jnp.float32
BF16 = jnp.bfloat16
D = 256
H = 128
ENT = 2048
EDGES = 1024
GROUP = 256
NEG = 1024
NREL = 2048
RATE = 0.1
AXES = ("blk", "rep")
VMEM_LIMIT = 48 * 1024 * 1024
CHUNK = 256
UNROLL = 4


def vmem():
    return pl.BlockSpec(memory_space=pltpu.VMEM)


def smem():
    return pl.BlockSpec(memory_space=pltpu.SMEM)


def call(kernel, out_shape, n_smem, n_vmem, scratch=(), flops=0, bytes_accessed=0):
    return pl.pallas_call(
        kernel,
        out_shape=out_shape,
        in_specs=[smem()] * n_smem + [vmem()] * n_vmem,
        out_specs=jax.tree.map(lambda _: vmem(), out_shape),
        scratch_shapes=list(scratch),
        cost_estimate=pl.CostEstimate(
            flops=flops, bytes_accessed=bytes_accessed, transcendentals=0
        ),
        compiler_params=pltpu.CompilerParams(vmem_limit_bytes=VMEM_LIMIT),
    )


def columns(row):
    n = row.shape[1]
    parts = [
        jnp.transpose(jnp.broadcast_to(row[:, i : i + H], (H, H))) for i in range(0, n, H)
    ]
    return parts[0] if len(parts) == 1 else jnp.concatenate(parts, axis=0)


def one_hot_rows(col, n, base=0):
    e = col.shape[0]
    lane = lax.broadcasted_iota(jnp.int32, (e, H), 1)
    parts = [jnp.where(col == lane + (base + j), 1.0, 0.0).astype(BF16) for j in range(0, n, H)]
    return jnp.concatenate(parts, axis=1)


def one_hot_cols(row, n, base):
    e = row.shape[1]
    sub = lax.broadcasted_iota(jnp.int32, (n, e), 0) + base
    return jnp.where(jnp.broadcast_to(row, (n, e)) == sub, 1.0, 0.0).astype(BF16)


def dot(a, b):
    return jnp.dot(a, b, preferred_element_type=F32)


def dot_nt(a, b):
    return lax.dot_general(a, b, (((1,), (1,)), ((), ())), preferred_element_type=F32)


def gather_kernel(ids_ref, negs_ref, low_ref, rel_ref, head_ref, relrow_ref, prod_ref, cnt_ref, hi_ref, mid_ref, lo_ref):
    for r in range(0, NREL, 256):
        x = rel_ref[r : r + 256, :]
        for ref in (hi_ref, mid_ref, lo_ref):
            part = x.astype(BF16)
            ref[r : r + 256, :] = part
            x = x - part.astype(F32)

    def group(g, _):
        rows = pl.ds(pl.multiple_of(g * GROUP, GROUP), GROUP)
        src = columns(ids_ref[0:1, rows])
        heads = dot(one_hot_rows(src, ENT), low_ref[...])
        pick = one_hot_rows(columns(ids_ref[1:2, rows]), NREL)
        rel = dot(pick, hi_ref[...]) + dot(pick, mid_ref[...]) + dot(pick, lo_ref[...])
        hr, hi, rr, ri = heads[:, :H], heads[:, H:], rel[:, :H], rel[:, H:]
        head_ref[rows, :] = heads.astype(BF16)
        relrow_ref[rows, :] = rel
        prod_ref[rows, :H] = hr * rr - hi * ri
        prod_ref[rows, H:] = hr * ri + hi * rr
        negs = negs_ref[pl.ds(g, 1), :]
        high = one_hot_cols(lax.shift_right_logical(negs, 7), ENT // H, 0)
        low = one_hot_cols(lax.bitwise_and(negs, H - 1), H, 0)
        cnt_ref[g] = dot_nt(high, low) * (1.0 / NEG)
        return 0

    lax.fori_loop(0, EDGES // GROUP, group, 0, unroll=UNROLL)


def against(part, ids_ref, near_ref, far_ref, prod_ref, cnt_ref, cc_ref, rows, g):
    size = near_ref.shape[0]
    dst = columns(ids_ref[2:3, rows])
    low = prod_ref[rows, :].astype(BF16)
    tails = neg = None
    for j, table in ((0, near_ref), (1, far_ref)):
        base = j * (ENT // 2) + part * size
        tail = dot(one_hot_rows(dst, size, base), table[...])
        scores = dot_nt(low, table[...])
        for i in range(size // H):
            w = cnt_ref[g, base // H + i : base // H + i + 1, :]
            cc_ref[rows, j * size + i * H : j * size + (i + 1) * H] = (
                jax.nn.sigmoid(scores[:, i * H : (i + 1) * H]) * w
            ).astype(BF16)
        drawn = dot(cc_ref[rows, j * size : (j + 1) * size], table[...])
        tails = tail if tails is None else tails + tail
        neg = drawn if neg is None else neg + drawn
    return tails, neg


def first_score_kernel(ids_ref, near_ref, far_ref, prod_ref, cnt_ref, cc_ref, tails_ref, neg_ref):
    def group(g, _):
        rows = pl.ds(pl.multiple_of(g * GROUP, GROUP), GROUP)
        tails, neg = against(0, ids_ref, near_ref, far_ref, prod_ref, cnt_ref, cc_ref, rows, g)
        tails_ref[rows, :] = tails
        neg_ref[rows, :] = neg
        return 0

    lax.fori_loop(0, EDGES // GROUP, group, 0, unroll=UNROLL)


def score_kernel(
    count_ref,
    ids_ref,
    near_ref,
    far_ref,
    head_ref,
    relrow_ref,
    prod_ref,
    cnt_ref,
    tails_ref,
    neg_ref,
    keep_ref,
    send_ref,
    cc_ref,
    plt_ref,
    pd_ref,
    gh_ref,
    gr_ref,
):
    half = ENT // 2
    count = count_ref[0, 0]

    def group(g, _):
        rows = pl.ds(pl.multiple_of(g * GROUP, GROUP), GROUP)
        tails, neg = against(1, ids_ref, near_ref, far_ref, prod_ref, cnt_ref, cc_ref, rows, g)
        tails = tails + tails_ref[rows, :]
        neg = neg + neg_ref[rows, :]
        prod = prod_ref[rows, :]
        edge = lax.broadcasted_iota(jnp.int32, (GROUP, 1), 0) + g * GROUP
        live = jnp.where(edge < count, 1.0, 0.0).astype(F32)
        positive = jnp.sum(prod * tails, axis=1, keepdims=True)
        pos = -live * jax.nn.sigmoid(-positive)
        grad = pos * tails + live * neg
        rel = relrow_ref[rows, :]
        head = head_ref[rows, :].astype(F32)
        gr, gi = grad[:, :H], grad[:, H:]
        for out, other in ((gh_ref, rel), (gr_ref, head)):
            a, b = other[:, :H], other[:, H:]
            out[rows, :H] = (gr * a + gi * b).astype(BF16)
            out[rows, H:] = (gi * a - gr * b).astype(BF16)
        pd_ref[rows, :] = (pos * prod).astype(BF16)
        plt_ref[:, rows] = jnp.transpose(live * prod).astype(BF16)
        return 0

    lax.fori_loop(0, EDGES // GROUP, group, 0, unroll=UNROLL)

    def scatter(i, _):
        rows = pl.ds(pl.multiple_of(i * CHUNK, CHUNK), CHUNK)
        keep_ref[rows, :] = dot(one_hot_cols(ids_ref[3:4, :], CHUNK, i * CHUNK), gr_ref[...])
        send_ref[rows, :] = dot(
            one_hot_cols(ids_ref[3:4, :], CHUNK, half + i * CHUNK), gr_ref[...]
        ).astype(BF16)
        return 0

    lax.fori_loop(0, half // CHUNK, scatter, 0, unroll=UNROLL)


def scatter_kernel(
    place_ref,
    ids_ref,
    first_ref,
    second_ref,
    plt_ref,
    pd_ref,
    gh_ref,
    src_keep_ref,
    src_send_ref,
    dst_keep_ref,
    dst_send_ref,
):
    half = ENT // 2
    quarter = half // 2
    xl = place_ref[0]

    def scatter(i, part, cc_ref):
        at = part * quarter + i * CHUNK
        rows = pl.ds(pl.multiple_of(at, CHUNK), CHUNK)
        to = lax.bitwise_xor(part, xl) * quarter + i * CHUNK
        out = pl.ds(pl.multiple_of(to, CHUNK), CHUNK)
        for j, src_ref, dst_ref in (
            (0, src_keep_ref, dst_keep_ref),
            (1, src_send_ref, dst_send_ref),
        ):
            src = dot(one_hot_cols(ids_ref[4:5, :], CHUNK, j * half + at), gh_ref[...])
            src_ref[rows, :] = src.astype(src_ref.dtype)
            cols = pl.ds(pl.multiple_of(j * quarter + i * CHUNK, CHUNK), CHUNK)
            drawn = jnp.transpose(dot(plt_ref[...], cc_ref[:, cols]))
            dst = dot(one_hot_cols(ids_ref[2:3, :], CHUNK, j * half + at), pd_ref[...])
            dst_ref[out, :] = (drawn + dst).astype(dst_ref.dtype)

    for part, ref in ((0, first_ref), (1, second_ref)):
        for i in range(quarter // CHUNK):
            scatter(i, part, ref)


def add_split_kernel(n_in, n_out, *refs):
    ins, outs = refs[:n_in], refs[n_in:]
    size = outs[0].shape[0]
    step = min(size, 64)
    for k, out in enumerate(outs):
        for r in range(0, size, step):
            total = ins[0][k * size + r : k * size + r + step, :].astype(F32)
            for ref in ins[1:]:
                total = total + ref[k * size + r : k * size + r + step, :].astype(F32)
            out[r : r + step, :] = total.astype(out.dtype)


def add_split(parts, n_out, own=BF16, sent=BF16):
    rows = parts[0].shape[0] // n_out
    shapes = [jax.ShapeDtypeStruct((rows, D), sent if k else own) for k in range(n_out)]
    return call(
        functools.partial(add_split_kernel, len(parts), n_out),
        shapes,
        0,
        len(parts),
        flops=len(parts) * n_out * rows * D,
        bytes_accessed=3 * len(parts) * n_out * rows * D,
    )(*parts)


def split3(x):
    hi = x.astype(BF16).astype(F32)
    mid = (x - hi).astype(BF16).astype(F32)
    return hi, mid, x - hi - mid


def sum_with_means_kernel(*refs):
    parts, out_ref = refs[:-1], refs[-1]
    rows = parts[0].shape[0]
    means = []
    for r in range(0, rows, H):
        total = parts[0][r : r + H, :].astype(F32)
        for ref in parts[1:]:
            total = total + ref[r : r + H, :].astype(F32)
        out_ref[r : r + H, :] = total.astype(BF16)
        mean = jnp.sum(total * total, axis=1, keepdims=True) * (1.0 / D)
        means.append(jnp.transpose(jnp.broadcast_to(mean, (H, H)))[0:1, :])
    means.append(jnp.zeros((8 - len(means), H), F32))
    hi, mid, lo = split3(jnp.concatenate(means, axis=0))
    top = jnp.concatenate([hi, mid], axis=1)
    bottom = jnp.concatenate([lo, jnp.zeros_like(lo)], axis=1)
    out_ref[rows : rows + 16, :] = jnp.concatenate([top, bottom], axis=0).astype(BF16)


def sum_with_means(parts):
    rows = parts[0].shape[0]
    return call(
        sum_with_means_kernel,
        jax.ShapeDtypeStruct((rows + 16, D), BF16),
        0,
        len(parts),
        flops=len(parts) * rows * D,
        bytes_accessed=3 * len(parts) * rows * D,
    )(*parts)


def means_of(piece, start, row):
    tile = piece[start : start + 16, :].astype(F32)
    return tile[row : row + 1, :H] + tile[row : row + 1, H:] + tile[8 + row : 9 + row, :H]


def update_kernel(n_pieces, place_ref, rows_ref, acc_ref, *refs):
    pieces, new_ref, new_acc_ref = refs[:n_pieces], refs[n_pieces], refs[n_pieces + 1]
    size = rows_ref.shape[0]
    i = pl.program_id(0)
    want = lax.bitwise_xor(i, place_ref[0])
    for k, piece in enumerate(pieces):

        @pl.when(want == k)
        def _(piece=piece):
            for r in range(0, size, H):
                g = piece[r : r + H, :].astype(F32)
                at = pl.ds(i * (size // H) + r // H, 1)
                acc = acc_ref[at, :] + means_of(piece, size, r // H)
                new_acc_ref[at, :] = acc
                scale = jnp.transpose(jnp.broadcast_to(RATE / jnp.sqrt(acc), (H, H)))
                new_ref[r : r + H, :H] = rows_ref[r : r + H, :H] - g[:, :H] * scale
                new_ref[r : r + H, H:] = rows_ref[r : r + H, H:] - g[:, H:] * scale


def update(rows, acc, pieces, place):
    n = rows.shape[0]
    size = n // len(pieces)
    whole = lambda i: (0, 0)
    new, new_acc = pl.pallas_call(
        functools.partial(update_kernel, len(pieces)),
        grid=(n // size,),
        out_shape=[
            jax.ShapeDtypeStruct((n, D), F32),
            jax.ShapeDtypeStruct((n // H, H), F32),
        ],
        in_specs=[
            smem(),
            pl.BlockSpec((size, D), lambda i: (i, 0)),
            pl.BlockSpec((n // H, H), whole),
        ]
        + [pl.BlockSpec(piece.shape, whole) for piece in pieces],
        out_specs=[
            pl.BlockSpec((size, D), lambda i: (i, 0)),
            pl.BlockSpec((n // H, H), whole),
        ],
        cost_estimate=pl.CostEstimate(flops=8 * n * D, bytes_accessed=10 * n * D, transcendentals=n),
        compiler_params=pltpu.CompilerParams(vmem_limit_bytes=VMEM_LIMIT),
    )(place, rows, acc.reshape(n // H, H), *pieces)
    return new, new_acc.reshape(n)


def sum_rows_kernel(parts_ref, out_ref):
    total = parts_ref[0].astype(F32)
    for k in range(1, parts_ref.shape[0]):
        total = total + parts_ref[k].astype(F32)
    out_ref[...] = jnp.broadcast_to(total, out_ref.shape)


def sum_rows(parts):
    return call(
        sum_rows_kernel,
        jax.ShapeDtypeStruct(parts.shape, F32),
        0,
        1,
        flops=parts.size,
        bytes_accessed=6 * parts.size,
    )(parts)


def spread(parts):
    groups = [[2 * k + hi for k in range(32)] for hi in range(2)]
    return lax.all_to_all(parts, "blk", 0, 0, axis_index_groups=groups, tiled=True)


def swap(x, mask):
    return lax.ppermute(x, AXES, [(i, i ^ mask) for i in range(256)])


def shift(x, distance, mask):
    route = [(((i // 4 - distance) % 64) * 4 + ((i % 4) ^ mask), i) for i in range(256)]
    return lax.ppermute(x, AXES, route)


CORE, XL = 1, 2
X_MASKS = (2, 4, 6)


def shards(
    entities, entity_acc, relations, relation_acc, src_ids, rel_ids, dst_ids, neg_ids, counts
):
    blk, rep = lax.axis_index("blk"), lax.axis_index("rep")
    core, xl = rep % 2, rep // 2
    x = (blk % 2) * 2 + xl

    low = entities.astype(BF16)
    halves = [
        lax.dynamic_slice_in_dim(entities, core * 1024 + part * 512, 512, 0).astype(BF16)
        for part in range(2)
    ]
    near = [shift(part, -1, XL) for part in halves]

    ids = jnp.concatenate(
        [
            src_ids,
            rel_ids,
            dst_ids ^ (core * 1024),
            rel_ids ^ (core * 1024 + x * 256),
            src_ids ^ (core * 1024 + xl * 512),
            jnp.zeros((3, EDGES), jnp.int32),
        ],
        axis=0,
    )
    negs = (neg_ids ^ (core * 1024)).reshape(4, NEG)
    near_first, ids = lax.optimization_barrier((near[0], ids))
    head, rel_rows, prod, cnt = call(
        gather_kernel,
        [
            jax.ShapeDtypeStruct((EDGES, D), BF16),
            jax.ShapeDtypeStruct((EDGES, D), F32),
            jax.ShapeDtypeStruct((EDGES, D), F32),
            jax.ShapeDtypeStruct((4, ENT // H, H), F32),
        ],
        0,
        4,
        [pltpu.VMEM((NREL, D), BF16)] * 3,
    )(ids, negs, low, relations)

    kept = jax.ShapeDtypeStruct((ENT // 2, D), F32)
    sent = jax.ShapeDtypeStruct((ENT // 2, D), BF16)
    slots = jax.ShapeDtypeStruct((EDGES, D), F32)
    slots_low = jax.ShapeDtypeStruct((EDGES, D), BF16)
    weights = jax.ShapeDtypeStruct((EDGES, ENT // 2), BF16)
    far_first = swap(near_first, CORE)
    cc_first, tails, neg = call(
        first_score_kernel,
        [weights, slots, slots],
        0,
        5,
    )(ids, near_first, far_first, prod, cnt)
    near_second, tails = lax.optimization_barrier((near[1], tails))
    far_second = swap(near_second, CORE)
    rel_keep, rel_send, cc, plt, pd, gh = call(
        score_kernel,
        [kept, sent, weights, jax.ShapeDtypeStruct((D, EDGES), BF16), slots_low, slots_low],
        1,
        9,
        [pltpu.VMEM((EDGES, D), BF16)],
        flops=5 * EDGES * ENT * D,
        bytes_accessed=1 << 23,
    )(counts, ids, near_second, far_second, head, rel_rows, prod, cnt, tails, neg)
    rel_recv = swap(rel_send, CORE)
    parts = add_split([rel_keep, rel_recv], 4, own=F32)
    parts, cc = lax.optimization_barrier((parts, cc))
    recv = [swap(part, mask) for part, mask in zip(parts[1:], X_MASKS)]

    src_keep, src_send, dst_keep, dst_send = call(
        scatter_kernel,
        [kept, sent, kept, sent],
        1,
        6,
        flops=3 * 2 * EDGES * ENT * D,
        bytes_accessed=1 << 23,
    )(xl.reshape(1), ids, cc_first, cc, plt, pd, gh)
    recv, src_send, dst_send = lax.optimization_barrier((recv, src_send, dst_send))
    src_recv = swap(src_send, CORE)
    dst_recv = swap(dst_send, CORE)
    src_own, src_away = add_split([src_keep, src_recv], 2, own=F32)
    dst_own, dst_away = add_split([dst_keep, dst_recv], 2)
    (mine,) = add_split([parts[0], *recv], 1)
    src_other = swap(src_away, XL)
    dst_first = shift(dst_own, 1, 0)
    dst_second = shift(dst_away, 1, XL)

    landed = spread(mine.reshape(32, 8, D))
    landed, src_other, dst_first, dst_second = lax.optimization_barrier(
        (landed, src_other, dst_first, dst_second)
    )
    summed = sum_rows(landed)
    ent_own = sum_with_means([src_own, src_other, dst_first, dst_second])
    ent_xl = swap(ent_own, XL)
    ent_core = [swap(ent_own, CORE), swap(ent_xl, CORE)]
    place = (core * 2 + xl).reshape(1)
    new_entities, new_entity_acc = update(
        entities, entity_acc, [ent_own, ent_xl, *ent_core], place
    )
    total, new_entity_acc = lax.optimization_barrier((spread(summed), new_entity_acc))
    quarter = sum_with_means([total.reshape(256, D)])
    recv = [swap(quarter, mask) for mask in X_MASKS]

    pieces = [quarter, *recv]
    pieces = pieces + [swap(piece, CORE) for piece in pieces]
    place = (core * 4 + x).reshape(1)
    new_relations, new_relation_acc = update(relations, relation_acc, pieces, place)
    return (new_entities, new_entity_acc, new_relations, new_relation_acc)


def solution(mesh):
    in_specs = (
        P("blk", None),
        P("blk"),
        P(),
        P(),
        P("blk", "rep"),
        P("blk", "rep"),
        P("blk", "rep"),
        P("blk", "rep"),
        P("blk", "rep"),
    )
    out_specs = (P("blk", None), P("blk"), P(), P())
    return jax.shard_map(shards, mesh=mesh, in_specs=in_specs, out_specs=out_specs, check_vma=False)
```

```python
import functools

import jax
import jax.numpy as jnp
from jax import lax
from jax.experimental import pallas as pl
from jax.experimental.pallas import tpu as pltpu
from jax.sharding import PartitionSpec as P

F32 = jnp.float32
BF16 = jnp.bfloat16
D = 256
H = 128
ENT = 2048
EDGES = 1024
GROUP = 256
NEG = 1024
NREL = 2048
RATE = 0.1
AXES = ("blk", "rep")
VMEM_LIMIT = 48 * 1024 * 1024
CHUNK = 256
UNROLL = 4


def vmem():
    return pl.BlockSpec(memory_space=pltpu.VMEM)


def smem():
    return pl.BlockSpec(memory_space=pltpu.SMEM)


def call(kernel, out_shape, n_smem, n_vmem, scratch=(), flops=0, bytes_accessed=0):
    return pl.pallas_call(
        kernel,
        out_shape=out_shape,
        in_specs=[smem()] * n_smem + [vmem()] * n_vmem,
        out_specs=jax.tree.map(lambda _: vmem(), out_shape),
        scratch_shapes=list(scratch),
        cost_estimate=pl.CostEstimate(
            flops=flops, bytes_accessed=bytes_accessed, transcendentals=0
        ),
        compiler_params=pltpu.CompilerParams(vmem_limit_bytes=VMEM_LIMIT),
    )


def columns(row):
    n = row.shape[1]
    parts = [
        jnp.transpose(jnp.broadcast_to(row[:, i : i + H], (H, H))) for i in range(0, n, H)
    ]
    return parts[0] if len(parts) == 1 else jnp.concatenate(parts, axis=0)


def one_hot_rows(col, n, base=0):
    e = col.shape[0]
    lane = lax.broadcasted_iota(jnp.int32, (e, H), 1)
    parts = [jnp.where(col == lane + (base + j), 1.0, 0.0).astype(BF16) for j in range(0, n, H)]
    return jnp.concatenate(parts, axis=1)


def one_hot_cols(row, n, base):
    e = row.shape[1]
    sub = lax.broadcasted_iota(jnp.int32, (n, e), 0) + base
    return jnp.where(jnp.broadcast_to(row, (n, e)) == sub, 1.0, 0.0).astype(BF16)


def dot(a, b):
    return jnp.dot(a, b, preferred_element_type=F32)


def dot_nt(a, b):
    return lax.dot_general(a, b, (((1,), (1,)), ((), ())), preferred_element_type=F32)


def gather_kernel(ids_ref, negs_ref, low_ref, rel_ref, head_ref, relrow_ref, prod_ref, cnt_ref, hi_ref, mid_ref, lo_ref):
    for r in range(0, NREL, 256):
        x = rel_ref[r : r + 256, :]
        for ref in (hi_ref, mid_ref, lo_ref):
            part = x.astype(BF16)
            ref[r : r + 256, :] = part
            x = x - part.astype(F32)

    def group(g, _):
        rows = pl.ds(pl.multiple_of(g * GROUP, GROUP), GROUP)
        src = columns(ids_ref[0:1, rows])
        heads = dot(one_hot_rows(src, ENT), low_ref[...])
        pick = one_hot_rows(columns(ids_ref[1:2, rows]), NREL)
        rel = dot(pick, hi_ref[...]) + dot(pick, mid_ref[...]) + dot(pick, lo_ref[...])
        hr, hi, rr, ri = heads[:, :H], heads[:, H:], rel[:, :H], rel[:, H:]
        head_ref[rows, :] = heads.astype(BF16)
        relrow_ref[rows, :] = rel
        prod_ref[rows, :H] = hr * rr - hi * ri
        prod_ref[rows, H:] = hr * ri + hi * rr
        negs = negs_ref[pl.ds(g, 1), :]
        high = one_hot_cols(lax.shift_right_logical(negs, 7), ENT // H, 0)
        low = one_hot_cols(lax.bitwise_and(negs, H - 1), H, 0)
        cnt_ref[g] = dot_nt(high, low) * (1.0 / NEG)
        return 0

    lax.fori_loop(0, EDGES // GROUP, group, 0, unroll=UNROLL)


def against(part, ids_ref, near_ref, far_ref, prod_ref, cnt_ref, cc_ref, rows, g):
    size = near_ref.shape[0]
    dst = columns(ids_ref[2:3, rows])
    low = prod_ref[rows, :].astype(BF16)
    tails = neg = None
    for j, table in ((0, near_ref), (1, far_ref)):
        base = j * (ENT // 2) + part * size
        tail = dot(one_hot_rows(dst, size, base), table[...])
        scores = dot_nt(low, table[...])
        for i in range(size // H):
            w = cnt_ref[g, base // H + i : base // H + i + 1, :]
            cc_ref[rows, j * size + i * H : j * size + (i + 1) * H] = (
                jax.nn.sigmoid(scores[:, i * H : (i + 1) * H]) * w
            ).astype(BF16)
        drawn = dot(cc_ref[rows, j * size : (j + 1) * size], table[...])
        tails = tail if tails is None else tails + tail
        neg = drawn if neg is None else neg + drawn
    return tails, neg


def first_score_kernel(ids_ref, near_ref, far_ref, prod_ref, cnt_ref, cc_ref, tails_ref, neg_ref):
    def group(g, _):
        rows = pl.ds(pl.multiple_of(g * GROUP, GROUP), GROUP)
        tails, neg = against(0, ids_ref, near_ref, far_ref, prod_ref, cnt_ref, cc_ref, rows, g)
        tails_ref[rows, :] = tails
        neg_ref[rows, :] = neg
        return 0

    lax.fori_loop(0, EDGES // GROUP, group, 0, unroll=UNROLL)


def score_kernel(
    count_ref,
    ids_ref,
    near_ref,
    far_ref,
    head_ref,
    relrow_ref,
    prod_ref,
    cnt_ref,
    tails_ref,
    neg_ref,
    keep_ref,
    send_ref,
    cc_ref,
    plt_ref,
    pd_ref,
    gh_ref,
    gr_ref,
):
    half = ENT // 2
    count = count_ref[0, 0]

    def group(g, _):
        rows = pl.ds(pl.multiple_of(g * GROUP, GROUP), GROUP)
        tails, neg = against(1, ids_ref, near_ref, far_ref, prod_ref, cnt_ref, cc_ref, rows, g)
        tails = tails + tails_ref[rows, :]
        neg = neg + neg_ref[rows, :]
        prod = prod_ref[rows, :]
        edge = lax.broadcasted_iota(jnp.int32, (GROUP, 1), 0) + g * GROUP
        live = jnp.where(edge < count, 1.0, 0.0).astype(F32)
        positive = jnp.sum(prod * tails, axis=1, keepdims=True)
        pos = -live * jax.nn.sigmoid(-positive)
        grad = pos * tails + live * neg
        rel = relrow_ref[rows, :]
        head = head_ref[rows, :].astype(F32)
        gr, gi = grad[:, :H], grad[:, H:]
        for out, other in ((gh_ref, rel), (gr_ref, head)):
            a, b = other[:, :H], other[:, H:]
            out[rows, :H] = (gr * a + gi * b).astype(BF16)
            out[rows, H:] = (gi * a - gr * b).astype(BF16)
        pd_ref[rows, :] = (pos * prod).astype(BF16)
        plt_ref[:, rows] = jnp.transpose(live * prod).astype(BF16)
        return 0

    lax.fori_loop(0, EDGES // GROUP, group, 0, unroll=UNROLL)

    def scatter(i, _):
        rows = pl.ds(pl.multiple_of(i * CHUNK, CHUNK), CHUNK)
        keep_ref[rows, :] = dot(one_hot_cols(ids_ref[3:4, :], CHUNK, i * CHUNK), gr_ref[...])
        send_ref[rows, :] = dot(
            one_hot_cols(ids_ref[3:4, :], CHUNK, half + i * CHUNK), gr_ref[...]
        ).astype(BF16)
        return 0

    lax.fori_loop(0, half // CHUNK, scatter, 0, unroll=UNROLL)


def scatter_kernel(
    ids_ref,
    first_ref,
    second_ref,
    plt_ref,
    pd_ref,
    gh_ref,
    src_keep_ref,
    src_send_ref,
    dst_keep_ref,
    dst_send_ref,
):
    half = ENT // 2
    quarter = half // 2

    def scatter(i, part, cc_ref):
        at = part * quarter + i * CHUNK
        rows = pl.ds(at, CHUNK)
        for j, src_ref, dst_ref in (
            (0, src_keep_ref, dst_keep_ref),
            (1, src_send_ref, dst_send_ref),
        ):
            src = dot(one_hot_cols(ids_ref[4:5, :], CHUNK, j * half + at), gh_ref[...])
            src_ref[rows, :] = src.astype(src_ref.dtype)
            cols = pl.ds(j * quarter + i * CHUNK, CHUNK)
            drawn = jnp.transpose(dot(plt_ref[...], cc_ref[:, cols]))
            dst = dot(one_hot_cols(ids_ref[2:3, :], CHUNK, j * half + at), pd_ref[...])
            dst_ref[rows, :] = (drawn + dst).astype(dst_ref.dtype)

    for part, ref in ((0, first_ref), (1, second_ref)):
        for i in range(quarter // CHUNK):
            scatter(i, part, ref)


def add_split_kernel(n_in, n_out, *refs):
    ins, outs = refs[:n_in], refs[n_in:]
    size = outs[0].shape[0]
    step = min(size, 64)
    for k, out in enumerate(outs):
        for r in range(0, size, step):
            total = ins[0][k * size + r : k * size + r + step, :].astype(F32)
            for ref in ins[1:]:
                total = total + ref[k * size + r : k * size + r + step, :].astype(F32)
            out[r : r + step, :] = total.astype(out.dtype)


def add_split(parts, n_out, own=BF16, sent=BF16):
    rows = parts[0].shape[0] // n_out
    shapes = [jax.ShapeDtypeStruct((rows, D), sent if k else own) for k in range(n_out)]
    return call(
        functools.partial(add_split_kernel, len(parts), n_out),
        shapes,
        0,
        len(parts),
        flops=len(parts) * n_out * rows * D,
        bytes_accessed=3 * len(parts) * n_out * rows * D,
    )(*parts)


def split3(x):
    hi = x.astype(BF16).astype(F32)
    mid = (x - hi).astype(BF16).astype(F32)
    return hi, mid, x - hi - mid


def sum_with_means_kernel(*refs):
    parts, out_ref = refs[:-1], refs[-1]
    rows = parts[0].shape[0]
    means = []
    for r in range(0, rows, H):
        total = parts[0][r : r + H, :].astype(F32)
        for ref in parts[1:]:
            total = total + ref[r : r + H, :].astype(F32)
        out_ref[r : r + H, :] = total.astype(BF16)
        mean = jnp.sum(total * total, axis=1, keepdims=True) * (1.0 / D)
        means.append(jnp.transpose(jnp.broadcast_to(mean, (H, H)))[0:1, :])
    means.append(jnp.zeros((8 - len(means), H), F32))
    hi, mid, lo = split3(jnp.concatenate(means, axis=0))
    top = jnp.concatenate([hi, mid], axis=1)
    bottom = jnp.concatenate([lo, jnp.zeros_like(lo)], axis=1)
    out_ref[rows : rows + 16, :] = jnp.concatenate([top, bottom], axis=0).astype(BF16)


def sum_with_means(parts):
    rows = parts[0].shape[0]
    return call(
        sum_with_means_kernel,
        jax.ShapeDtypeStruct((rows + 16, D), BF16),
        0,
        len(parts),
        flops=len(parts) * rows * D,
        bytes_accessed=3 * len(parts) * rows * D,
    )(*parts)


def means_of(piece, start, row):
    tile = piece[start : start + 16, :].astype(F32)
    return tile[row : row + 1, :H] + tile[row : row + 1, H:] + tile[8 + row : 9 + row, :H]


def update_kernel(n, place_ref, rows_ref, acc_ref, *refs):
    pieces, (new_ref, new_acc_ref, buf_ref, sem_ref) = refs[:n], refs[n:]
    size = rows_ref.shape[0] // n
    copies = []
    for k, piece in enumerate(pieces):
        i = lax.bitwise_xor(k, place_ref[0])
        for r in range(0, size, H):
            g = piece[r : r + H, :].astype(F32)
            at = pl.ds(i * (size // H) + r // H, 1)
            acc = acc_ref[at, :] + means_of(piece, size, r // H)
            new_acc_ref[at, :] = acc
            scale = jnp.transpose(jnp.broadcast_to(RATE / jnp.sqrt(acc), (H, H)))
            rows = pl.ds(pl.multiple_of(i * size + r, H), H)
            buf_ref[rows, :H] = rows_ref[rows, :H] - g[:, :H] * scale
            buf_ref[rows, H:] = rows_ref[rows, H:] - g[:, H:] * scale
        rows = pl.ds(pl.multiple_of(i * size, size), size)
        copy = pltpu.make_async_copy(buf_ref.at[rows, :], new_ref.at[rows, :], sem_ref.at[k])
        copy.start()
        copies.append(copy)
    for copy in copies:
        copy.wait()


def update(rows, acc, pieces, place):
    n = rows.shape[0]
    new, new_acc = pl.pallas_call(
        functools.partial(update_kernel, len(pieces)),
        out_shape=[
            jax.ShapeDtypeStruct((n, D), F32),
            jax.ShapeDtypeStruct((n // H, H), F32),
        ],
        in_specs=[smem()] + [vmem()] * (2 + len(pieces)),
        out_specs=[pl.BlockSpec(memory_space=pl.ANY), vmem()],
        scratch_shapes=[pltpu.VMEM((n, D), F32), pltpu.SemaphoreType.DMA((len(pieces),))],
        cost_estimate=pl.CostEstimate(flops=8 * n * D, bytes_accessed=10 * n * D, transcendentals=n),
        compiler_params=pltpu.CompilerParams(vmem_limit_bytes=VMEM_LIMIT),
    )(place, rows, acc.reshape(n // H, H), *pieces)
    return new, new_acc.reshape(n)


def sum_rows_kernel(parts_ref, out_ref):
    total = parts_ref[0].astype(F32)
    for k in range(1, parts_ref.shape[0]):
        total = total + parts_ref[k].astype(F32)
    out_ref[...] = jnp.broadcast_to(total, out_ref.shape)


def sum_rows(parts):
    return call(
        sum_rows_kernel,
        jax.ShapeDtypeStruct(parts.shape, F32),
        0,
        1,
        flops=parts.size,
        bytes_accessed=6 * parts.size,
    )(parts)


def spread(parts):
    groups = [[2 * k + hi for k in range(32)] for hi in range(2)]
    return lax.all_to_all(parts, "blk", 0, 0, axis_index_groups=groups, tiled=True)


def swap(x, mask):
    return lax.ppermute(x, AXES, [(i, i ^ mask) for i in range(256)])


def shift(x, distance, mask):
    route = [(((i // 4 - distance) % 64) * 4 + ((i % 4) ^ mask), i) for i in range(256)]
    return lax.ppermute(x, AXES, route)


CORE, XL = 1, 2
X_MASKS = (2, 4, 6)


def shards(
    entities, entity_acc, relations, relation_acc, src_ids, rel_ids, dst_ids, neg_ids, counts
):
    blk, rep = lax.axis_index("blk"), lax.axis_index("rep")
    core, xl = rep % 2, rep // 2
    x = (blk % 2) * 2 + xl

    low = entities.astype(BF16)
    quarter = lax.dynamic_slice_in_dim(entities, core * 1024 + (1 - xl) * 512, 512, 0)
    near_first = shift(quarter.astype(BF16), -1, XL)

    ids = jnp.concatenate(
        [
            src_ids,
            rel_ids,
            dst_ids ^ (core * 1024 + xl * 512),
            rel_ids ^ (core * 1024 + x * 256),
            src_ids ^ (core * 1024 + xl * 512),
            jnp.zeros((3, EDGES), jnp.int32),
        ],
        axis=0,
    )
    negs = (neg_ids ^ (core * 1024 + xl * 512)).reshape(4, NEG)
    head, rel_rows, prod, cnt = call(
        gather_kernel,
        [
            jax.ShapeDtypeStruct((EDGES, D), BF16),
            jax.ShapeDtypeStruct((EDGES, D), F32),
            jax.ShapeDtypeStruct((EDGES, D), F32),
            jax.ShapeDtypeStruct((4, ENT // H, H), F32),
        ],
        0,
        4,
        [pltpu.VMEM((NREL, D), BF16)] * 3,
        flops=4 * 2 * EDGES * ENT * D,
        bytes_accessed=1 << 22,
    )(ids, negs, low, relations)

    kept = jax.ShapeDtypeStruct((ENT // 2, D), F32)
    sent = jax.ShapeDtypeStruct((ENT // 2, D), BF16)
    slots = jax.ShapeDtypeStruct((EDGES, D), F32)
    slots_low = jax.ShapeDtypeStruct((EDGES, D), BF16)
    weights = jax.ShapeDtypeStruct((EDGES, ENT // 2), BF16)
    near_first, head = lax.optimization_barrier((near_first, head))
    near_second = swap(near_first, XL)
    far_first = swap(near_first, CORE)
    cc_first, tails, neg = call(
        first_score_kernel,
        [weights, slots, slots],
        0,
        5,
        flops=3 * EDGES * ENT * D,
        bytes_accessed=1 << 22,
    )(ids, near_first, far_first, prod, cnt)
    near_second, tails = lax.optimization_barrier((near_second, tails))
    far_second = swap(near_second, CORE)
    rel_keep, rel_send, cc, plt, pd, gh = call(
        score_kernel,
        [kept, sent, weights, jax.ShapeDtypeStruct((D, EDGES), BF16), slots_low, slots_low],
        1,
        9,
        [pltpu.VMEM((EDGES, D), BF16)],
        flops=5 * EDGES * ENT * D,
        bytes_accessed=1 << 23,
    )(counts, ids, near_second, far_second, head, rel_rows, prod, cnt, tails, neg)
    rel_recv = swap(rel_send, CORE)
    parts = add_split([rel_keep, rel_recv], 4, own=F32)
    parts, cc = lax.optimization_barrier((parts, cc))
    recv = [swap(part, mask) for part, mask in zip(parts[1:], X_MASKS)]

    src_keep, src_send, dst_keep, dst_send = call(
        scatter_kernel,
        [kept, sent, kept, sent],
        0,
        6,
        flops=3 * 2 * EDGES * ENT * D,
        bytes_accessed=1 << 23,
    )(ids, cc_first, cc, plt, pd, gh)
    recv, src_send, dst_send = lax.optimization_barrier((recv, src_send, dst_send))
    src_recv = swap(src_send, CORE)
    dst_recv = swap(dst_send, CORE)
    src_own, src_away = add_split([src_keep, src_recv], 2, own=F32)
    dst_own, dst_away = add_split([dst_keep, dst_recv], 2)
    (mine,) = add_split([parts[0], *recv], 1)
    src_other = swap(src_away, XL)
    dst_first = shift(dst_own, 1, 0)
    dst_second = shift(dst_away, 1, XL)

    landed = spread(mine.reshape(32, 8, D))
    summed = sum_rows(landed)
    ent_own = sum_with_means([src_own, src_other, dst_first, dst_second])
    ent_xl = swap(ent_own, XL)
    ent_core = [swap(ent_own, CORE), swap(ent_xl, CORE)]
    place = (core * 2 + xl).reshape(1)
    new_entities, new_entity_acc = update(
        entities, entity_acc, [ent_own, ent_xl, *ent_core], place
    )
    total = spread(summed)
    quarter = sum_with_means([total.reshape(256, D)])
    recv = [swap(quarter, mask) for mask in X_MASKS]

    pieces = [quarter, *recv]
    pieces = pieces + [swap(piece, CORE) for piece in pieces]
    pieces, new_entity_acc = lax.optimization_barrier((pieces, new_entity_acc))
    place = (core * 4 + x).reshape(1)
    new_relations, new_relation_acc = update(relations, relation_acc, pieces, place)
    return (new_entities, new_entity_acc, new_relations, new_relation_acc)


def solution(mesh):
    in_specs = (
        P("blk", None),
        P("blk"),
        P(),
        P(),
        P("blk", "rep"),
        P("blk", "rep"),
        P("blk", "rep"),
        P("blk", "rep"),
        P("blk", "rep"),
    )
    out_specs = (P("blk", None), P("blk"), P(), P())
    return jax.shard_map(shards, mesh=mesh, in_specs=in_specs, out_specs=out_specs, check_vma=False)
```

```python
import functools

import jax
import jax.numpy as jnp
from jax import lax
from jax.experimental import pallas as pl
from jax.experimental.pallas import tpu as pltpu
from jax.sharding import PartitionSpec as P

F32 = jnp.float32
BF16 = jnp.bfloat16
D = 256
H = 128
ENT = 2048
EDGES = 1024
GROUP = 256
NEG = 1024
NREL = 2048
RATE = 0.1
AXES = ("blk", "rep")
VMEM_LIMIT = 48 * 1024 * 1024
CHUNK = 256
UNROLL = 4


def vmem():
    return pl.BlockSpec(memory_space=pltpu.VMEM)


def smem():
    return pl.BlockSpec(memory_space=pltpu.SMEM)


def call(kernel, out_shape, n_smem, n_vmem, scratch=(), flops=0, bytes_accessed=0):
    return pl.pallas_call(
        kernel,
        out_shape=out_shape,
        in_specs=[smem()] * n_smem + [vmem()] * n_vmem,
        out_specs=jax.tree.map(lambda _: vmem(), out_shape),
        scratch_shapes=list(scratch),
        cost_estimate=pl.CostEstimate(
            flops=flops, bytes_accessed=bytes_accessed, transcendentals=0
        ),
        compiler_params=pltpu.CompilerParams(vmem_limit_bytes=VMEM_LIMIT),
    )


def columns(row):
    n = row.shape[1]
    parts = [
        jnp.transpose(jnp.broadcast_to(row[:, i : i + H], (H, H))) for i in range(0, n, H)
    ]
    return parts[0] if len(parts) == 1 else jnp.concatenate(parts, axis=0)


def one_hot_rows(col, n, base=0):
    e = col.shape[0]
    lane = lax.broadcasted_iota(jnp.int32, (e, H), 1)
    parts = [jnp.where(col == lane + (base + j), 1.0, 0.0).astype(BF16) for j in range(0, n, H)]
    return jnp.concatenate(parts, axis=1)


def one_hot_cols(row, n, base):
    e = row.shape[1]
    sub = lax.broadcasted_iota(jnp.int32, (n, e), 0) + base
    return jnp.where(jnp.broadcast_to(row, (n, e)) == sub, 1.0, 0.0).astype(BF16)


def dot(a, b):
    return jnp.dot(a, b, preferred_element_type=F32)


def dot_nt(a, b):
    return lax.dot_general(a, b, (((1,), (1,)), ((), ())), preferred_element_type=F32)


def gather_kernel(ids_ref, negs_ref, low_ref, rel_ref, head_ref, relrow_ref, prod_ref, cnt_ref, hi_ref, mid_ref, lo_ref):
    for r in range(0, NREL, 256):
        x = rel_ref[r : r + 256, :]
        for ref in (hi_ref, mid_ref, lo_ref):
            part = x.astype(BF16)
            ref[r : r + 256, :] = part
            x = x - part.astype(F32)

    def group(g, _):
        rows = pl.ds(pl.multiple_of(g * GROUP, GROUP), GROUP)
        src = columns(ids_ref[0:1, rows])
        heads = dot(one_hot_rows(src, ENT), low_ref[...])
        pick = one_hot_rows(columns(ids_ref[1:2, rows]), NREL)
        rel = dot(pick, hi_ref[...]) + dot(pick, mid_ref[...]) + dot(pick, lo_ref[...])
        hr, hi, rr, ri = heads[:, :H], heads[:, H:], rel[:, :H], rel[:, H:]
        head_ref[rows, :] = heads.astype(BF16)
        relrow_ref[rows, :] = rel
        prod_ref[rows, :H] = hr * rr - hi * ri
        prod_ref[rows, H:] = hr * ri + hi * rr
        negs = negs_ref[pl.ds(g, 1), :]
        high = one_hot_cols(lax.shift_right_logical(negs, 7), ENT // H, 0)
        low = one_hot_cols(lax.bitwise_and(negs, H - 1), H, 0)
        cnt_ref[g] = dot_nt(high, low) * (1.0 / NEG)
        return 0

    lax.fori_loop(0, EDGES // GROUP, group, 0, unroll=UNROLL)


def against(part, ids_ref, near_ref, far_ref, prod_ref, cnt_ref, cc_ref, rows, g):
    size = near_ref.shape[0]
    dst = columns(ids_ref[2:3, rows])
    low = prod_ref[rows, :].astype(BF16)
    tails = neg = None
    for j, table in ((0, near_ref), (1, far_ref)):
        base = j * (ENT // 2) + part * size
        tail = dot(one_hot_rows(dst, size, base), table[...])
        scores = dot_nt(low, table[...])
        for i in range(size // H):
            w = cnt_ref[g, base // H + i : base // H + i + 1, :]
            cc_ref[rows, j * size + i * H : j * size + (i + 1) * H] = (
                jax.nn.sigmoid(scores[:, i * H : (i + 1) * H]) * w
            ).astype(BF16)
        drawn = dot(cc_ref[rows, j * size : (j + 1) * size], table[...])
        tails = tail if tails is None else tails + tail
        neg = drawn if neg is None else neg + drawn
    return tails, neg


def first_score_kernel(ids_ref, near_ref, far_ref, prod_ref, cnt_ref, cc_ref, tails_ref, neg_ref):
    def group(g, _):
        rows = pl.ds(pl.multiple_of(g * GROUP, GROUP), GROUP)
        tails, neg = against(0, ids_ref, near_ref, far_ref, prod_ref, cnt_ref, cc_ref, rows, g)
        tails_ref[rows, :] = tails
        neg_ref[rows, :] = neg
        return 0

    lax.fori_loop(0, EDGES // GROUP, group, 0, unroll=UNROLL)


def score_kernel(
    count_ref,
    ids_ref,
    near_ref,
    far_ref,
    head_ref,
    relrow_ref,
    prod_ref,
    cnt_ref,
    tails_ref,
    neg_ref,
    first_ref,
    src_keep_ref,
    src_send_ref,
    dst_keep_ref,
    dst_send_ref,
    gr_ref,
    cc_ref,
    plt_ref,
    pd_ref,
    gh_ref,
):
    half = ENT // 2
    quarter = half // 2
    count = count_ref[0, 0]

    def group(g, _):
        rows = pl.ds(pl.multiple_of(g * GROUP, GROUP), GROUP)
        tails, neg = against(1, ids_ref, near_ref, far_ref, prod_ref, cnt_ref, cc_ref, rows, g)
        tails = tails + tails_ref[rows, :]
        neg = neg + neg_ref[rows, :]
        prod = prod_ref[rows, :]
        edge = lax.broadcasted_iota(jnp.int32, (GROUP, 1), 0) + g * GROUP
        live = jnp.where(edge < count, 1.0, 0.0).astype(F32)
        positive = jnp.sum(prod * tails, axis=1, keepdims=True)
        pos = -live * jax.nn.sigmoid(-positive)
        grad = pos * tails + live * neg
        rel = relrow_ref[rows, :]
        head = head_ref[rows, :].astype(F32)
        gr, gi = grad[:, :H], grad[:, H:]
        for out, other in ((gh_ref, rel), (gr_ref, head)):
            a, b = other[:, :H], other[:, H:]
            out[rows, :H] = (gr * a + gi * b).astype(BF16)
            out[rows, H:] = (gi * a - gr * b).astype(BF16)
        pd_ref[rows, :] = (pos * prod).astype(BF16)
        plt_ref[:, rows] = jnp.transpose(live * prod).astype(BF16)
        return 0

    lax.fori_loop(0, EDGES // GROUP, group, 0, unroll=UNROLL)

    for part, ref in ((0, first_ref), (1, cc_ref)):
        for i in range(quarter // CHUNK):
            at = part * quarter + i * CHUNK
            rows = slice(at, at + CHUNK)
            for j, src_ref, dst_ref in (
                (0, src_keep_ref, dst_keep_ref),
                (1, src_send_ref, dst_send_ref),
            ):
                src = dot(one_hot_cols(ids_ref[4:5, :], CHUNK, j * half + at), gh_ref[...])
                src_ref[rows, :] = src.astype(src_ref.dtype)
                cols = slice(j * quarter + i * CHUNK, j * quarter + (i + 1) * CHUNK)
                drawn = jnp.transpose(dot(plt_ref[...], ref[:, cols]))
                dst = dot(one_hot_cols(ids_ref[2:3, :], CHUNK, j * half + at), pd_ref[...])
                dst_ref[rows, :] = (drawn + dst).astype(dst_ref.dtype)


def relation_kernel(ids_ref, gr_ref, keep_ref, send_ref):
    half = NREL // 2
    for i in range(half // CHUNK):
        rows = slice(i * CHUNK, (i + 1) * CHUNK)
        keep_ref[rows, :] = dot(one_hot_cols(ids_ref[3:4, :], CHUNK, i * CHUNK), gr_ref[...])
        send_ref[rows, :] = dot(
            one_hot_cols(ids_ref[3:4, :], CHUNK, half + i * CHUNK), gr_ref[...]
        ).astype(BF16)


def add_split_kernel(n_in, n_out, *refs):
    ins, outs = refs[:n_in], refs[n_in:]
    size = outs[0].shape[0]
    step = min(size, 64)
    for k, out in enumerate(outs):
        for r in range(0, size, step):
            total = ins[0][k * size + r : k * size + r + step, :].astype(F32)
            for ref in ins[1:]:
                total = total + ref[k * size + r : k * size + r + step, :].astype(F32)
            out[r : r + step, :] = total.astype(out.dtype)


def add_split(parts, n_out, own=BF16, sent=BF16):
    rows = parts[0].shape[0] // n_out
    shapes = [jax.ShapeDtypeStruct((rows, D), sent if k else own) for k in range(n_out)]
    return call(
        functools.partial(add_split_kernel, len(parts), n_out),
        shapes,
        0,
        len(parts),
        flops=len(parts) * n_out * rows * D,
        bytes_accessed=3 * len(parts) * n_out * rows * D,
    )(*parts)


def split3(x):
    hi = x.astype(BF16).astype(F32)
    mid = (x - hi).astype(BF16).astype(F32)
    return hi, mid, x - hi - mid


def sum_with_means_kernel(*refs):
    parts, out_ref = refs[:-1], refs[-1]
    rows = parts[0].shape[0]
    means = []
    for r in range(0, rows, H):
        total = parts[0][r : r + H, :].astype(F32)
        for ref in parts[1:]:
            total = total + ref[r : r + H, :].astype(F32)
        out_ref[r : r + H, :] = total.astype(BF16)
        mean = jnp.sum(total * total, axis=1, keepdims=True) * (1.0 / D)
        means.append(jnp.transpose(jnp.broadcast_to(mean, (H, H)))[0:1, :])
    means.append(jnp.zeros((8 - len(means), H), F32))
    hi, mid, lo = split3(jnp.concatenate(means, axis=0))
    top = jnp.concatenate([hi, mid], axis=1)
    bottom = jnp.concatenate([lo, jnp.zeros_like(lo)], axis=1)
    out_ref[rows : rows + 16, :] = jnp.concatenate([top, bottom], axis=0).astype(BF16)


def sum_with_means(parts):
    rows = parts[0].shape[0]
    return call(
        sum_with_means_kernel,
        jax.ShapeDtypeStruct((rows + 16, D), BF16),
        0,
        len(parts),
        flops=len(parts) * rows * D,
        bytes_accessed=3 * len(parts) * rows * D,
    )(*parts)


def means_of(piece, start, row):
    tile = piece[start : start + 16, :].astype(F32)
    return tile[row : row + 1, :H] + tile[row : row + 1, H:] + tile[8 + row : 9 + row, :H]


def update_kernel(n, place_ref, rows_ref, acc_ref, *refs):
    pieces, (new_ref, new_acc_ref, buf_ref, sem_ref) = refs[:n], refs[n:]
    size = rows_ref.shape[0] // n
    copies = []
    for k, piece in enumerate(pieces):
        i = lax.bitwise_xor(k, place_ref[0])
        for r in range(0, size, H):
            g = piece[r : r + H, :].astype(F32)
            at = pl.ds(i * (size // H) + r // H, 1)
            acc = acc_ref[at, :] + means_of(piece, size, r // H)
            new_acc_ref[at, :] = acc
            scale = jnp.transpose(jnp.broadcast_to(RATE / jnp.sqrt(acc), (H, H)))
            rows = pl.ds(pl.multiple_of(i * size + r, H), H)
            buf_ref[rows, :H] = rows_ref[rows, :H] - g[:, :H] * scale
            buf_ref[rows, H:] = rows_ref[rows, H:] - g[:, H:] * scale
        rows = pl.ds(pl.multiple_of(i * size, size), size)
        copy = pltpu.make_async_copy(buf_ref.at[rows, :], new_ref.at[rows, :], sem_ref.at[k])
        copy.start()
        copies.append(copy)
    for copy in copies:
        copy.wait()


def update(rows, acc, pieces, place):
    n = rows.shape[0]
    new, new_acc = pl.pallas_call(
        functools.partial(update_kernel, len(pieces)),
        out_shape=[
            jax.ShapeDtypeStruct((n, D), F32),
            jax.ShapeDtypeStruct((n // H, H), F32),
        ],
        in_specs=[smem()] + [vmem()] * (2 + len(pieces)),
        out_specs=[pl.BlockSpec(memory_space=pl.ANY), vmem()],
        scratch_shapes=[pltpu.VMEM((n, D), F32), pltpu.SemaphoreType.DMA((len(pieces),))],
        cost_estimate=pl.CostEstimate(flops=8 * n * D, bytes_accessed=10 * n * D, transcendentals=n),
        compiler_params=pltpu.CompilerParams(vmem_limit_bytes=VMEM_LIMIT),
    )(place, rows, acc.reshape(n // H, H), *pieces)
    return new, new_acc.reshape(n)


def sum_rows_kernel(parts_ref, out_ref):
    total = parts_ref[0].astype(F32)
    for k in range(1, parts_ref.shape[0]):
        total = total + parts_ref[k].astype(F32)
    out_ref[...] = jnp.broadcast_to(total, out_ref.shape)


def sum_rows(parts):
    return call(
        sum_rows_kernel,
        jax.ShapeDtypeStruct(parts.shape, F32),
        0,
        1,
        flops=parts.size,
        bytes_accessed=6 * parts.size,
    )(parts)


def spread(parts):
    groups = [[2 * k + hi for k in range(32)] for hi in range(2)]
    return lax.all_to_all(parts, "blk", 0, 0, axis_index_groups=groups, tiled=True)


def swap(x, mask):
    return lax.ppermute(x, AXES, [(i, i ^ mask) for i in range(256)])


def shift(x, distance, mask):
    route = [(((i // 4 - distance) % 64) * 4 + ((i % 4) ^ mask), i) for i in range(256)]
    return lax.ppermute(x, AXES, route)


CORE, XL = 1, 2
X_MASKS = (2, 4, 6)


def shards(
    entities, entity_acc, relations, relation_acc, src_ids, rel_ids, dst_ids, neg_ids, counts
):
    blk, rep = lax.axis_index("blk"), lax.axis_index("rep")
    core, xl = rep % 2, rep // 2
    x = (blk % 2) * 2 + xl

    low = entities.astype(BF16)
    quarter = lax.dynamic_slice_in_dim(entities, core * 1024 + (1 - xl) * 512, 512, 0)
    near_first = shift(quarter.astype(BF16), -1, XL)

    ids = jnp.concatenate(
        [
            src_ids,
            rel_ids,
            dst_ids ^ (core * 1024 + xl * 512),
            rel_ids ^ (core * 1024 + x * 256),
            src_ids ^ (core * 1024 + xl * 512),
            jnp.zeros((3, EDGES), jnp.int32),
        ],
        axis=0,
    )
    negs = (neg_ids ^ (core * 1024 + xl * 512)).reshape(4, NEG)
    head, rel_rows, prod, cnt = call(
        gather_kernel,
        [
            jax.ShapeDtypeStruct((EDGES, D), BF16),
            jax.ShapeDtypeStruct((EDGES, D), F32),
            jax.ShapeDtypeStruct((EDGES, D), F32),
            jax.ShapeDtypeStruct((4, ENT // H, H), F32),
        ],
        0,
        4,
        [pltpu.VMEM((NREL, D), BF16)] * 3,
        flops=4 * 2 * EDGES * ENT * D,
        bytes_accessed=1 << 22,
    )(ids, negs, low, relations)

    kept = jax.ShapeDtypeStruct((ENT // 2, D), F32)
    sent = jax.ShapeDtypeStruct((ENT // 2, D), BF16)
    slots = jax.ShapeDtypeStruct((EDGES, D), F32)
    slots_low = jax.ShapeDtypeStruct((EDGES, D), BF16)
    weights = jax.ShapeDtypeStruct((EDGES, ENT // 2), BF16)
    near_first, head = lax.optimization_barrier((near_first, head))
    near_second = swap(near_first, XL)
    far_first = swap(near_first, CORE)
    cc_first, tails, neg = call(
        first_score_kernel,
        [weights, slots, slots],
        0,
        5,
        flops=3 * EDGES * ENT * D,
        bytes_accessed=1 << 22,
    )(ids, near_first, far_first, prod, cnt)
    near_second, tails = lax.optimization_barrier((near_second, tails))
    far_second = swap(near_second, CORE)
    src_keep, src_send, dst_keep, dst_send, gr = call(
        score_kernel,
        [kept, sent, kept, sent, slots_low],
        1,
        10,
        [
            pltpu.VMEM((EDGES, ENT // 2), BF16),
            pltpu.VMEM((D, EDGES), BF16),
            pltpu.VMEM((EDGES, D), BF16),
            pltpu.VMEM((EDGES, D), BF16),
        ],
        flops=9 * EDGES * ENT * D,
        bytes_accessed=1 << 23,
    )(counts, ids, near_second, far_second, head, rel_rows, prod, cnt, tails, neg, cc_first)
    src_recv = swap(src_send, CORE)
    dst_recv = swap(dst_send, CORE)
    rel_keep, rel_send = call(
        relation_kernel,
        [kept, sent],
        0,
        2,
        flops=2 * EDGES * NREL * D,
        bytes_accessed=1 << 21,
    )(ids, gr)

    rel_recv = swap(rel_send, CORE)
    src_own, src_away = add_split([src_keep, src_recv], 2, own=F32)
    dst_own, dst_away = add_split([dst_keep, dst_recv], 2)
    parts = add_split([rel_keep, rel_recv], 4, own=F32)
    parts, src_away, dst_own, dst_away = lax.optimization_barrier(
        (parts, src_away, dst_own, dst_away)
    )
    recv = [swap(part, mask) for part, mask in zip(parts[1:], X_MASKS)]
    src_other = swap(src_away, XL)
    dst_first = shift(dst_own, 1, 0)
    dst_second = shift(dst_away, 1, XL)
    (mine,) = add_split([parts[0], *recv], 1)

    landed = spread(mine.reshape(32, 8, D))
    ent_own = sum_with_means([src_own, src_other, dst_first, dst_second])
    landed, ent_own = lax.optimization_barrier((landed, ent_own))
    summed = sum_rows(landed)
    ent_xl = swap(ent_own, XL)
    ent_core = [swap(ent_own, CORE), swap(ent_xl, CORE)]
    place = (core * 2 + xl).reshape(1)
    new_entities, new_entity_acc = update(
        entities, entity_acc, [ent_own, ent_xl, *ent_core], place
    )
    total, new_entity_acc = lax.optimization_barrier((spread(summed), new_entity_acc))
    quarter = sum_with_means([total.reshape(256, D)])
    recv = [swap(quarter, mask) for mask in X_MASKS]

    pieces = [quarter, *recv]
    pieces = pieces + [swap(piece, CORE) for piece in pieces]
    place = (core * 4 + x).reshape(1)
    new_relations, new_relation_acc = update(relations, relation_acc, pieces, place)
    return (new_entities, new_entity_acc, new_relations, new_relation_acc)


def solution(mesh):
    in_specs = (
        P("blk", None),
        P("blk"),
        P(),
        P(),
        P("blk", "rep"),
        P("blk", "rep"),
        P("blk", "rep"),
        P("blk", "rep"),
        P("blk", "rep"),
    )
    out_specs = (P("blk", None), P("blk"), P(), P())
    return jax.shard_map(shards, mesh=mesh, in_specs=in_specs, out_specs=out_specs, check_vma=False)
```

```python
import functools

import jax
import jax.numpy as jnp
from jax import lax
from jax.experimental import pallas as pl
from jax.experimental.pallas import tpu as pltpu
from jax.sharding import PartitionSpec as P

F32 = jnp.float32
BF16 = jnp.bfloat16
D = 256
H = 128
ENT = 2048
EDGES = 1024
GROUP = 256
NEG = 1024
NREL = 2048
RATE = 0.1
AXES = ("blk", "rep")
VMEM_LIMIT = 48 * 1024 * 1024
CHUNK = 256
UNROLL = 4


def vmem():
    return pl.BlockSpec(memory_space=pltpu.VMEM)


def smem():
    return pl.BlockSpec(memory_space=pltpu.SMEM)


def call(kernel, out_shape, n_smem, n_vmem, scratch=(), flops=0, bytes_accessed=0):
    return pl.pallas_call(
        kernel,
        out_shape=out_shape,
        in_specs=[smem()] * n_smem + [vmem()] * n_vmem,
        out_specs=jax.tree.map(lambda _: vmem(), out_shape),
        scratch_shapes=list(scratch),
        cost_estimate=pl.CostEstimate(
            flops=flops, bytes_accessed=bytes_accessed, transcendentals=0
        ),
        compiler_params=pltpu.CompilerParams(vmem_limit_bytes=VMEM_LIMIT),
    )


def columns(row):
    n = row.shape[1]
    parts = [
        jnp.transpose(jnp.broadcast_to(row[:, i : i + H], (H, H))) for i in range(0, n, H)
    ]
    return parts[0] if len(parts) == 1 else jnp.concatenate(parts, axis=0)


def one_hot_rows(col, n, base=0):
    e = col.shape[0]
    lane = lax.broadcasted_iota(jnp.int32, (e, H), 1)
    parts = [jnp.where(col == lane + (base + j), 1.0, 0.0).astype(BF16) for j in range(0, n, H)]
    return jnp.concatenate(parts, axis=1)


def one_hot_cols(row, n, base):
    e = row.shape[1]
    sub = lax.broadcasted_iota(jnp.int32, (n, e), 0) + base
    return jnp.where(jnp.broadcast_to(row, (n, e)) == sub, 1.0, 0.0).astype(BF16)


def dot(a, b):
    return jnp.dot(a, b, preferred_element_type=F32)


def dot_nt(a, b):
    return lax.dot_general(a, b, (((1,), (1,)), ((), ())), preferred_element_type=F32)


def gather_kernel(ids_ref, negs_ref, low_ref, rel_ref, head_ref, relrow_ref, prod_ref, cnt_ref, hi_ref, mid_ref, lo_ref):
    for r in range(0, NREL, 256):
        x = rel_ref[r : r + 256, :]
        for ref in (hi_ref, mid_ref, lo_ref):
            part = x.astype(BF16)
            ref[r : r + 256, :] = part
            x = x - part.astype(F32)

    def group(g, _):
        rows = pl.ds(pl.multiple_of(g * GROUP, GROUP), GROUP)
        src = columns(ids_ref[0:1, rows])
        heads = dot(one_hot_rows(src, ENT), low_ref[...])
        pick = one_hot_rows(columns(ids_ref[1:2, rows]), NREL)
        rel = dot(pick, hi_ref[...]) + dot(pick, mid_ref[...]) + dot(pick, lo_ref[...])
        hr, hi, rr, ri = heads[:, :H], heads[:, H:], rel[:, :H], rel[:, H:]
        head_ref[rows, :] = heads.astype(BF16)
        relrow_ref[rows, :] = rel
        prod_ref[rows, :H] = hr * rr - hi * ri
        prod_ref[rows, H:] = hr * ri + hi * rr
        negs = negs_ref[pl.ds(g, 1), :]
        high = one_hot_cols(lax.shift_right_logical(negs, 7), ENT // H, 0)
        low = one_hot_cols(lax.bitwise_and(negs, H - 1), H, 0)
        cnt_ref[g] = dot_nt(high, low) * (1.0 / NEG)
        return 0

    lax.fori_loop(0, EDGES // GROUP, group, 0, unroll=UNROLL)


def against(part, ids_ref, near_ref, far_ref, prod_ref, cnt_ref, cc_ref, rows, g):
    size = near_ref.shape[0]
    dst = columns(ids_ref[2:3, rows])
    low = prod_ref[rows, :].astype(BF16)
    tails = neg = None
    for j, table in ((0, near_ref), (1, far_ref)):
        base = j * (ENT // 2) + part * size
        tail = dot(one_hot_rows(dst, size, base), table[...])
        scores = dot_nt(low, table[...])
        for i in range(size // H):
            w = cnt_ref[g, base // H + i : base // H + i + 1, :]
            cc_ref[rows, j * size + i * H : j * size + (i + 1) * H] = (
                jax.nn.sigmoid(scores[:, i * H : (i + 1) * H]) * w
            ).astype(BF16)
        drawn = dot(cc_ref[rows, j * size : (j + 1) * size], table[...])
        tails = tail if tails is None else tails + tail
        neg = drawn if neg is None else neg + drawn
    return tails, neg


def first_score_kernel(ids_ref, near_ref, far_ref, prod_ref, cnt_ref, cc_ref, tails_ref, neg_ref):
    def group(g, _):
        rows = pl.ds(pl.multiple_of(g * GROUP, GROUP), GROUP)
        tails, neg = against(0, ids_ref, near_ref, far_ref, prod_ref, cnt_ref, cc_ref, rows, g)
        tails_ref[rows, :] = tails
        neg_ref[rows, :] = neg
        return 0

    lax.fori_loop(0, EDGES // GROUP, group, 0, unroll=UNROLL)


def score_kernel(
    count_ref,
    ids_ref,
    near_ref,
    far_ref,
    head_ref,
    relrow_ref,
    prod_ref,
    cnt_ref,
    tails_ref,
    neg_ref,
    first_ref,
    src_keep_ref,
    src_send_ref,
    dst_keep_ref,
    dst_send_ref,
    gr_ref,
    cc_ref,
    plt_ref,
    pd_ref,
    gh_ref,
):
    half = ENT // 2
    quarter = half // 2
    count = count_ref[0, 0]

    def group(g, _):
        rows = pl.ds(pl.multiple_of(g * GROUP, GROUP), GROUP)
        tails, neg = against(1, ids_ref, near_ref, far_ref, prod_ref, cnt_ref, cc_ref, rows, g)
        tails = tails + tails_ref[rows, :]
        neg = neg + neg_ref[rows, :]
        prod = prod_ref[rows, :]
        edge = lax.broadcasted_iota(jnp.int32, (GROUP, 1), 0) + g * GROUP
        live = jnp.where(edge < count, 1.0, 0.0).astype(F32)
        positive = jnp.sum(prod * tails, axis=1, keepdims=True)
        pos = -live * jax.nn.sigmoid(-positive)
        grad = pos * tails + live * neg
        rel = relrow_ref[rows, :]
        head = head_ref[rows, :].astype(F32)
        gr, gi = grad[:, :H], grad[:, H:]
        for out, other in ((gh_ref, rel), (gr_ref, head)):
            a, b = other[:, :H], other[:, H:]
            out[rows, :H] = (gr * a + gi * b).astype(BF16)
            out[rows, H:] = (gi * a - gr * b).astype(BF16)
        pd_ref[rows, :] = (pos * prod).astype(BF16)
        plt_ref[:, rows] = jnp.transpose(live * prod).astype(BF16)
        return 0

    lax.fori_loop(0, EDGES // GROUP, group, 0, unroll=UNROLL)

    for part, ref in ((0, first_ref), (1, cc_ref)):
        for i in range(quarter // CHUNK):
            at = part * quarter + i * CHUNK
            rows = slice(at, at + CHUNK)
            for j, src_ref, dst_ref in (
                (0, src_keep_ref, dst_keep_ref),
                (1, src_send_ref, dst_send_ref),
            ):
                src = dot(one_hot_cols(ids_ref[4:5, :], CHUNK, j * half + at), gh_ref[...])
                src_ref[rows, :] = src.astype(src_ref.dtype)
                cols = slice(j * quarter + i * CHUNK, j * quarter + (i + 1) * CHUNK)
                drawn = jnp.transpose(dot(plt_ref[...], ref[:, cols]))
                dst = dot(one_hot_cols(ids_ref[2:3, :], CHUNK, j * half + at), pd_ref[...])
                dst_ref[rows, :] = (drawn + dst).astype(dst_ref.dtype)


def relation_kernel(ids_ref, gr_ref, keep_ref, send_ref):
    half = NREL // 2
    for i in range(half // CHUNK):
        rows = slice(i * CHUNK, (i + 1) * CHUNK)
        keep_ref[rows, :] = dot(one_hot_cols(ids_ref[3:4, :], CHUNK, i * CHUNK), gr_ref[...])
        send_ref[rows, :] = dot(
            one_hot_cols(ids_ref[3:4, :], CHUNK, half + i * CHUNK), gr_ref[...]
        ).astype(BF16)


def add_split_kernel(n_in, n_out, *refs):
    ins, outs = refs[:n_in], refs[n_in:]
    size = outs[0].shape[0]
    step = min(size, 64)
    for k, out in enumerate(outs):
        for r in range(0, size, step):
            total = ins[0][k * size + r : k * size + r + step, :].astype(F32)
            for ref in ins[1:]:
                total = total + ref[k * size + r : k * size + r + step, :].astype(F32)
            out[r : r + step, :] = total.astype(out.dtype)


def add_split(parts, n_out, own=BF16, sent=BF16):
    rows = parts[0].shape[0] // n_out
    shapes = [jax.ShapeDtypeStruct((rows, D), sent if k else own) for k in range(n_out)]
    return call(
        functools.partial(add_split_kernel, len(parts), n_out),
        shapes,
        0,
        len(parts),
        flops=len(parts) * n_out * rows * D,
        bytes_accessed=3 * len(parts) * n_out * rows * D,
    )(*parts)


def split3(x):
    hi = x.astype(BF16).astype(F32)
    mid = (x - hi).astype(BF16).astype(F32)
    return hi, mid, x - hi - mid


def sum_with_means_kernel(*refs):
    parts, out_ref = refs[:-1], refs[-1]
    rows = parts[0].shape[0]
    means = []
    for r in range(0, rows, H):
        total = parts[0][r : r + H, :].astype(F32)
        for ref in parts[1:]:
            total = total + ref[r : r + H, :].astype(F32)
        out_ref[r : r + H, :] = total.astype(BF16)
        mean = jnp.sum(total * total, axis=1, keepdims=True) * (1.0 / D)
        means.append(jnp.transpose(jnp.broadcast_to(mean, (H, H)))[0:1, :])
    means.append(jnp.zeros((8 - len(means), H), F32))
    hi, mid, lo = split3(jnp.concatenate(means, axis=0))
    top = jnp.concatenate([hi, mid], axis=1)
    bottom = jnp.concatenate([lo, jnp.zeros_like(lo)], axis=1)
    out_ref[rows : rows + 16, :] = jnp.concatenate([top, bottom], axis=0).astype(BF16)


def sum_with_means(parts):
    rows = parts[0].shape[0]
    return call(
        sum_with_means_kernel,
        jax.ShapeDtypeStruct((rows + 16, D), BF16),
        0,
        len(parts),
        flops=len(parts) * rows * D,
        bytes_accessed=3 * len(parts) * rows * D,
    )(*parts)


def means_of(piece, start, row):
    tile = piece[start : start + 16, :].astype(F32)
    return tile[row : row + 1, :H] + tile[row : row + 1, H:] + tile[8 + row : 9 + row, :H]


def update_kernel(n, place_ref, rows_ref, acc_ref, *refs):
    pieces, (new_ref, new_acc_ref, buf_ref, sem_ref) = refs[:n], refs[n:]
    size = rows_ref.shape[0] // n
    copies = []
    for k, piece in enumerate(pieces):
        i = lax.bitwise_xor(k, place_ref[0])
        for r in range(0, size, H):
            g = piece[r : r + H, :].astype(F32)
            at = pl.ds(i * (size // H) + r // H, 1)
            acc = acc_ref[at, :] + means_of(piece, size, r // H)
            new_acc_ref[at, :] = acc
            scale = jnp.transpose(jnp.broadcast_to(RATE / jnp.sqrt(acc), (H, H)))
            rows = pl.ds(pl.multiple_of(i * size + r, H), H)
            buf_ref[rows, :H] = rows_ref[rows, :H] - g[:, :H] * scale
            buf_ref[rows, H:] = rows_ref[rows, H:] - g[:, H:] * scale
        rows = pl.ds(pl.multiple_of(i * size, size), size)
        copy = pltpu.make_async_copy(buf_ref.at[rows, :], new_ref.at[rows, :], sem_ref.at[k])
        copy.start()
        copies.append(copy)
    for copy in copies:
        copy.wait()


def update(rows, acc, pieces, place):
    n = rows.shape[0]
    new, new_acc = pl.pallas_call(
        functools.partial(update_kernel, len(pieces)),
        out_shape=[
            jax.ShapeDtypeStruct((n, D), F32),
            jax.ShapeDtypeStruct((n // H, H), F32),
        ],
        in_specs=[smem()] + [vmem()] * (2 + len(pieces)),
        out_specs=[pl.BlockSpec(memory_space=pl.ANY), vmem()],
        scratch_shapes=[pltpu.VMEM((n, D), F32), pltpu.SemaphoreType.DMA((len(pieces),))],
        cost_estimate=pl.CostEstimate(flops=8 * n * D, bytes_accessed=10 * n * D, transcendentals=n),
        compiler_params=pltpu.CompilerParams(vmem_limit_bytes=VMEM_LIMIT),
    )(place, rows, acc.reshape(n // H, H), *pieces)
    return new, new_acc.reshape(n)


def sum_rows_kernel(parts_ref, out_ref):
    total = parts_ref[0].astype(F32)
    for k in range(1, parts_ref.shape[0]):
        total = total + parts_ref[k].astype(F32)
    out_ref[...] = jnp.broadcast_to(total, out_ref.shape)


def sum_rows(parts):
    return call(
        sum_rows_kernel,
        jax.ShapeDtypeStruct(parts.shape, F32),
        0,
        1,
        flops=parts.size,
        bytes_accessed=6 * parts.size,
    )(parts)


def spread(parts):
    groups = [[2 * k + hi for k in range(32)] for hi in range(2)]
    return lax.all_to_all(parts, "blk", 0, 0, axis_index_groups=groups, tiled=True)


def swap(x, mask):
    return lax.ppermute(x, AXES, [(i, i ^ mask) for i in range(256)])


def shift(x, distance, mask):
    route = [(((i // 4 - distance) % 64) * 4 + ((i % 4) ^ mask), i) for i in range(256)]
    return lax.ppermute(x, AXES, route)


CORE, XL = 1, 2
X_MASKS = (2, 4, 6)


def shards(
    entities, entity_acc, relations, relation_acc, src_ids, rel_ids, dst_ids, neg_ids, counts
):
    blk, rep = lax.axis_index("blk"), lax.axis_index("rep")
    core, xl = rep % 2, rep // 2
    x = (blk % 2) * 2 + xl

    low = entities.astype(BF16)
    quarter = lax.dynamic_slice_in_dim(entities, core * 1024 + (1 - xl) * 512, 512, 0)
    near_first = shift(quarter.astype(BF16), -1, XL)

    ids = jnp.concatenate(
        [
            src_ids,
            rel_ids,
            dst_ids ^ (core * 1024 + xl * 512),
            rel_ids ^ (core * 1024 + x * 256),
            src_ids ^ (core * 1024 + xl * 512),
            jnp.zeros((3, EDGES), jnp.int32),
        ],
        axis=0,
    )
    negs = (neg_ids ^ (core * 1024 + xl * 512)).reshape(4, NEG)
    head, rel_rows, prod, cnt = call(
        gather_kernel,
        [
            jax.ShapeDtypeStruct((EDGES, D), BF16),
            jax.ShapeDtypeStruct((EDGES, D), F32),
            jax.ShapeDtypeStruct((EDGES, D), F32),
            jax.ShapeDtypeStruct((4, ENT // H, H), F32),
        ],
        0,
        4,
        [pltpu.VMEM((NREL, D), BF16)] * 3,
        flops=4 * 2 * EDGES * ENT * D,
        bytes_accessed=1 << 22,
    )(ids, negs, low, relations)

    kept = jax.ShapeDtypeStruct((ENT // 2, D), F32)
    sent = jax.ShapeDtypeStruct((ENT // 2, D), BF16)
    slots = jax.ShapeDtypeStruct((EDGES, D), F32)
    slots_low = jax.ShapeDtypeStruct((EDGES, D), BF16)
    weights = jax.ShapeDtypeStruct((EDGES, ENT // 2), BF16)
    near_first, head = lax.optimization_barrier((near_first, head))
    near_second = swap(near_first, XL)
    far_first = swap(near_first, CORE)
    cc_first, tails, neg = call(
        first_score_kernel,
        [weights, slots, slots],
        0,
        5,
        flops=3 * EDGES * ENT * D,
        bytes_accessed=1 << 22,
    )(ids, near_first, far_first, prod, cnt)
    near_second, tails = lax.optimization_barrier((near_second, tails))
    far_second = swap(near_second, CORE)
    src_keep, src_send, dst_keep, dst_send, gr = call(
        score_kernel,
        [kept, sent, kept, sent, slots_low],
        1,
        10,
        [
            pltpu.VMEM((EDGES, ENT // 2), BF16),
            pltpu.VMEM((D, EDGES), BF16),
            pltpu.VMEM((EDGES, D), BF16),
            pltpu.VMEM((EDGES, D), BF16),
        ],
        flops=9 * EDGES * ENT * D,
        bytes_accessed=1 << 23,
    )(counts, ids, near_second, far_second, head, rel_rows, prod, cnt, tails, neg, cc_first)
    src_recv = swap(src_send, CORE)
    dst_recv = swap(dst_send, CORE)
    rel_keep, rel_send = call(
        relation_kernel,
        [kept, sent],
        0,
        2,
        flops=2 * EDGES * NREL * D,
        bytes_accessed=1 << 21,
    )(ids, gr)

    rel_recv = swap(rel_send, CORE)
    src_own, src_away = add_split([src_keep, src_recv], 2, own=F32)
    dst_away, dst_own = add_split([dst_keep, dst_recv], 2)
    parts = add_split([rel_keep, rel_recv], 4, own=F32)
    parts, src_away, dst_own, dst_away = lax.optimization_barrier(
        (parts, src_away, dst_own, dst_away)
    )
    recv = [swap(part, mask) for part, mask in zip(parts[1:], X_MASKS)]
    dst_other = swap(dst_away, XL)
    src_other = swap(src_away, XL)
    recv, dst_other = lax.optimization_barrier((recv, dst_other))
    (mine,) = add_split([parts[0], *recv], 1)

    landed = spread(mine.reshape(32, 8, D))
    (dst_sum,) = add_split([dst_own, dst_other], 1)
    dst_total = shift(dst_sum, 1, XL)
    ent_own = sum_with_means([src_own, src_other, dst_total])
    landed, ent_own = lax.optimization_barrier((landed, ent_own))
    summed = sum_rows(landed)
    total = spread(summed)
    ent_xl = swap(ent_own, XL)
    ent_core = [swap(ent_own, CORE), swap(ent_xl, CORE)]
    place = (core * 2 + xl).reshape(1)
    new_entities, new_entity_acc = update(
        entities, entity_acc, [ent_own, ent_xl, *ent_core], place
    )
    quarter = sum_with_means([total.reshape(256, D)])
    recv = [swap(quarter, mask) for mask in X_MASKS]

    pieces = [quarter, *recv]
    pieces = pieces + [swap(piece, CORE) for piece in pieces]
    pieces, new_entity_acc = lax.optimization_barrier((pieces, new_entity_acc))
    place = (core * 4 + x).reshape(1)
    new_relations, new_relation_acc = update(relations, relation_acc, pieces, place)
    return (new_entities, new_entity_acc, new_relations, new_relation_acc)


def solution(mesh):
    in_specs = (
        P("blk", None),
        P("blk"),
        P(),
        P(),
        P("blk", "rep"),
        P("blk", "rep"),
        P("blk", "rep"),
        P("blk", "rep"),
        P("blk", "rep"),
    )
    out_specs = (P("blk", None), P("blk"), P(), P())
    return jax.shard_map(shards, mesh=mesh, in_specs=in_specs, out_specs=out_specs, check_vma=False)
```

```python
import functools

import jax
import jax.numpy as jnp
from jax import lax
from jax.experimental import pallas as pl
from jax.experimental.pallas import tpu as pltpu
from jax.sharding import PartitionSpec as P

F32 = jnp.float32
BF16 = jnp.bfloat16
D = 256
H = 128
ENT = 2048
EDGES = 1024
GROUP = 256
NEG = 1024
NREL = 2048
RATE = 0.1
AXES = ("blk", "rep")
VMEM_LIMIT = 32 * 1024 * 1024
SMALL_VMEM_LIMIT = 16 * 1024 * 1024
CHUNK = 256
UNROLL = 4


def vmem():
    return pl.BlockSpec(memory_space=pltpu.VMEM)


def smem():
    return pl.BlockSpec(memory_space=pltpu.SMEM)


def call(kernel, out_shape, n_smem, n_vmem, scratch=(), flops=0, bytes_accessed=0):
    return pl.pallas_call(
        kernel,
        out_shape=out_shape,
        in_specs=[smem()] * n_smem + [vmem()] * n_vmem,
        out_specs=jax.tree.map(lambda _: vmem(), out_shape),
        scratch_shapes=list(scratch),
        cost_estimate=pl.CostEstimate(
            flops=flops, bytes_accessed=bytes_accessed, transcendentals=0
        ),
        compiler_params=pltpu.CompilerParams(vmem_limit_bytes=VMEM_LIMIT),
    )


def columns(row):
    n = row.shape[1]
    parts = [
        jnp.transpose(jnp.broadcast_to(row[:, i : i + H], (H, H))) for i in range(0, n, H)
    ]
    return parts[0] if len(parts) == 1 else jnp.concatenate(parts, axis=0)


def one_hot_rows(col, n, base=0):
    e = col.shape[0]
    lane = lax.broadcasted_iota(jnp.int32, (e, H), 1)
    parts = [jnp.where(col == lane + (base + j), 1.0, 0.0).astype(BF16) for j in range(0, n, H)]
    return jnp.concatenate(parts, axis=1)


def one_hot_cols(row, n, base):
    e = row.shape[1]
    sub = lax.broadcasted_iota(jnp.int32, (n, e), 0) + base
    return jnp.where(jnp.broadcast_to(row, (n, e)) == sub, 1.0, 0.0).astype(BF16)


def dot(a, b):
    return jnp.dot(a, b, preferred_element_type=F32)


def dot_nt(a, b):
    return lax.dot_general(a, b, (((1,), (1,)), ((), ())), preferred_element_type=F32)


def gather_kernel(ids_ref, negs_ref, low_ref, rel_ref, head_ref, relrow_ref, prod_ref, cnt_ref, hi_ref, mid_ref, lo_ref):
    for r in range(0, NREL, 256):
        x = rel_ref[r : r + 256, :]
        for ref in (hi_ref, mid_ref, lo_ref):
            part = x.astype(BF16)
            ref[r : r + 256, :] = part
            x = x - part.astype(F32)

    def group(g, _):
        rows = pl.ds(pl.multiple_of(g * GROUP, GROUP), GROUP)
        src = columns(ids_ref[0:1, rows])
        heads = dot(one_hot_rows(src, ENT), low_ref[...])
        pick = one_hot_rows(columns(ids_ref[1:2, rows]), NREL)
        rel = dot(pick, hi_ref[...]) + dot(pick, mid_ref[...]) + dot(pick, lo_ref[...])
        hr, hi, rr, ri = heads[:, :H], heads[:, H:], rel[:, :H], rel[:, H:]
        head_ref[rows, :] = heads.astype(BF16)
        relrow_ref[rows, :] = rel
        prod_ref[rows, :H] = hr * rr - hi * ri
        prod_ref[rows, H:] = hr * ri + hi * rr
        negs = negs_ref[pl.ds(g, 1), :]
        high = one_hot_cols(lax.shift_right_logical(negs, 7), ENT // H, 0)
        low = one_hot_cols(lax.bitwise_and(negs, H - 1), H, 0)
        cnt_ref[g] = dot_nt(high, low) * (1.0 / NEG)
        return 0

    lax.fori_loop(0, EDGES // GROUP, group, 0, unroll=UNROLL)


def against(part, ids_ref, near_ref, far_ref, prod_ref, cnt_ref, cc_ref, rows, g):
    size = near_ref.shape[0]
    dst = columns(ids_ref[2:3, rows])
    low = prod_ref[rows, :].astype(BF16)
    tails = neg = None
    for j, table in ((0, near_ref), (1, far_ref)):
        base = j * (ENT // 2) + part * size
        tail = dot(one_hot_rows(dst, size, base), table[...])
        scores = dot_nt(low, table[...])
        for i in range(size // H):
            w = cnt_ref[g, base // H + i : base // H + i + 1, :]
            cc_ref[rows, j * size + i * H : j * size + (i + 1) * H] = (
                jax.nn.sigmoid(scores[:, i * H : (i + 1) * H]) * w
            ).astype(BF16)
        drawn = dot(cc_ref[rows, j * size : (j + 1) * size], table[...])
        tails = tail if tails is None else tails + tail
        neg = drawn if neg is None else neg + drawn
    return tails, neg


def first_score_kernel(ids_ref, near_ref, far_ref, prod_ref, cnt_ref, cc_ref, tails_ref, neg_ref):
    def group(g, _):
        rows = pl.ds(pl.multiple_of(g * GROUP, GROUP), GROUP)
        tails, neg = against(0, ids_ref, near_ref, far_ref, prod_ref, cnt_ref, cc_ref, rows, g)
        tails_ref[rows, :] = tails
        neg_ref[rows, :] = neg
        return 0

    lax.fori_loop(0, EDGES // GROUP, group, 0, unroll=UNROLL)


def score_kernel(
    count_ref,
    ids_ref,
    near_ref,
    far_ref,
    head_ref,
    relrow_ref,
    prod_ref,
    cnt_ref,
    tails_ref,
    neg_ref,
    first_ref,
    src_keep_ref,
    src_send_ref,
    dst_keep_ref,
    dst_send_ref,
    gr_ref,
    cc_ref,
    plt_ref,
    pd_ref,
    gh_ref,
):
    half = ENT // 2
    quarter = half // 2
    count = count_ref[0, 0]

    def group(g, _):
        rows = pl.ds(pl.multiple_of(g * GROUP, GROUP), GROUP)
        tails, neg = against(1, ids_ref, near_ref, far_ref, prod_ref, cnt_ref, cc_ref, rows, g)
        tails = tails + tails_ref[rows, :]
        neg = neg + neg_ref[rows, :]
        prod = prod_ref[rows, :]
        edge = lax.broadcasted_iota(jnp.int32, (GROUP, 1), 0) + g * GROUP
        live = jnp.where(edge < count, 1.0, 0.0).astype(F32)
        positive = jnp.sum(prod * tails, axis=1, keepdims=True)
        pos = -live * jax.nn.sigmoid(-positive)
        grad = pos * tails + live * neg
        rel = relrow_ref[rows, :]
        head = head_ref[rows, :].astype(F32)
        gr, gi = grad[:, :H], grad[:, H:]
        for out, other in ((gh_ref, rel), (gr_ref, head)):
            a, b = other[:, :H], other[:, H:]
            out[rows, :H] = (gr * a + gi * b).astype(BF16)
            out[rows, H:] = (gi * a - gr * b).astype(BF16)
        pd_ref[rows, :] = (pos * prod).astype(BF16)
        plt_ref[:, rows] = jnp.transpose(live * prod).astype(BF16)
        return 0

    lax.fori_loop(0, EDGES // GROUP, group, 0, unroll=UNROLL)

    for part, ref in ((0, first_ref), (1, cc_ref)):
        for i in range(quarter // CHUNK):
            at = part * quarter + i * CHUNK
            rows = slice(at, at + CHUNK)
            for j, src_ref, dst_ref in (
                (0, src_keep_ref, dst_keep_ref),
                (1, src_send_ref, dst_send_ref),
            ):
                src = dot(one_hot_cols(ids_ref[4:5, :], CHUNK, j * half + at), gh_ref[...])
                src_ref[rows, :] = src.astype(src_ref.dtype)
                cols = slice(j * quarter + i * CHUNK, j * quarter + (i + 1) * CHUNK)
                drawn = jnp.transpose(dot(plt_ref[...], ref[:, cols]))
                dst = dot(one_hot_cols(ids_ref[2:3, :], CHUNK, j * half + at), pd_ref[...])
                dst_ref[rows, :] = (drawn + dst).astype(dst_ref.dtype)


def relation_kernel(ids_ref, gr_ref, keep_ref, send_ref):
    half = NREL // 2
    for i in range(half // CHUNK):
        rows = slice(i * CHUNK, (i + 1) * CHUNK)
        keep_ref[rows, :] = dot(one_hot_cols(ids_ref[3:4, :], CHUNK, i * CHUNK), gr_ref[...])
        send_ref[rows, :] = dot(
            one_hot_cols(ids_ref[3:4, :], CHUNK, half + i * CHUNK), gr_ref[...]
        ).astype(BF16)


def add_split_kernel(n_in, n_out, *refs):
    ins, outs = refs[:n_in], refs[n_in:]
    size = outs[0].shape[0]
    step = min(size, 64)
    for k, out in enumerate(outs):
        for r in range(0, size, step):
            total = ins[0][k * size + r : k * size + r + step, :].astype(F32)
            for ref in ins[1:]:
                total = total + ref[k * size + r : k * size + r + step, :].astype(F32)
            out[r : r + step, :] = total.astype(out.dtype)


def add_split(parts, n_out, own=BF16, sent=BF16):
    rows = parts[0].shape[0] // n_out
    shapes = [jax.ShapeDtypeStruct((rows, D), sent if k else own) for k in range(n_out)]
    return call(
        functools.partial(add_split_kernel, len(parts), n_out),
        shapes,
        0,
        len(parts),
        flops=len(parts) * n_out * rows * D,
        bytes_accessed=3 * len(parts) * n_out * rows * D,
    )(*parts)


def split3(x):
    hi = x.astype(BF16).astype(F32)
    mid = (x - hi).astype(BF16).astype(F32)
    return hi, mid, x - hi - mid


def sum_with_means_kernel(*refs):
    parts, out_ref = refs[:-1], refs[-1]
    rows = parts[0].shape[0]
    means = []
    for r in range(0, rows, H):
        total = parts[0][r : r + H, :].astype(F32)
        for ref in parts[1:]:
            total = total + ref[r : r + H, :].astype(F32)
        out_ref[r : r + H, :] = total.astype(BF16)
        mean = jnp.sum(total * total, axis=1, keepdims=True) * (1.0 / D)
        means.append(jnp.transpose(jnp.broadcast_to(mean, (H, H)))[0:1, :])
    means.append(jnp.zeros((8 - len(means), H), F32))
    hi, mid, lo = split3(jnp.concatenate(means, axis=0))
    top = jnp.concatenate([hi, mid], axis=1)
    bottom = jnp.concatenate([lo, jnp.zeros_like(lo)], axis=1)
    out_ref[rows : rows + 16, :] = jnp.concatenate([top, bottom], axis=0).astype(BF16)


def sum_with_means(parts):
    rows = parts[0].shape[0]
    return call(
        sum_with_means_kernel,
        jax.ShapeDtypeStruct((rows + 16, D), BF16),
        0,
        len(parts),
        flops=len(parts) * rows * D,
        bytes_accessed=3 * len(parts) * rows * D,
    )(*parts)


def means_of(piece, start, row):
    tile = piece[start : start + 16, :].astype(F32)
    return tile[row : row + 1, :H] + tile[row : row + 1, H:] + tile[8 + row : 9 + row, :H]


def update_kernel(n, place_ref, rows_ref, acc_ref, *refs):
    pieces, (new_ref, new_acc_ref, in_ref, buf_ref, in_sem, out_sem) = refs[:n], refs[n:]
    size = in_ref.shape[0] // n
    starts = [lax.bitwise_xor(k, place_ref[0]) * size for k in range(n)]
    fetches, copies = [], []
    for k, start in enumerate(starts):
        rows = pl.ds(pl.multiple_of(start, size), size)
        fetch = pltpu.make_async_copy(rows_ref.at[rows, :], in_ref.at[rows, :], in_sem.at[k])
        fetch.start()
        fetches.append(fetch)
    for k, (start, piece) in enumerate(zip(starts, pieces)):
        fetches[k].wait()
        for r in range(0, size, H):
            g = piece[r : r + H, :].astype(F32)
            at = pl.ds(start // H + r // H, 1)
            acc = acc_ref[at, :] + means_of(piece, size, r // H)
            new_acc_ref[at, :] = acc
            scale = jnp.transpose(jnp.broadcast_to(RATE / jnp.sqrt(acc), (H, H)))
            rows = pl.ds(pl.multiple_of(start + r, H), H)
            buf_ref[rows, :H] = in_ref[rows, :H] - g[:, :H] * scale
            buf_ref[rows, H:] = in_ref[rows, H:] - g[:, H:] * scale
        rows = pl.ds(pl.multiple_of(start, size), size)
        copy = pltpu.make_async_copy(buf_ref.at[rows, :], new_ref.at[rows, :], out_sem.at[k])
        copy.start()
        copies.append(copy)
    for copy in copies:
        copy.wait()


def update(rows, acc, pieces, place):
    n = rows.shape[0]
    k = len(pieces)
    new, new_acc = pl.pallas_call(
        functools.partial(update_kernel, k),
        out_shape=[
            jax.ShapeDtypeStruct((n, D), F32),
            jax.ShapeDtypeStruct((n // H, H), F32),
        ],
        in_specs=[smem(), pl.BlockSpec(memory_space=pl.ANY)] + [vmem()] * (1 + k),
        out_specs=[pl.BlockSpec(memory_space=pl.ANY), vmem()],
        scratch_shapes=[
            pltpu.VMEM((n, D), F32),
            pltpu.VMEM((n, D), F32),
            pltpu.SemaphoreType.DMA((k,)),
            pltpu.SemaphoreType.DMA((k,)),
        ],
        cost_estimate=pl.CostEstimate(flops=8 * n * D, bytes_accessed=10 * n * D, transcendentals=n),
        compiler_params=pltpu.CompilerParams(vmem_limit_bytes=SMALL_VMEM_LIMIT),
    )(place, rows, acc.reshape(n // H, H), *pieces)
    return new, new_acc.reshape(n)


def sum_rows_kernel(parts_ref, out_ref):
    total = parts_ref[0].astype(F32)
    for k in range(1, parts_ref.shape[0]):
        total = total + parts_ref[k].astype(F32)
    out_ref[...] = jnp.broadcast_to(total, out_ref.shape)


def sum_rows(parts):
    return call(
        sum_rows_kernel,
        jax.ShapeDtypeStruct(parts.shape, F32),
        0,
        1,
        flops=parts.size,
        bytes_accessed=6 * parts.size,
    )(parts)


def spread(parts):
    groups = [[2 * k + hi for k in range(32)] for hi in range(2)]
    return lax.all_to_all(parts, "blk", 0, 0, axis_index_groups=groups, tiled=True)


def swap(x, mask):
    return lax.ppermute(x, AXES, [(i, i ^ mask) for i in range(256)])


def shift(x, distance, mask):
    route = [(((i // 4 - distance) % 64) * 4 + ((i % 4) ^ mask), i) for i in range(256)]
    return lax.ppermute(x, AXES, route)


CORE, XL = 1, 2
X_MASKS = (2, 4, 6)


def shards(
    entities, entity_acc, relations, relation_acc, src_ids, rel_ids, dst_ids, neg_ids, counts
):
    blk, rep = lax.axis_index("blk"), lax.axis_index("rep")
    core, xl = rep % 2, rep // 2
    x = (blk % 2) * 2 + xl

    low = entities.astype(BF16)
    quarter = lax.dynamic_slice_in_dim(entities, core * 1024 + (1 - xl) * 512, 512, 0)
    near_first = shift(quarter.astype(BF16), -1, XL)

    ids = jnp.concatenate(
        [
            src_ids,
            rel_ids,
            dst_ids ^ (core * 1024 + xl * 512),
            rel_ids ^ (core * 1024 + x * 256),
            src_ids ^ (core * 1024 + xl * 512),
            jnp.zeros((3, EDGES), jnp.int32),
        ],
        axis=0,
    )
    negs = (neg_ids ^ (core * 1024 + xl * 512)).reshape(4, NEG)
    head, rel_rows, prod, cnt = call(
        gather_kernel,
        [
            jax.ShapeDtypeStruct((EDGES, D), BF16),
            jax.ShapeDtypeStruct((EDGES, D), F32),
            jax.ShapeDtypeStruct((EDGES, D), F32),
            jax.ShapeDtypeStruct((4, ENT // H, H), F32),
        ],
        0,
        4,
        [pltpu.VMEM((NREL, D), BF16)] * 3,
        flops=4 * 2 * EDGES * ENT * D,
        bytes_accessed=1 << 22,
    )(ids, negs, low, relations)

    kept = jax.ShapeDtypeStruct((ENT // 2, D), F32)
    sent = jax.ShapeDtypeStruct((ENT // 2, D), BF16)
    slots = jax.ShapeDtypeStruct((EDGES, D), F32)
    slots_low = jax.ShapeDtypeStruct((EDGES, D), BF16)
    weights = jax.ShapeDtypeStruct((EDGES, ENT // 2), BF16)
    near_first, head = lax.optimization_barrier((near_first, head))
    near_second = swap(near_first, XL)
    far_first = swap(near_first, CORE)
    cc_first, tails, neg = call(
        first_score_kernel,
        [weights, slots, slots],
        0,
        5,
        flops=3 * EDGES * ENT * D,
        bytes_accessed=1 << 22,
    )(ids, near_first, far_first, prod, cnt)
    near_second, tails = lax.optimization_barrier((near_second, tails))
    far_second = swap(near_second, CORE)
    src_keep, src_send, dst_keep, dst_send, gr = call(
        score_kernel,
        [kept, sent, kept, sent, slots_low],
        1,
        10,
        [
            pltpu.VMEM((EDGES, ENT // 2), BF16),
            pltpu.VMEM((D, EDGES), BF16),
            pltpu.VMEM((EDGES, D), BF16),
            pltpu.VMEM((EDGES, D), BF16),
        ],
        flops=9 * EDGES * ENT * D,
        bytes_accessed=1 << 23,
    )(counts, ids, near_second, far_second, head, rel_rows, prod, cnt, tails, neg, cc_first)
    src_recv = swap(src_send, CORE)
    dst_recv = swap(dst_send, CORE)
    rel_keep, rel_send = call(
        relation_kernel,
        [kept, sent],
        0,
        2,
        flops=2 * EDGES * NREL * D,
        bytes_accessed=1 << 21,
    )(ids, gr)

    rel_recv = swap(rel_send, CORE)
    src_own, src_away = add_split([src_keep, src_recv], 2, own=F32)
    dst_away, dst_own = add_split([dst_keep, dst_recv], 2)
    parts = add_split([rel_keep, rel_recv], 4, own=F32)
    recv = [swap(part, mask) for part, mask in zip(parts[1:], X_MASKS)]
    recv, dst_away, src_away = lax.optimization_barrier((recv, dst_away, src_away))
    dst_other = swap(dst_away, XL)
    src_other = swap(src_away, XL)
    (mine,) = add_split([parts[0], *recv], 1)

    landed = spread(mine.reshape(32, 8, D))
    (dst_sum,) = add_split([dst_own, dst_other], 1)
    dst_total = shift(dst_sum, 1, XL)
    ent_own = sum_with_means([src_own, src_other, dst_total])
    landed, _, src_other = lax.optimization_barrier((landed, dst_sum, src_other))
    summed = sum_rows(landed)
    ent_xl = swap(ent_own, XL)
    total, ent_xl = lax.optimization_barrier((spread(summed), ent_xl))
    ent_core = [swap(ent_own, CORE), swap(ent_xl, CORE)]
    place = (core * 2 + xl).reshape(1)
    new_entities, new_entity_acc = update(
        entities, entity_acc, [ent_own, ent_xl, *ent_core], place
    )
    quarter = sum_with_means([total.reshape(256, D)])
    recv = [swap(quarter, mask) for mask in X_MASKS]

    pieces = [quarter, *recv]
    pieces = pieces + [swap(piece, CORE) for piece in pieces]
    pieces, new_entity_acc = lax.optimization_barrier((pieces, new_entity_acc))
    place = (core * 4 + x).reshape(1)
    new_relations, new_relation_acc = update(relations, relation_acc, pieces, place)
    return (new_entities, new_entity_acc, new_relations, new_relation_acc)


def solution(mesh):
    in_specs = (
        P("blk", None),
        P("blk"),
        P(),
        P(),
        P("blk", "rep"),
        P("blk", "rep"),
        P("blk", "rep"),
        P("blk", "rep"),
        P("blk", "rep"),
    )
    out_specs = (P("blk", None), P("blk"), P(), P())
    return jax.shard_map(shards, mesh=mesh, in_specs=in_specs, out_specs=out_specs, check_vma=False)
```

```python
import functools

import jax
import jax.numpy as jnp
from jax import lax
from jax.experimental import pallas as pl
from jax.experimental.pallas import tpu as pltpu
from jax.sharding import PartitionSpec as P

F32 = jnp.float32
BF16 = jnp.bfloat16
D = 256
H = 128
ENT = 2048
EDGES = 1024
GROUP = 256
NEG = 1024
NREL = 2048
RATE = 0.1
AXES = ("blk", "rep")
VMEM_LIMIT = 32 * 1024 * 1024
SMALL_VMEM_LIMIT = 16 * 1024 * 1024
CHUNK = 256
UNROLL = 4


def vmem():
    return pl.BlockSpec(memory_space=pltpu.VMEM)


def smem():
    return pl.BlockSpec(memory_space=pltpu.SMEM)


def call(kernel, out_shape, n_smem, n_vmem, scratch=(), flops=0, bytes_accessed=0):
    return pl.pallas_call(
        kernel,
        out_shape=out_shape,
        in_specs=[smem()] * n_smem + [vmem()] * n_vmem,
        out_specs=jax.tree.map(lambda _: vmem(), out_shape),
        scratch_shapes=list(scratch),
        cost_estimate=pl.CostEstimate(
            flops=flops, bytes_accessed=bytes_accessed, transcendentals=0
        ),
        compiler_params=pltpu.CompilerParams(vmem_limit_bytes=VMEM_LIMIT),
    )


def columns(row):
    n = row.shape[1]
    parts = [
        jnp.transpose(jnp.broadcast_to(row[:, i : i + H], (H, H))) for i in range(0, n, H)
    ]
    return parts[0] if len(parts) == 1 else jnp.concatenate(parts, axis=0)


def one_hot_rows(col, n, base=0):
    e = col.shape[0]
    lane = lax.broadcasted_iota(jnp.int32, (e, H), 1)
    parts = [jnp.where(col == lane + (base + j), 1.0, 0.0).astype(BF16) for j in range(0, n, H)]
    return jnp.concatenate(parts, axis=1)


def one_hot_cols(row, n, base):
    e = row.shape[1]
    sub = lax.broadcasted_iota(jnp.int32, (n, e), 0) + base
    return jnp.where(jnp.broadcast_to(row, (n, e)) == sub, 1.0, 0.0).astype(BF16)


def dot(a, b):
    return jnp.dot(a, b, preferred_element_type=F32)


def dot_nt(a, b):
    return lax.dot_general(a, b, (((1,), (1,)), ((), ())), preferred_element_type=F32)


def gather_kernel(ids_ref, negs_ref, low_ref, rel_ref, head_ref, relrow_ref, prod_ref, cnt_ref, hi_ref, mid_ref, lo_ref):
    for r in range(0, NREL, 256):
        x = rel_ref[r : r + 256, :]
        for ref in (hi_ref, mid_ref, lo_ref):
            part = x.astype(BF16)
            ref[r : r + 256, :] = part
            x = x - part.astype(F32)

    def group(g, _):
        rows = pl.ds(pl.multiple_of(g * GROUP, GROUP), GROUP)
        src = columns(ids_ref[0:1, rows])
        heads = dot(one_hot_rows(src, ENT), low_ref[...])
        pick = one_hot_rows(columns(ids_ref[1:2, rows]), NREL)
        rel = dot(pick, hi_ref[...]) + dot(pick, mid_ref[...]) + dot(pick, lo_ref[...])
        hr, hi, rr, ri = heads[:, :H], heads[:, H:], rel[:, :H], rel[:, H:]
        head_ref[rows, :] = heads.astype(BF16)
        relrow_ref[rows, :] = rel
        prod_ref[rows, :H] = hr * rr - hi * ri
        prod_ref[rows, H:] = hr * ri + hi * rr
        negs = negs_ref[pl.ds(g, 1), :]
        high = one_hot_cols(lax.shift_right_logical(negs, 7), ENT // H, 0)
        low = one_hot_cols(lax.bitwise_and(negs, H - 1), H, 0)
        cnt_ref[g] = dot_nt(high, low) * (1.0 / NEG)
        return 0

    lax.fori_loop(0, EDGES // GROUP, group, 0, unroll=UNROLL)


def against(part, ids_ref, near_ref, far_ref, prod_ref, cnt_ref, cc_ref, rows, g):
    size = near_ref.shape[0]
    dst = columns(ids_ref[2:3, rows])
    low = prod_ref[rows, :].astype(BF16)
    tails = neg = None
    for j, table in ((0, near_ref), (1, far_ref)):
        base = j * (ENT // 2) + part * size
        tail = dot(one_hot_rows(dst, size, base), table[...])
        scores = dot_nt(low, table[...])
        for i in range(size // H):
            w = cnt_ref[g, base // H + i : base // H + i + 1, :]
            cc_ref[rows, j * size + i * H : j * size + (i + 1) * H] = (
                jax.nn.sigmoid(scores[:, i * H : (i + 1) * H]) * w
            ).astype(BF16)
        drawn = dot(cc_ref[rows, j * size : (j + 1) * size], table[...])
        tails = tail if tails is None else tails + tail
        neg = drawn if neg is None else neg + drawn
    return tails, neg


def first_score_kernel(ids_ref, near_ref, far_ref, prod_ref, cnt_ref, cc_ref, tails_ref, neg_ref):
    def group(g, _):
        rows = pl.ds(pl.multiple_of(g * GROUP, GROUP), GROUP)
        tails, neg = against(0, ids_ref, near_ref, far_ref, prod_ref, cnt_ref, cc_ref, rows, g)
        tails_ref[rows, :] = tails
        neg_ref[rows, :] = neg
        return 0

    lax.fori_loop(0, EDGES // GROUP, group, 0, unroll=UNROLL)


def score_kernel(
    count_ref,
    ids_ref,
    near_ref,
    far_ref,
    head_ref,
    relrow_ref,
    prod_ref,
    cnt_ref,
    tails_ref,
    neg_ref,
    first_ref,
    src_keep_ref,
    src_send_ref,
    dst_keep_ref,
    dst_send_ref,
    gr_ref,
    cc_ref,
    plt_ref,
    pd_ref,
    gh_ref,
):
    half = ENT // 2
    quarter = half // 2
    count = count_ref[0, 0]

    def group(g, _):
        rows = pl.ds(pl.multiple_of(g * GROUP, GROUP), GROUP)
        tails, neg = against(1, ids_ref, near_ref, far_ref, prod_ref, cnt_ref, cc_ref, rows, g)
        tails = tails + tails_ref[rows, :]
        neg = neg + neg_ref[rows, :]
        prod = prod_ref[rows, :]
        edge = lax.broadcasted_iota(jnp.int32, (GROUP, 1), 0) + g * GROUP
        live = jnp.where(edge < count, 1.0, 0.0).astype(F32)
        positive = jnp.sum(prod * tails, axis=1, keepdims=True)
        pos = -live * jax.nn.sigmoid(-positive)
        grad = pos * tails + live * neg
        rel = relrow_ref[rows, :]
        head = head_ref[rows, :].astype(F32)
        gr, gi = grad[:, :H], grad[:, H:]
        for out, other in ((gh_ref, rel), (gr_ref, head)):
            a, b = other[:, :H], other[:, H:]
            out[rows, :H] = (gr * a + gi * b).astype(BF16)
            out[rows, H:] = (gi * a - gr * b).astype(BF16)
        pd_ref[rows, :] = (pos * prod).astype(BF16)
        plt_ref[:, rows] = jnp.transpose(live * prod).astype(BF16)
        return 0

    lax.fori_loop(0, EDGES // GROUP, group, 0, unroll=UNROLL)

    for part, ref in ((0, first_ref), (1, cc_ref)):
        for i in range(quarter // CHUNK):
            at = part * quarter + i * CHUNK
            rows = slice(at, at + CHUNK)
            for j, src_ref, dst_ref in (
                (0, src_keep_ref, dst_keep_ref),
                (1, src_send_ref, dst_send_ref),
            ):
                src = dot(one_hot_cols(ids_ref[4:5, :], CHUNK, j * half + at), gh_ref[...])
                src_ref[rows, :] = src.astype(src_ref.dtype)
                cols = slice(j * quarter + i * CHUNK, j * quarter + (i + 1) * CHUNK)
                drawn = jnp.transpose(dot(plt_ref[...], ref[:, cols]))
                dst = dot(one_hot_cols(ids_ref[2:3, :], CHUNK, j * half + at), pd_ref[...])
                dst_ref[rows, :] = (drawn + dst).astype(dst_ref.dtype)


def relation_kernel(ids_ref, gr_ref, keep_ref, send_ref):
    half = NREL // 2
    for i in range(half // CHUNK):
        rows = slice(i * CHUNK, (i + 1) * CHUNK)
        keep_ref[rows, :] = dot(one_hot_cols(ids_ref[3:4, :], CHUNK, i * CHUNK), gr_ref[...])
        send_ref[rows, :] = dot(
            one_hot_cols(ids_ref[3:4, :], CHUNK, half + i * CHUNK), gr_ref[...]
        ).astype(BF16)


def add_split_kernel(n_in, n_out, *refs):
    ins, outs = refs[:n_in], refs[n_in:]
    size = outs[0].shape[0]
    step = min(size, 64)
    for k, out in enumerate(outs):
        for r in range(0, size, step):
            total = ins[0][k * size + r : k * size + r + step, :].astype(F32)
            for ref in ins[1:]:
                total = total + ref[k * size + r : k * size + r + step, :].astype(F32)
            out[r : r + step, :] = total.astype(out.dtype)


def add_split(parts, n_out, own=BF16, sent=BF16):
    rows = parts[0].shape[0] // n_out
    shapes = [jax.ShapeDtypeStruct((rows, D), sent if k else own) for k in range(n_out)]
    return call(
        functools.partial(add_split_kernel, len(parts), n_out),
        shapes,
        0,
        len(parts),
        flops=len(parts) * n_out * rows * D,
        bytes_accessed=3 * len(parts) * n_out * rows * D,
    )(*parts)


def split3(x):
    hi = x.astype(BF16).astype(F32)
    mid = (x - hi).astype(BF16).astype(F32)
    return hi, mid, x - hi - mid


def sum_with_means_kernel(*refs):
    parts, out_ref = refs[:-1], refs[-1]
    rows = parts[0].shape[0]
    means = []
    for r in range(0, rows, H):
        total = parts[0][r : r + H, :].astype(F32)
        for ref in parts[1:]:
            total = total + ref[r : r + H, :].astype(F32)
        out_ref[r : r + H, :] = total.astype(BF16)
        mean = jnp.sum(total * total, axis=1, keepdims=True) * (1.0 / D)
        means.append(jnp.transpose(jnp.broadcast_to(mean, (H, H)))[0:1, :])
    means.append(jnp.zeros((8 - len(means), H), F32))
    hi, mid, lo = split3(jnp.concatenate(means, axis=0))
    top = jnp.concatenate([hi, mid], axis=1)
    bottom = jnp.concatenate([lo, jnp.zeros_like(lo)], axis=1)
    out_ref[rows : rows + 16, :] = jnp.concatenate([top, bottom], axis=0).astype(BF16)


def sum_with_means(parts):
    rows = parts[0].shape[0]
    return call(
        sum_with_means_kernel,
        jax.ShapeDtypeStruct((rows + 16, D), BF16),
        0,
        len(parts),
        flops=len(parts) * rows * D,
        bytes_accessed=3 * len(parts) * rows * D,
    )(*parts)


def means_of(piece, start, row):
    tile = piece[start : start + 16, :].astype(F32)
    return tile[row : row + 1, :H] + tile[row : row + 1, H:] + tile[8 + row : 9 + row, :H]


def update_kernel(n, place_ref, rows_ref, acc_ref, *refs):
    pieces, (new_ref, new_acc_ref, buf_ref, sem_ref) = refs[:n], refs[n:]
    size = rows_ref.shape[0] // n
    copies = []
    for k, piece in enumerate(pieces):
        i = lax.bitwise_xor(k, place_ref[0])
        for r in range(0, size, H):
            g = piece[r : r + H, :].astype(F32)
            at = pl.ds(i * (size // H) + r // H, 1)
            acc = acc_ref[at, :] + means_of(piece, size, r // H)
            new_acc_ref[at, :] = acc
            scale = jnp.transpose(jnp.broadcast_to(RATE / jnp.sqrt(acc), (H, H)))
            rows = pl.ds(pl.multiple_of(i * size + r, H), H)
            buf_ref[rows, :H] = rows_ref[rows, :H] - g[:, :H] * scale
            buf_ref[rows, H:] = rows_ref[rows, H:] - g[:, H:] * scale
        rows = pl.ds(pl.multiple_of(i * size, size), size)
        copy = pltpu.make_async_copy(buf_ref.at[rows, :], new_ref.at[rows, :], sem_ref.at[k])
        copy.start()
        copies.append(copy)
    for copy in copies:
        copy.wait()


def update(rows, acc, pieces, place):
    n = rows.shape[0]
    new, new_acc = pl.pallas_call(
        functools.partial(update_kernel, len(pieces)),
        out_shape=[
            jax.ShapeDtypeStruct((n, D), F32),
            jax.ShapeDtypeStruct((n // H, H), F32),
        ],
        in_specs=[smem()] + [vmem()] * (2 + len(pieces)),
        out_specs=[pl.BlockSpec(memory_space=pl.ANY), vmem()],
        scratch_shapes=[pltpu.VMEM((n, D), F32), pltpu.SemaphoreType.DMA((len(pieces),))],
        cost_estimate=pl.CostEstimate(flops=8 * n * D, bytes_accessed=10 * n * D, transcendentals=n),
        compiler_params=pltpu.CompilerParams(vmem_limit_bytes=SMALL_VMEM_LIMIT),
    )(place, rows, acc.reshape(n // H, H), *pieces)
    return new, new_acc.reshape(n)


def sum_rows_kernel(parts_ref, out_ref):
    total = parts_ref[0].astype(F32)
    for k in range(1, parts_ref.shape[0]):
        total = total + parts_ref[k].astype(F32)
    out_ref[...] = jnp.broadcast_to(total, out_ref.shape)


def sum_rows(parts):
    return call(
        sum_rows_kernel,
        jax.ShapeDtypeStruct(parts.shape, F32),
        0,
        1,
        flops=parts.size,
        bytes_accessed=6 * parts.size,
    )(parts)


def spread(parts):
    groups = [[2 * k + hi for k in range(32)] for hi in range(2)]
    return lax.all_to_all(parts, "blk", 0, 0, axis_index_groups=groups, tiled=True)


def swap(x, mask):
    return lax.ppermute(x, AXES, [(i, i ^ mask) for i in range(256)])


def shift(x, distance, mask):
    route = [(((i // 4 - distance) % 64) * 4 + ((i % 4) ^ mask), i) for i in range(256)]
    return lax.ppermute(x, AXES, route)


CORE, XL = 1, 2
X_MASKS = (2, 4, 6)


def shards(
    entities, entity_acc, relations, relation_acc, src_ids, rel_ids, dst_ids, neg_ids, counts
):
    blk, rep = lax.axis_index("blk"), lax.axis_index("rep")
    core, xl = rep % 2, rep // 2
    x = (blk % 2) * 2 + xl

    low = entities.astype(BF16)
    quarter = lax.dynamic_slice_in_dim(entities, core * 1024 + (1 - xl) * 512, 512, 0)
    near_first = shift(quarter.astype(BF16), -1, XL)

    ids = jnp.concatenate(
        [
            src_ids,
            rel_ids,
            dst_ids ^ (core * 1024 + xl * 512),
            rel_ids ^ (core * 1024 + x * 256),
            src_ids ^ (core * 1024 + xl * 512),
            jnp.zeros((3, EDGES), jnp.int32),
        ],
        axis=0,
    )
    negs = (neg_ids ^ (core * 1024 + xl * 512)).reshape(4, NEG)
    head, rel_rows, prod, cnt = call(
        gather_kernel,
        [
            jax.ShapeDtypeStruct((EDGES, D), BF16),
            jax.ShapeDtypeStruct((EDGES, D), F32),
            jax.ShapeDtypeStruct((EDGES, D), F32),
            jax.ShapeDtypeStruct((4, ENT // H, H), F32),
        ],
        0,
        4,
        [pltpu.VMEM((NREL, D), BF16)] * 3,
        flops=4 * 2 * EDGES * ENT * D,
        bytes_accessed=1 << 22,
    )(ids, negs, low, relations)

    kept = jax.ShapeDtypeStruct((ENT // 2, D), F32)
    sent = jax.ShapeDtypeStruct((ENT // 2, D), BF16)
    slots = jax.ShapeDtypeStruct((EDGES, D), F32)
    slots_low = jax.ShapeDtypeStruct((EDGES, D), BF16)
    weights = jax.ShapeDtypeStruct((EDGES, ENT // 2), BF16)
    near_first, head = lax.optimization_barrier((near_first, head))
    near_second = swap(near_first, XL)
    far_first = swap(near_first, CORE)
    cc_first, tails, neg = call(
        first_score_kernel,
        [weights, slots, slots],
        0,
        5,
        flops=3 * EDGES * ENT * D,
        bytes_accessed=1 << 22,
    )(ids, near_first, far_first, prod, cnt)
    near_second, tails = lax.optimization_barrier((near_second, tails))
    far_second = swap(near_second, CORE)
    src_keep, src_send, dst_keep, dst_send, gr = call(
        score_kernel,
        [kept, sent, kept, sent, slots_low],
        1,
        10,
        [
            pltpu.VMEM((EDGES, ENT // 2), BF16),
            pltpu.VMEM((D, EDGES), BF16),
            pltpu.VMEM((EDGES, D), BF16),
            pltpu.VMEM((EDGES, D), BF16),
        ],
        flops=9 * EDGES * ENT * D,
        bytes_accessed=1 << 23,
    )(counts, ids, near_second, far_second, head, rel_rows, prod, cnt, tails, neg, cc_first)
    src_recv = swap(src_send, CORE)
    dst_recv = swap(dst_send, CORE)
    rel_keep, rel_send = call(
        relation_kernel,
        [kept, sent],
        0,
        2,
        flops=2 * EDGES * NREL * D,
        bytes_accessed=1 << 21,
    )(ids, gr)

    rel_recv = swap(rel_send, CORE)
    src_own, src_away = add_split([src_keep, src_recv], 2, own=F32)
    dst_away, dst_own = add_split([dst_keep, dst_recv], 2)
    parts = add_split([rel_keep, rel_recv], 4, own=F32)
    recv = [swap(part, mask) for part, mask in zip(parts[1:], X_MASKS)]
    recv, dst_away, src_away = lax.optimization_barrier((recv, dst_away, src_away))
    dst_other = swap(dst_away, XL)
    src_other = swap(src_away, XL)
    (mine,) = add_split([parts[0], *recv], 1)

    landed = spread(mine.reshape(32, 8, D))
    (dst_sum,) = add_split([dst_own, dst_other], 1)
    dst_total = shift(dst_sum, 1, XL)
    ent_own = sum_with_means([src_own, src_other, dst_total])
    landed, _, src_other = lax.optimization_barrier((landed, dst_sum, src_other))
    summed = sum_rows(landed)
    ent_xl = swap(ent_own, XL)
    total, ent_xl = lax.optimization_barrier((spread(summed), ent_xl))
    ent_core = [swap(ent_own, CORE), swap(ent_xl, CORE)]
    place = (core * 2 + xl).reshape(1)
    new_entities, new_entity_acc = update(
        entities, entity_acc, [ent_own, ent_xl, *ent_core], place
    )
    quarter = sum_with_means([total.reshape(256, D)])
    recv = [swap(quarter, mask) for mask in X_MASKS]
    recv, new_entity_acc = lax.optimization_barrier((recv, new_entity_acc))
    pieces = [quarter, *recv]
    pieces = pieces + [swap(piece, CORE) for piece in pieces]
    pieces, new_entity_acc = lax.optimization_barrier((pieces, new_entity_acc))
    place = (core * 4 + x).reshape(1)
    new_relations, new_relation_acc = update(relations, relation_acc, pieces, place)
    return (new_entities, new_entity_acc, new_relations, new_relation_acc)


def solution(mesh):
    in_specs = (
        P("blk", None),
        P("blk"),
        P(),
        P(),
        P("blk", "rep"),
        P("blk", "rep"),
        P("blk", "rep"),
        P("blk", "rep"),
        P("blk", "rep"),
    )
    out_specs = (P("blk", None), P("blk"), P(), P())
    return jax.shard_map(shards, mesh=mesh, in_specs=in_specs, out_specs=out_specs, check_vma=False)
```

```python
import functools

import jax
import jax.numpy as jnp
from jax import lax
from jax.experimental import pallas as pl
from jax.experimental.pallas import tpu as pltpu
from jax.sharding import PartitionSpec as P

F32 = jnp.float32
BF16 = jnp.bfloat16
D = 256
H = 128
ENT = 2048
EDGES = 1024
GROUP = 256
NEG = 1024
NREL = 2048
RATE = 0.1
AXES = ("blk", "rep")
VMEM_LIMIT = 32 * 1024 * 1024
UPDATE_VMEM_LIMIT = 52 * 1024 * 1024
LARGE_VMEM_LIMIT = 62 * 1024 * 1024
CHUNK = 256
UNROLL = 4


def vmem():
    return pl.BlockSpec(memory_space=pltpu.VMEM)


def smem():
    return pl.BlockSpec(memory_space=pltpu.SMEM)


def call(kernel, out_shape, n_smem, n_vmem, scratch=(), flops=0, bytes_accessed=0):
    return pl.pallas_call(
        kernel,
        out_shape=out_shape,
        in_specs=[smem()] * n_smem + [vmem()] * n_vmem,
        out_specs=jax.tree.map(lambda _: vmem(), out_shape),
        scratch_shapes=list(scratch),
        cost_estimate=pl.CostEstimate(
            flops=flops, bytes_accessed=bytes_accessed, transcendentals=0
        ),
        compiler_params=pltpu.CompilerParams(vmem_limit_bytes=VMEM_LIMIT),
    )


def columns(row):
    n = row.shape[1]
    parts = [
        jnp.transpose(jnp.broadcast_to(row[:, i : i + H], (H, H))) for i in range(0, n, H)
    ]
    return parts[0] if len(parts) == 1 else jnp.concatenate(parts, axis=0)


def one_hot_rows(col, n, base=0):
    e = col.shape[0]
    lane = lax.broadcasted_iota(jnp.int32, (e, H), 1)
    parts = [jnp.where(col == lane + (base + j), 1.0, 0.0).astype(BF16) for j in range(0, n, H)]
    return jnp.concatenate(parts, axis=1)


def one_hot_cols(row, n, base):
    e = row.shape[1]
    sub = lax.broadcasted_iota(jnp.int32, (n, e), 0) + base
    return jnp.where(jnp.broadcast_to(row, (n, e)) == sub, 1.0, 0.0).astype(BF16)


def dot(a, b):
    return jnp.dot(a, b, preferred_element_type=F32)


def dot_nt(a, b):
    return lax.dot_general(a, b, (((1,), (1,)), ((), ())), preferred_element_type=F32)


def gather_kernel(ids_ref, negs_ref, low_ref, rel_ref, head_ref, relrow_ref, prod_ref, cnt_ref, hi_ref, mid_ref, lo_ref):
    for r in range(0, NREL, 256):
        x = rel_ref[r : r + 256, :]
        for ref in (hi_ref, mid_ref, lo_ref):
            part = x.astype(BF16)
            ref[r : r + 256, :] = part
            x = x - part.astype(F32)

    def group(g, _):
        rows = pl.ds(pl.multiple_of(g * GROUP, GROUP), GROUP)
        src = columns(ids_ref[0:1, rows])
        heads = dot(one_hot_rows(src, ENT), low_ref[...])
        pick = one_hot_rows(columns(ids_ref[1:2, rows]), NREL)
        rel = dot(pick, hi_ref[...]) + dot(pick, mid_ref[...]) + dot(pick, lo_ref[...])
        hr, hi, rr, ri = heads[:, :H], heads[:, H:], rel[:, :H], rel[:, H:]
        head_ref[rows, :] = heads.astype(BF16)
        relrow_ref[rows, :] = rel
        prod_ref[rows, :H] = hr * rr - hi * ri
        prod_ref[rows, H:] = hr * ri + hi * rr
        negs = negs_ref[pl.ds(g, 1), :]
        high = one_hot_cols(lax.shift_right_logical(negs, 7), ENT // H, 0)
        low = one_hot_cols(lax.bitwise_and(negs, H - 1), H, 0)
        cnt_ref[g] = dot_nt(high, low) * (1.0 / NEG)
        return 0

    lax.fori_loop(0, EDGES // GROUP, group, 0, unroll=UNROLL)


def against(part, ids_ref, near_ref, far_ref, prod_ref, cnt_ref, cc_ref, rows, g):
    size = near_ref.shape[0]
    dst = columns(ids_ref[2:3, rows])
    low = prod_ref[rows, :].astype(BF16)
    tails = neg = None
    for j, table in ((0, near_ref), (1, far_ref)):
        base = j * (ENT // 2) + part * size
        tail = dot(one_hot_rows(dst, size, base), table[...])
        scores = dot_nt(low, table[...])
        for i in range(size // H):
            w = cnt_ref[g, base // H + i : base // H + i + 1, :]
            cc_ref[rows, j * size + i * H : j * size + (i + 1) * H] = (
                jax.nn.sigmoid(scores[:, i * H : (i + 1) * H]) * w
            ).astype(BF16)
        drawn = dot(cc_ref[rows, j * size : (j + 1) * size], table[...])
        tails = tail if tails is None else tails + tail
        neg = drawn if neg is None else neg + drawn
    return tails, neg


def first_score_kernel(ids_ref, near_ref, far_ref, prod_ref, cnt_ref, cc_ref, tails_ref, neg_ref):
    def group(g, _):
        rows = pl.ds(pl.multiple_of(g * GROUP, GROUP), GROUP)
        tails, neg = against(0, ids_ref, near_ref, far_ref, prod_ref, cnt_ref, cc_ref, rows, g)
        tails_ref[rows, :] = tails
        neg_ref[rows, :] = neg
        return 0

    lax.fori_loop(0, EDGES // GROUP, group, 0, unroll=UNROLL)


def score_kernel(
    count_ref,
    ids_ref,
    near_ref,
    far_ref,
    head_ref,
    relrow_ref,
    prod_ref,
    cnt_ref,
    tails_ref,
    neg_ref,
    first_ref,
    src_keep_ref,
    src_send_ref,
    dst_keep_ref,
    dst_send_ref,
    gr_ref,
    cc_ref,
    plt_ref,
    pd_ref,
    gh_ref,
):
    half = ENT // 2
    quarter = half // 2
    count = count_ref[0, 0]

    def group(g, _):
        rows = pl.ds(pl.multiple_of(g * GROUP, GROUP), GROUP)
        tails, neg = against(1, ids_ref, near_ref, far_ref, prod_ref, cnt_ref, cc_ref, rows, g)
        tails = tails + tails_ref[rows, :]
        neg = neg + neg_ref[rows, :]
        prod = prod_ref[rows, :]
        edge = lax.broadcasted_iota(jnp.int32, (GROUP, 1), 0) + g * GROUP
        live = jnp.where(edge < count, 1.0, 0.0).astype(F32)
        positive = jnp.sum(prod * tails, axis=1, keepdims=True)
        pos = -live * jax.nn.sigmoid(-positive)
        grad = pos * tails + live * neg
        rel = relrow_ref[rows, :]
        head = head_ref[rows, :].astype(F32)
        gr, gi = grad[:, :H], grad[:, H:]
        for out, other in ((gh_ref, rel), (gr_ref, head)):
            a, b = other[:, :H], other[:, H:]
            out[rows, :H] = (gr * a + gi * b).astype(BF16)
            out[rows, H:] = (gi * a - gr * b).astype(BF16)
        pd_ref[rows, :] = (pos * prod).astype(BF16)
        plt_ref[:, rows] = jnp.transpose(live * prod).astype(BF16)
        return 0

    lax.fori_loop(0, EDGES // GROUP, group, 0, unroll=UNROLL)

    for part, ref in ((0, first_ref), (1, cc_ref)):
        for i in range(quarter // CHUNK):
            at = part * quarter + i * CHUNK
            rows = slice(at, at + CHUNK)
            for j, src_ref, dst_ref in (
                (0, src_keep_ref, dst_keep_ref),
                (1, src_send_ref, dst_send_ref),
            ):
                src = dot(one_hot_cols(ids_ref[4:5, :], CHUNK, j * half + at), gh_ref[...])
                src_ref[rows, :] = src.astype(src_ref.dtype)
                cols = slice(j * quarter + i * CHUNK, j * quarter + (i + 1) * CHUNK)
                drawn = jnp.transpose(dot(plt_ref[...], ref[:, cols]))
                dst = dot(one_hot_cols(ids_ref[2:3, :], CHUNK, j * half + at), pd_ref[...])
                dst_ref[rows, :] = (drawn + dst).astype(dst_ref.dtype)


def relation_kernel(ids_ref, gr_ref, keep_ref, send_ref):
    half = NREL // 2
    for i in range(half // CHUNK):
        rows = slice(i * CHUNK, (i + 1) * CHUNK)
        keep_ref[rows, :] = dot(one_hot_cols(ids_ref[3:4, :], CHUNK, i * CHUNK), gr_ref[...])
        send_ref[rows, :] = dot(
            one_hot_cols(ids_ref[3:4, :], CHUNK, half + i * CHUNK), gr_ref[...]
        ).astype(BF16)


def add_split_kernel(n_in, n_out, *refs):
    ins, outs = refs[:n_in], refs[n_in:]
    size = outs[0].shape[0]
    step = min(size, 64)
    for k, out in enumerate(outs):
        for r in range(0, size, step):
            total = ins[0][k * size + r : k * size + r + step, :].astype(F32)
            for ref in ins[1:]:
                total = total + ref[k * size + r : k * size + r + step, :].astype(F32)
            out[r : r + step, :] = total.astype(out.dtype)


def add_split(parts, n_out, own=BF16, sent=BF16):
    rows = parts[0].shape[0] // n_out
    shapes = [jax.ShapeDtypeStruct((rows, D), sent if k else own) for k in range(n_out)]
    return call(
        functools.partial(add_split_kernel, len(parts), n_out),
        shapes,
        0,
        len(parts),
        flops=len(parts) * n_out * rows * D,
        bytes_accessed=3 * len(parts) * n_out * rows * D,
    )(*parts)


def split3(x):
    hi = x.astype(BF16).astype(F32)
    mid = (x - hi).astype(BF16).astype(F32)
    return hi, mid, x - hi - mid


def sum_with_means_kernel(*refs):
    parts, out_ref = refs[:-1], refs[-1]
    rows = parts[0].shape[0]
    means = []
    for r in range(0, rows, H):
        total = parts[0][r : r + H, :].astype(F32)
        for ref in parts[1:]:
            total = total + ref[r : r + H, :].astype(F32)
        out_ref[r : r + H, :] = total.astype(BF16)
        mean = jnp.sum(total * total, axis=1, keepdims=True) * (1.0 / D)
        means.append(jnp.transpose(jnp.broadcast_to(mean, (H, H)))[0:1, :])
    means.append(jnp.zeros((8 - len(means), H), F32))
    hi, mid, lo = split3(jnp.concatenate(means, axis=0))
    top = jnp.concatenate([hi, mid], axis=1)
    bottom = jnp.concatenate([lo, jnp.zeros_like(lo)], axis=1)
    out_ref[rows : rows + 16, :] = jnp.concatenate([top, bottom], axis=0).astype(BF16)


def sum_with_means(parts):
    rows = parts[0].shape[0]
    return call(
        sum_with_means_kernel,
        jax.ShapeDtypeStruct((rows + 16, D), BF16),
        0,
        len(parts),
        flops=len(parts) * rows * D,
        bytes_accessed=3 * len(parts) * rows * D,
    )(*parts)


def means_of(piece, start, row):
    tile = piece[start : start + 16, :].astype(F32)
    return tile[row : row + 1, :H] + tile[row : row + 1, H:] + tile[8 + row : 9 + row, :H]


def update_kernel(n, total, first, place_ref, rows_ref, acc_ref, *refs):
    if first:
        _, old_acc_ref, *refs = refs
    pieces, (new_ref, new_acc_ref, in_ref, buf_ref, in_sem, out_sem) = refs[:n], refs[n:]
    size = in_ref.shape[0] // n
    starts = [lax.bitwise_xor(first + k, place_ref[0]) * size for k in range(n)]
    spans = [pl.ds(pl.multiple_of(start, size), size) for start in starts]
    fetches = [
        pltpu.make_async_copy(
            rows_ref.at[span, :], in_ref.at[pl.ds(k * size, size), :], in_sem.at[k]
        )
        for k, span in enumerate(spans)
    ]
    for fetch in fetches:
        fetch.start()
    if first:
        new_acc_ref[...] = old_acc_ref[...]
    copies = []
    for k, (start, piece) in enumerate(zip(starts, pieces)):
        fetches[k].wait()
        for r in range(0, size, H):
            g = piece[r : r + H, :].astype(F32)
            at = pl.ds(start // H + r // H, 1)
            acc = acc_ref[at, :] + means_of(piece, size, r // H)
            new_acc_ref[at, :] = acc
            scale = jnp.transpose(jnp.broadcast_to(RATE / jnp.sqrt(acc), (H, H)))
            rows = slice(k * size + r, k * size + r + H)
            buf_ref[rows, :H] = in_ref[rows, :H] - g[:, :H] * scale
            buf_ref[rows, H:] = in_ref[rows, H:] - g[:, H:] * scale
        copy = pltpu.make_async_copy(
            buf_ref.at[pl.ds(k * size, size), :], new_ref.at[spans[k], :], out_sem.at[k]
        )
        copy.start()
        copies.append(copy)
    for copy in copies:
        copy.wait()


def update(rows, acc, pieces, place, total=None, old=()):
    n = rows.shape[0]
    k = len(pieces)
    total = total or k
    first = total - k if old else 0
    size = n // total
    any_space = pl.BlockSpec(memory_space=pl.ANY)
    return pl.pallas_call(
        functools.partial(update_kernel, k, total, first),
        out_shape=[
            jax.ShapeDtypeStruct((n, D), F32),
            jax.ShapeDtypeStruct((n // H, H), F32),
        ],
        in_specs=[smem(), pl.BlockSpec(memory_space=pltpu.HBM), vmem()]
        + ([any_space, vmem()] if old else [])
        + [vmem()] * k,
        out_specs=[any_space, vmem()],
        scratch_shapes=[
            pltpu.VMEM((k * size, D), F32),
            pltpu.VMEM((k * size, D), F32),
            pltpu.SemaphoreType.DMA((k,)),
            pltpu.SemaphoreType.DMA((k,)),
        ],
        input_output_aliases={3: 0} if old else {},
        cost_estimate=pl.CostEstimate(flops=8 * n * D, bytes_accessed=10 * n * D, transcendentals=n),
        compiler_params=pltpu.CompilerParams(vmem_limit_bytes=UPDATE_VMEM_LIMIT),
    )(place, rows, acc.reshape(n // H, H), *old, *pieces)


def low_quarter_kernel(place_ref, rows_ref, out_ref, in_ref, sem_ref):
    size = out_ref.shape[0]
    step = size // 4
    fetches = []
    for k in range(4):
        start = pl.multiple_of(place_ref[0] * size + k * step, step)
        fetch = pltpu.make_async_copy(
            rows_ref.at[pl.ds(start, step), :],
            in_ref.at[pl.ds(k * step, step), :],
            sem_ref.at[k],
        )
        fetch.start()
        fetches.append(fetch)
    for k, fetch in enumerate(fetches):
        fetch.wait()
        out_ref[k * step : (k + 1) * step, :] = in_ref[k * step : (k + 1) * step, :].astype(BF16)


def low_quarter(rows, place):
    size = rows.shape[0] // 4
    return pl.pallas_call(
        low_quarter_kernel,
        out_shape=jax.ShapeDtypeStruct((size, D), BF16),
        in_specs=[smem(), pl.BlockSpec(memory_space=pl.ANY)],
        out_specs=vmem(),
        scratch_shapes=[pltpu.VMEM((size, D), F32), pltpu.SemaphoreType.DMA((4,))],
        compiler_params=pltpu.CompilerParams(vmem_limit_bytes=LARGE_VMEM_LIMIT),
    )(place, rows)


def sum_rows_kernel(parts_ref, out_ref):
    total = parts_ref[0].astype(F32)
    for k in range(1, parts_ref.shape[0]):
        total = total + parts_ref[k].astype(F32)
    out_ref[...] = jnp.broadcast_to(total, out_ref.shape)


def sum_rows(parts):
    return call(
        sum_rows_kernel,
        jax.ShapeDtypeStruct(parts.shape, F32),
        0,
        1,
        flops=parts.size,
        bytes_accessed=6 * parts.size,
    )(parts)


def spread(parts):
    groups = [[2 * k + hi for k in range(32)] for hi in range(2)]
    return lax.all_to_all(parts, "blk", 0, 0, axis_index_groups=groups, tiled=True)


def swap(x, mask):
    return lax.ppermute(x, AXES, [(i, i ^ mask) for i in range(256)])


def shift(x, distance, mask):
    route = [(((i // 4 - distance) % 64) * 4 + ((i % 4) ^ mask), i) for i in range(256)]
    return lax.ppermute(x, AXES, route)


CORE, XL = 1, 2
X_MASKS = (2, 4, 6)


def shards(
    entities, entity_acc, relations, relation_acc, src_ids, rel_ids, dst_ids, neg_ids, counts
):
    blk, rep = lax.axis_index("blk"), lax.axis_index("rep")
    core, xl = rep % 2, rep // 2
    x = (blk % 2) * 2 + xl

    low = entities.astype(BF16)
    quarter = low_quarter(entities, (core * 2 + 1 - xl).reshape(1))
    near_first = shift(quarter, -1, XL)

    ids = jnp.concatenate(
        [
            src_ids,
            rel_ids,
            dst_ids ^ (core * 1024 + xl * 512),
            rel_ids ^ (core * 1024 + x * 256),
            src_ids ^ (core * 1024 + xl * 512),
            jnp.zeros((3, EDGES), jnp.int32),
        ],
        axis=0,
    )
    negs = (neg_ids ^ (core * 1024 + xl * 512)).reshape(4, NEG)
    head, rel_rows, prod, cnt = call(
        gather_kernel,
        [
            jax.ShapeDtypeStruct((EDGES, D), BF16),
            jax.ShapeDtypeStruct((EDGES, D), F32),
            jax.ShapeDtypeStruct((EDGES, D), F32),
            jax.ShapeDtypeStruct((4, ENT // H, H), F32),
        ],
        0,
        4,
        [pltpu.VMEM((NREL, D), BF16)] * 3,
        flops=4 * 2 * EDGES * ENT * D,
        bytes_accessed=1 << 22,
    )(ids, negs, low, relations)

    kept = jax.ShapeDtypeStruct((ENT // 2, D), F32)
    sent = jax.ShapeDtypeStruct((ENT // 2, D), BF16)
    slots = jax.ShapeDtypeStruct((EDGES, D), F32)
    slots_low = jax.ShapeDtypeStruct((EDGES, D), BF16)
    weights = jax.ShapeDtypeStruct((EDGES, ENT // 2), BF16)
    near_first, head = lax.optimization_barrier((near_first, head))
    near_second = swap(near_first, XL)
    far_first = swap(near_first, CORE)
    cc_first, tails, neg = call(
        first_score_kernel,
        [weights, slots, slots],
        0,
        5,
        flops=3 * EDGES * ENT * D,
        bytes_accessed=1 << 22,
    )(ids, near_first, far_first, prod, cnt)
    near_second, tails = lax.optimization_barrier((near_second, tails))
    far_second = swap(near_second, CORE)
    src_keep, src_send, dst_keep, dst_send, gr = call(
        score_kernel,
        [kept, sent, kept, sent, slots_low],
        1,
        10,
        [
            pltpu.VMEM((EDGES, ENT // 2), BF16),
            pltpu.VMEM((D, EDGES), BF16),
            pltpu.VMEM((EDGES, D), BF16),
            pltpu.VMEM((EDGES, D), BF16),
        ],
        flops=9 * EDGES * ENT * D,
        bytes_accessed=1 << 23,
    )(counts, ids, near_second, far_second, head, rel_rows, prod, cnt, tails, neg, cc_first)
    src_recv = swap(src_send, CORE)
    dst_recv = swap(dst_send, CORE)
    rel_keep, rel_send = call(
        relation_kernel,
        [kept, sent],
        0,
        2,
        flops=2 * EDGES * NREL * D,
        bytes_accessed=1 << 21,
    )(ids, gr)

    rel_recv = swap(rel_send, CORE)
    src_own, src_away = add_split([src_keep, src_recv], 2, own=F32)
    dst_away, dst_own = add_split([dst_keep, dst_recv], 2)
    parts = add_split([rel_keep, rel_recv], 4, own=F32)
    recv = [swap(part, mask) for part, mask in zip(parts[1:], X_MASKS)]
    recv, dst_away, src_away = lax.optimization_barrier((recv, dst_away, src_away))
    dst_other = swap(dst_away, XL)
    src_other = swap(src_away, XL)
    (mine,) = add_split([parts[0], *recv], 1)

    landed = spread(mine.reshape(32, 8, D))
    (dst_sum,) = add_split([dst_own, dst_other], 1)
    dst_total = shift(dst_sum, 1, XL)
    ent_own = sum_with_means([src_own, src_other, dst_total])
    landed, _, src_other = lax.optimization_barrier((landed, dst_sum, src_other))
    summed = sum_rows(landed)
    ent_xl = swap(ent_own, XL)
    total, ent_xl = lax.optimization_barrier((spread(summed), ent_xl))
    ent_core = [swap(ent_own, CORE), swap(ent_xl, CORE)]
    place = (core * 2 + xl).reshape(1)
    new_entities, new_entity_acc = update(
        entities, entity_acc, [ent_own, ent_xl, *ent_core], place
    )
    quarter = sum_with_means([total.reshape(256, D)])
    recv = [swap(quarter, mask) for mask in X_MASKS]
    recv, new_entity_acc = lax.optimization_barrier((recv, new_entity_acc))
    near_pieces = [quarter, *recv]
    far_pieces = [swap(piece, CORE) for piece in near_pieces]
    place = (core * 4 + x).reshape(1)
    half = update(relations, relation_acc, near_pieces, place, total=8)
    new_relations, new_relation_acc = update(
        relations, relation_acc, far_pieces, place, total=8, old=half
    )
    return (
        new_entities,
        new_entity_acc.reshape(ENT),
        new_relations,
        new_relation_acc.reshape(NREL),
    )


def solution(mesh):
    in_specs = (
        P("blk", None),
        P("blk"),
        P(),
        P(),
        P("blk", "rep"),
        P("blk", "rep"),
        P("blk", "rep"),
        P("blk", "rep"),
        P("blk", "rep"),
    )
    out_specs = (P("blk", None), P("blk"), P(), P())
    return jax.shard_map(shards, mesh=mesh, in_specs=in_specs, out_specs=out_specs, check_vma=False)
```

```python
import functools

import jax
import jax.numpy as jnp
from jax import lax
from jax.experimental import pallas as pl
from jax.experimental.pallas import tpu as pltpu
from jax.sharding import PartitionSpec as P

F32 = jnp.float32
BF16 = jnp.bfloat16
D = 256
H = 128
ENT = 2048
EDGES = 1024
GROUP = 256
NEG = 1024
NREL = 2048
RATE = 0.1
AXES = ("blk", "rep")
VMEM_LIMIT = 32 * 1024 * 1024
SMALL_VMEM_LIMIT = 16 * 1024 * 1024
CHUNK = 256
UNROLL = 4


def vmem():
    return pl.BlockSpec(memory_space=pltpu.VMEM)


def smem():
    return pl.BlockSpec(memory_space=pltpu.SMEM)


def call(kernel, out_shape, n_smem, n_vmem, scratch=(), flops=0, bytes_accessed=0):
    return pl.pallas_call(
        kernel,
        out_shape=out_shape,
        in_specs=[smem()] * n_smem + [vmem()] * n_vmem,
        out_specs=jax.tree.map(lambda _: vmem(), out_shape),
        scratch_shapes=list(scratch),
        cost_estimate=pl.CostEstimate(
            flops=flops, bytes_accessed=bytes_accessed, transcendentals=0
        ),
        compiler_params=pltpu.CompilerParams(vmem_limit_bytes=VMEM_LIMIT),
    )


def columns(row):
    n = row.shape[1]
    parts = [
        jnp.transpose(jnp.broadcast_to(row[:, i : i + H], (H, H))) for i in range(0, n, H)
    ]
    return parts[0] if len(parts) == 1 else jnp.concatenate(parts, axis=0)


def one_hot_rows(col, n, base=0):
    e = col.shape[0]
    lane = lax.broadcasted_iota(jnp.int32, (e, H), 1)
    parts = [jnp.where(col == lane + (base + j), 1.0, 0.0).astype(BF16) for j in range(0, n, H)]
    return jnp.concatenate(parts, axis=1)


def one_hot_cols(row, n, base):
    e = row.shape[1]
    sub = lax.broadcasted_iota(jnp.int32, (n, e), 0) + base
    return jnp.where(jnp.broadcast_to(row, (n, e)) == sub, 1.0, 0.0).astype(BF16)


def dot(a, b):
    return jnp.dot(a, b, preferred_element_type=F32)


def dot_nt(a, b):
    return lax.dot_general(a, b, (((1,), (1,)), ((), ())), preferred_element_type=F32)


def gather_kernel(ids_ref, negs_ref, low_ref, rel_ref, head_ref, relrow_ref, prod_ref, cnt_ref, hi_ref, mid_ref, lo_ref):
    for r in range(0, NREL, 256):
        x = rel_ref[r : r + 256, :]
        for ref in (hi_ref, mid_ref, lo_ref):
            part = x.astype(BF16)
            ref[r : r + 256, :] = part
            x = x - part.astype(F32)

    def group(g, _):
        rows = pl.ds(pl.multiple_of(g * GROUP, GROUP), GROUP)
        src = columns(ids_ref[0:1, rows])
        heads = dot(one_hot_rows(src, ENT), low_ref[...])
        pick = one_hot_rows(columns(ids_ref[1:2, rows]), NREL)
        rel = dot(pick, hi_ref[...]) + dot(pick, mid_ref[...]) + dot(pick, lo_ref[...])
        hr, hi, rr, ri = heads[:, :H], heads[:, H:], rel[:, :H], rel[:, H:]
        head_ref[rows, :] = heads.astype(BF16)
        relrow_ref[rows, :] = rel
        prod_ref[rows, :H] = hr * rr - hi * ri
        prod_ref[rows, H:] = hr * ri + hi * rr
        negs = negs_ref[pl.ds(g, 1), :]
        high = one_hot_cols(lax.shift_right_logical(negs, 7), ENT // H, 0)
        low = one_hot_cols(lax.bitwise_and(negs, H - 1), H, 0)
        cnt_ref[g] = dot_nt(high, low) * (1.0 / NEG)
        return 0

    lax.fori_loop(0, EDGES // GROUP, group, 0, unroll=UNROLL)


def against(part, ids_ref, near_ref, far_ref, prod_ref, cnt_ref, cc_ref, rows, g):
    size = near_ref.shape[0]
    dst = columns(ids_ref[2:3, rows])
    low = prod_ref[rows, :].astype(BF16)
    tails = neg = None
    for j, table in ((0, near_ref), (1, far_ref)):
        base = j * (ENT // 2) + part * size
        tail = dot(one_hot_rows(dst, size, base), table[...])
        scores = dot_nt(low, table[...])
        for i in range(size // H):
            w = cnt_ref[g, base // H + i : base // H + i + 1, :]
            cc_ref[rows, j * size + i * H : j * size + (i + 1) * H] = (
                jax.nn.sigmoid(scores[:, i * H : (i + 1) * H]) * w
            ).astype(BF16)
        drawn = dot(cc_ref[rows, j * size : (j + 1) * size], table[...])
        tails = tail if tails is None else tails + tail
        neg = drawn if neg is None else neg + drawn
    return tails, neg


def first_score_kernel(ids_ref, near_ref, far_ref, prod_ref, cnt_ref, cc_ref, tails_ref, neg_ref):
    def group(g, _):
        rows = pl.ds(pl.multiple_of(g * GROUP, GROUP), GROUP)
        tails, neg = against(0, ids_ref, near_ref, far_ref, prod_ref, cnt_ref, cc_ref, rows, g)
        tails_ref[rows, :] = tails
        neg_ref[rows, :] = neg
        return 0

    lax.fori_loop(0, EDGES // GROUP, group, 0, unroll=UNROLL)


def score_kernel(
    count_ref,
    ids_ref,
    near_ref,
    far_ref,
    head_ref,
    relrow_ref,
    prod_ref,
    cnt_ref,
    tails_ref,
    neg_ref,
    first_ref,
    src_keep_ref,
    src_send_ref,
    dst_keep_ref,
    dst_send_ref,
    gr_ref,
    cc_ref,
    plt_ref,
    pd_ref,
    gh_ref,
):
    half = ENT // 2
    quarter = half // 2
    count = count_ref[0, 0]

    def group(g, _):
        rows = pl.ds(pl.multiple_of(g * GROUP, GROUP), GROUP)
        tails, neg = against(1, ids_ref, near_ref, far_ref, prod_ref, cnt_ref, cc_ref, rows, g)
        tails = tails + tails_ref[rows, :]
        neg = neg + neg_ref[rows, :]
        prod = prod_ref[rows, :]
        edge = lax.broadcasted_iota(jnp.int32, (GROUP, 1), 0) + g * GROUP
        live = jnp.where(edge < count, 1.0, 0.0).astype(F32)
        positive = jnp.sum(prod * tails, axis=1, keepdims=True)
        pos = -live * jax.nn.sigmoid(-positive)
        grad = pos * tails + live * neg
        rel = relrow_ref[rows, :]
        head = head_ref[rows, :].astype(F32)
        gr, gi = grad[:, :H], grad[:, H:]
        for out, other in ((gh_ref, rel), (gr_ref, head)):
            a, b = other[:, :H], other[:, H:]
            out[rows, :H] = (gr * a + gi * b).astype(BF16)
            out[rows, H:] = (gi * a - gr * b).astype(BF16)
        pd_ref[rows, :] = (pos * prod).astype(BF16)
        plt_ref[:, rows] = jnp.transpose(live * prod).astype(BF16)
        return 0

    lax.fori_loop(0, EDGES // GROUP, group, 0, unroll=UNROLL)

    for part, ref in ((0, first_ref), (1, cc_ref)):
        for i in range(quarter // CHUNK):
            at = part * quarter + i * CHUNK
            rows = slice(at, at + CHUNK)
            for j, src_ref, dst_ref in (
                (0, src_keep_ref, dst_keep_ref),
                (1, src_send_ref, dst_send_ref),
            ):
                src = dot(one_hot_cols(ids_ref[4:5, :], CHUNK, j * half + at), gh_ref[...])
                src_ref[rows, :] = src.astype(src_ref.dtype)
                cols = slice(j * quarter + i * CHUNK, j * quarter + (i + 1) * CHUNK)
                drawn = jnp.transpose(dot(plt_ref[...], ref[:, cols]))
                dst = dot(one_hot_cols(ids_ref[2:3, :], CHUNK, j * half + at), pd_ref[...])
                dst_ref[rows, :] = (drawn + dst).astype(dst_ref.dtype)


def relation_kernel(ids_ref, gr_ref, keep_ref, send_ref):
    half = NREL // 2
    for i in range(half // CHUNK):
        rows = slice(i * CHUNK, (i + 1) * CHUNK)
        keep_ref[rows, :] = dot(one_hot_cols(ids_ref[3:4, :], CHUNK, i * CHUNK), gr_ref[...])
        send_ref[rows, :] = dot(
            one_hot_cols(ids_ref[3:4, :], CHUNK, half + i * CHUNK), gr_ref[...]
        ).astype(BF16)


def add_split_kernel(n_in, n_out, *refs):
    ins, outs = refs[:n_in], refs[n_in:]
    size = outs[0].shape[0]
    step = min(size, 64)
    for k, out in enumerate(outs):
        for r in range(0, size, step):
            total = ins[0][k * size + r : k * size + r + step, :].astype(F32)
            for ref in ins[1:]:
                total = total + ref[k * size + r : k * size + r + step, :].astype(F32)
            out[r : r + step, :] = total.astype(out.dtype)


def add_split(parts, n_out, own=BF16, sent=BF16):
    rows = parts[0].shape[0] // n_out
    shapes = [jax.ShapeDtypeStruct((rows, D), sent if k else own) for k in range(n_out)]
    return call(
        functools.partial(add_split_kernel, len(parts), n_out),
        shapes,
        0,
        len(parts),
        flops=len(parts) * n_out * rows * D,
        bytes_accessed=3 * len(parts) * n_out * rows * D,
    )(*parts)


def split3(x):
    hi = x.astype(BF16).astype(F32)
    mid = (x - hi).astype(BF16).astype(F32)
    return hi, mid, x - hi - mid


def sum_with_means_kernel(*refs):
    parts, out_ref = refs[:-1], refs[-1]
    rows = parts[0].shape[0]
    means = []
    for r in range(0, rows, H):
        total = parts[0][r : r + H, :].astype(F32)
        for ref in parts[1:]:
            total = total + ref[r : r + H, :].astype(F32)
        out_ref[r : r + H, :] = total.astype(BF16)
        mean = jnp.sum(total * total, axis=1, keepdims=True) * (1.0 / D)
        means.append(jnp.transpose(jnp.broadcast_to(mean, (H, H)))[0:1, :])
    means.append(jnp.zeros((8 - len(means), H), F32))
    hi, mid, lo = split3(jnp.concatenate(means, axis=0))
    top = jnp.concatenate([hi, mid], axis=1)
    bottom = jnp.concatenate([lo, jnp.zeros_like(lo)], axis=1)
    out_ref[rows : rows + 16, :] = jnp.concatenate([top, bottom], axis=0).astype(BF16)


def sum_with_means(parts):
    rows = parts[0].shape[0]
    return call(
        sum_with_means_kernel,
        jax.ShapeDtypeStruct((rows + 16, D), BF16),
        0,
        len(parts),
        flops=len(parts) * rows * D,
        bytes_accessed=3 * len(parts) * rows * D,
    )(*parts)


def means_of(piece, start, row):
    tile = piece[start : start + 16, :].astype(F32)
    return tile[row : row + 1, :H] + tile[row : row + 1, H:] + tile[8 + row : 9 + row, :H]


def update_kernel(n, place_ref, rows_ref, acc_ref, *refs):
    pieces, (new_ref, new_acc_ref, buf_ref, sem_ref) = refs[:n], refs[n:]
    size = rows_ref.shape[0] // n
    copies = []
    for k, piece in enumerate(pieces):
        i = lax.bitwise_xor(k, place_ref[0])
        for r in range(0, size, H):
            g = piece[r : r + H, :].astype(F32)
            at = pl.ds(i * (size // H) + r // H, 1)
            acc = acc_ref[at, :] + means_of(piece, size, r // H)
            new_acc_ref[at, :] = acc
            scale = jnp.transpose(jnp.broadcast_to(RATE / jnp.sqrt(acc), (H, H)))
            rows = pl.ds(pl.multiple_of(i * size + r, H), H)
            buf_ref[rows, :H] = rows_ref[rows, :H] - g[:, :H] * scale
            buf_ref[rows, H:] = rows_ref[rows, H:] - g[:, H:] * scale
        rows = pl.ds(pl.multiple_of(i * size, size), size)
        copy = pltpu.make_async_copy(buf_ref.at[rows, :], new_ref.at[rows, :], sem_ref.at[k])
        copy.start()
        copies.append(copy)
    for copy in copies:
        copy.wait()


def update(rows, acc, pieces, place):
    n = rows.shape[0]
    new, new_acc = pl.pallas_call(
        functools.partial(update_kernel, len(pieces)),
        out_shape=[
            jax.ShapeDtypeStruct((n, D), F32),
            jax.ShapeDtypeStruct((n // H, H), F32),
        ],
        in_specs=[smem()] + [vmem()] * (2 + len(pieces)),
        out_specs=[pl.BlockSpec(memory_space=pl.ANY), vmem()],
        scratch_shapes=[pltpu.VMEM((n, D), F32), pltpu.SemaphoreType.DMA((len(pieces),))],
        cost_estimate=pl.CostEstimate(flops=8 * n * D, bytes_accessed=10 * n * D, transcendentals=n),
        compiler_params=pltpu.CompilerParams(vmem_limit_bytes=SMALL_VMEM_LIMIT),
    )(place, rows, acc.reshape(n // H, H), *pieces)
    return new, new_acc.reshape(n)


def sum_rows_kernel(parts_ref, out_ref):
    total = parts_ref[0].astype(F32)
    for k in range(1, parts_ref.shape[0]):
        total = total + parts_ref[k].astype(F32)
    out_ref[...] = jnp.broadcast_to(total, out_ref.shape)


def sum_rows(parts):
    return call(
        sum_rows_kernel,
        jax.ShapeDtypeStruct(parts.shape, F32),
        0,
        1,
        flops=parts.size,
        bytes_accessed=6 * parts.size,
    )(parts)


def spread(parts):
    groups = [[2 * k + hi for k in range(32)] for hi in range(2)]
    return lax.all_to_all(parts, "blk", 0, 0, axis_index_groups=groups, tiled=True)


def swap(x, mask):
    return lax.ppermute(x, AXES, [(i, i ^ mask) for i in range(256)])


def shift(x, distance, mask):
    route = [(((i // 4 - distance) % 64) * 4 + ((i % 4) ^ mask), i) for i in range(256)]
    return lax.ppermute(x, AXES, route)


CORE, XL = 1, 2
X_MASKS = (2, 4, 6)


def shards(
    entities, entity_acc, relations, relation_acc, src_ids, rel_ids, dst_ids, neg_ids, counts
):
    blk, rep = lax.axis_index("blk"), lax.axis_index("rep")
    core, xl = rep % 2, rep // 2
    x = (blk % 2) * 2 + xl

    low = entities.astype(BF16)
    quarter = lax.dynamic_slice_in_dim(entities, core * 1024 + (1 - xl) * 512, 512, 0)
    near_first = shift(quarter.astype(BF16), -1, XL)

    ids = jnp.concatenate(
        [
            src_ids,
            rel_ids,
            dst_ids ^ (core * 1024 + xl * 512),
            rel_ids ^ (core * 1024 + x * 256),
            src_ids ^ (core * 1024 + xl * 512),
            jnp.zeros((3, EDGES), jnp.int32),
        ],
        axis=0,
    )
    negs = (neg_ids ^ (core * 1024 + xl * 512)).reshape(4, NEG)
    head, rel_rows, prod, cnt = call(
        gather_kernel,
        [
            jax.ShapeDtypeStruct((EDGES, D), BF16),
            jax.ShapeDtypeStruct((EDGES, D), F32),
            jax.ShapeDtypeStruct((EDGES, D), F32),
            jax.ShapeDtypeStruct((4, ENT // H, H), F32),
        ],
        0,
        4,
        [pltpu.VMEM((NREL, D), BF16)] * 3,
        flops=4 * 2 * EDGES * ENT * D,
        bytes_accessed=1 << 22,
    )(ids, negs, low, relations)

    kept = jax.ShapeDtypeStruct((ENT // 2, D), F32)
    sent = jax.ShapeDtypeStruct((ENT // 2, D), BF16)
    slots = jax.ShapeDtypeStruct((EDGES, D), F32)
    slots_low = jax.ShapeDtypeStruct((EDGES, D), BF16)
    weights = jax.ShapeDtypeStruct((EDGES, ENT // 2), BF16)
    near_first, head = lax.optimization_barrier((near_first, head))
    near_second = swap(near_first, XL)
    far_first = swap(near_first, CORE)
    cc_first, tails, neg = call(
        first_score_kernel,
        [weights, slots, slots],
        0,
        5,
        flops=3 * EDGES * ENT * D,
        bytes_accessed=1 << 22,
    )(ids, near_first, far_first, prod, cnt)
    near_second, tails = lax.optimization_barrier((near_second, tails))
    far_second = swap(near_second, CORE)
    src_keep, src_send, dst_keep, dst_send, gr = call(
        score_kernel,
        [kept, sent, kept, sent, slots_low],
        1,
        10,
        [
            pltpu.VMEM((EDGES, ENT // 2), BF16),
            pltpu.VMEM((D, EDGES), BF16),
            pltpu.VMEM((EDGES, D), BF16),
            pltpu.VMEM((EDGES, D), BF16),
        ],
        flops=9 * EDGES * ENT * D,
        bytes_accessed=1 << 23,
    )(counts, ids, near_second, far_second, head, rel_rows, prod, cnt, tails, neg, cc_first)
    src_recv = swap(src_send, CORE)
    dst_recv = swap(dst_send, CORE)
    rel_keep, rel_send = call(
        relation_kernel,
        [kept, sent],
        0,
        2,
        flops=2 * EDGES * NREL * D,
        bytes_accessed=1 << 21,
    )(ids, gr)

    rel_recv = swap(rel_send, CORE)
    src_own, src_away = add_split([src_keep, src_recv], 2, own=F32)
    dst_away, dst_own = add_split([dst_keep, dst_recv], 2)
    parts = add_split([rel_keep, rel_recv], 4, own=F32)
    recv = [swap(part, mask) for part, mask in zip(parts[1:], X_MASKS)]
    recv, dst_away, src_away = lax.optimization_barrier((recv, dst_away, src_away))
    dst_other = swap(dst_away, XL)
    src_other = swap(src_away, XL)
    (mine,) = add_split([parts[0], *recv], 1)

    landed = spread(mine.reshape(32, 8, D))
    (dst_sum,) = add_split([dst_own, dst_other], 1)
    dst_total = shift(dst_sum, 1, XL)
    ent_own = sum_with_means([src_own, src_other, dst_total])
    landed, _, src_other = lax.optimization_barrier((landed, dst_sum, src_other))
    summed = sum_rows(landed)
    ent_xl = swap(ent_own, XL)
    total, ent_xl = lax.optimization_barrier((spread(summed), ent_xl))
    ent_core = [swap(ent_own, CORE), swap(ent_xl, CORE)]
    place = (core * 2 + xl).reshape(1)
    new_entities, new_entity_acc = update(
        entities, entity_acc, [ent_own, ent_xl, *ent_core], place
    )
    quarter = sum_with_means([total.reshape(256, D)])
    recv = [swap(quarter, mask) for mask in X_MASKS]
    pieces = [quarter, *recv]
    pieces = pieces + [swap(piece, CORE) for piece in pieces]
    pieces, new_entity_acc = lax.optimization_barrier((pieces, new_entity_acc))
    place = (core * 4 + x).reshape(1)
    new_relations, new_relation_acc = update(relations, relation_acc, pieces, place)
    return (new_entities, new_entity_acc, new_relations, new_relation_acc)


def solution(mesh):
    in_specs = (
        P("blk", None),
        P("blk"),
        P(),
        P(),
        P("blk", "rep"),
        P("blk", "rep"),
        P("blk", "rep"),
        P("blk", "rep"),
        P("blk", "rep"),
    )
    out_specs = (P("blk", None), P("blk"), P(), P())
    return jax.shard_map(shards, mesh=mesh, in_specs=in_specs, out_specs=out_specs, check_vma=False)
```

```python
import functools

import jax
import jax.numpy as jnp
from jax import lax
from jax.experimental import pallas as pl
from jax.experimental.pallas import tpu as pltpu
from jax.sharding import PartitionSpec as P

F32 = jnp.float32
BF16 = jnp.bfloat16
D = 256
H = 128
ENT = 2048
EDGES = 1024
GROUP = 256
NEG = 1024
NREL = 2048
RATE = 0.1
AXES = ("blk", "rep")
VMEM_LIMIT = 32 * 1024 * 1024
UPDATE_VMEM_LIMIT = 51 * 1024 * 1024
CHUNK = 256
UNROLL = 4


def vmem():
    return pl.BlockSpec(memory_space=pltpu.VMEM)


def smem():
    return pl.BlockSpec(memory_space=pltpu.SMEM)


def call(kernel, out_shape, n_smem, n_vmem, scratch=(), flops=0, bytes_accessed=0):
    return pl.pallas_call(
        kernel,
        out_shape=out_shape,
        in_specs=[smem()] * n_smem + [vmem()] * n_vmem,
        out_specs=jax.tree.map(lambda _: vmem(), out_shape),
        scratch_shapes=list(scratch),
        cost_estimate=pl.CostEstimate(
            flops=flops, bytes_accessed=bytes_accessed, transcendentals=0
        ),
        compiler_params=pltpu.CompilerParams(vmem_limit_bytes=VMEM_LIMIT),
    )


def columns(row):
    n = row.shape[1]
    parts = [
        jnp.transpose(jnp.broadcast_to(row[:, i : i + H], (H, H))) for i in range(0, n, H)
    ]
    return parts[0] if len(parts) == 1 else jnp.concatenate(parts, axis=0)


def one_hot_rows(col, n, base=0):
    e = col.shape[0]
    lane = lax.broadcasted_iota(jnp.int32, (e, H), 1)
    parts = [jnp.where(col == lane + (base + j), 1.0, 0.0).astype(BF16) for j in range(0, n, H)]
    return jnp.concatenate(parts, axis=1)


def one_hot_cols(row, n, base):
    e = row.shape[1]
    sub = lax.broadcasted_iota(jnp.int32, (n, e), 0) + base
    return jnp.where(jnp.broadcast_to(row, (n, e)) == sub, 1.0, 0.0).astype(BF16)


def dot(a, b):
    return jnp.dot(a, b, preferred_element_type=F32)


def dot_nt(a, b):
    return lax.dot_general(a, b, (((1,), (1,)), ((), ())), preferred_element_type=F32)


def gather_kernel(ids_ref, negs_ref, low_ref, rel_ref, head_ref, relrow_ref, prod_ref, cnt_ref, hi_ref, mid_ref, lo_ref):
    for r in range(0, NREL, 256):
        x = rel_ref[r : r + 256, :]
        for ref in (hi_ref, mid_ref, lo_ref):
            part = x.astype(BF16)
            ref[r : r + 256, :] = part
            x = x - part.astype(F32)

    def group(g, _):
        rows = pl.ds(pl.multiple_of(g * GROUP, GROUP), GROUP)
        src = columns(ids_ref[0:1, rows])
        heads = dot(one_hot_rows(src, ENT), low_ref[...])
        pick = one_hot_rows(columns(ids_ref[1:2, rows]), NREL)
        rel = dot(pick, hi_ref[...]) + dot(pick, mid_ref[...]) + dot(pick, lo_ref[...])
        hr, hi, rr, ri = heads[:, :H], heads[:, H:], rel[:, :H], rel[:, H:]
        head_ref[rows, :] = heads.astype(BF16)
        relrow_ref[rows, :] = rel
        prod_ref[rows, :H] = hr * rr - hi * ri
        prod_ref[rows, H:] = hr * ri + hi * rr
        negs = negs_ref[pl.ds(g, 1), :]
        high = one_hot_cols(lax.shift_right_logical(negs, 7), ENT // H, 0)
        low = one_hot_cols(lax.bitwise_and(negs, H - 1), H, 0)
        cnt_ref[g] = dot_nt(high, low) * (1.0 / NEG)
        return 0

    lax.fori_loop(0, EDGES // GROUP, group, 0, unroll=UNROLL)


def against(part, ids_ref, near_ref, far_ref, prod_ref, cnt_ref, cc_ref, rows, g):
    size = near_ref.shape[0]
    dst = columns(ids_ref[2:3, rows])
    low = prod_ref[rows, :].astype(BF16)
    tails = neg = None
    for j, table in ((0, near_ref), (1, far_ref)):
        base = j * (ENT // 2) + part * size
        tail = dot(one_hot_rows(dst, size, base), table[...])
        scores = dot_nt(low, table[...])
        for i in range(size // H):
            w = cnt_ref[g, base // H + i : base // H + i + 1, :]
            cc_ref[rows, j * size + i * H : j * size + (i + 1) * H] = (
                jax.nn.sigmoid(scores[:, i * H : (i + 1) * H]) * w
            ).astype(BF16)
        drawn = dot(cc_ref[rows, j * size : (j + 1) * size], table[...])
        tails = tail if tails is None else tails + tail
        neg = drawn if neg is None else neg + drawn
    return tails, neg


def first_score_kernel(ids_ref, near_ref, far_ref, prod_ref, cnt_ref, cc_ref, tails_ref, neg_ref):
    def group(g, _):
        rows = pl.ds(pl.multiple_of(g * GROUP, GROUP), GROUP)
        tails, neg = against(0, ids_ref, near_ref, far_ref, prod_ref, cnt_ref, cc_ref, rows, g)
        tails_ref[rows, :] = tails
        neg_ref[rows, :] = neg
        return 0

    lax.fori_loop(0, EDGES // GROUP, group, 0, unroll=UNROLL)


def score_kernel(
    count_ref,
    ids_ref,
    near_ref,
    far_ref,
    head_ref,
    relrow_ref,
    prod_ref,
    cnt_ref,
    tails_ref,
    neg_ref,
    first_ref,
    src_keep_ref,
    src_send_ref,
    dst_keep_ref,
    dst_send_ref,
    gr_ref,
    cc_ref,
    plt_ref,
    pd_ref,
    gh_ref,
):
    half = ENT // 2
    quarter = half // 2
    count = count_ref[0, 0]

    def group(g, _):
        rows = pl.ds(pl.multiple_of(g * GROUP, GROUP), GROUP)
        tails, neg = against(1, ids_ref, near_ref, far_ref, prod_ref, cnt_ref, cc_ref, rows, g)
        tails = tails + tails_ref[rows, :]
        neg = neg + neg_ref[rows, :]
        prod = prod_ref[rows, :]
        edge = lax.broadcasted_iota(jnp.int32, (GROUP, 1), 0) + g * GROUP
        live = jnp.where(edge < count, 1.0, 0.0).astype(F32)
        positive = jnp.sum(prod * tails, axis=1, keepdims=True)
        pos = -live * jax.nn.sigmoid(-positive)
        grad = pos * tails + live * neg
        rel = relrow_ref[rows, :]
        head = head_ref[rows, :].astype(F32)
        gr, gi = grad[:, :H], grad[:, H:]
        for out, other in ((gh_ref, rel), (gr_ref, head)):
            a, b = other[:, :H], other[:, H:]
            out[rows, :H] = (gr * a + gi * b).astype(BF16)
            out[rows, H:] = (gi * a - gr * b).astype(BF16)
        pd_ref[rows, :] = (pos * prod).astype(BF16)
        plt_ref[:, rows] = jnp.transpose(live * prod).astype(BF16)
        return 0

    lax.fori_loop(0, EDGES // GROUP, group, 0, unroll=UNROLL)

    for part, ref in ((0, first_ref), (1, cc_ref)):
        for i in range(quarter // CHUNK):
            at = part * quarter + i * CHUNK
            rows = slice(at, at + CHUNK)
            for j, src_ref, dst_ref in (
                (0, src_keep_ref, dst_keep_ref),
                (1, src_send_ref, dst_send_ref),
            ):
                src = dot(one_hot_cols(ids_ref[4:5, :], CHUNK, j * half + at), gh_ref[...])
                src_ref[rows, :] = src.astype(src_ref.dtype)
                cols = slice(j * quarter + i * CHUNK, j * quarter + (i + 1) * CHUNK)
                drawn = jnp.transpose(dot(plt_ref[...], ref[:, cols]))
                dst = dot(one_hot_cols(ids_ref[2:3, :], CHUNK, j * half + at), pd_ref[...])
                dst_ref[rows, :] = (drawn + dst).astype(dst_ref.dtype)


def relation_kernel(ids_ref, gr_ref, keep_ref, send_ref):
    half = NREL // 2
    for i in range(half // CHUNK):
        rows = slice(i * CHUNK, (i + 1) * CHUNK)
        keep_ref[rows, :] = dot(one_hot_cols(ids_ref[3:4, :], CHUNK, i * CHUNK), gr_ref[...])
        send_ref[rows, :] = dot(
            one_hot_cols(ids_ref[3:4, :], CHUNK, half + i * CHUNK), gr_ref[...]
        ).astype(BF16)


def add_split_kernel(n_in, n_out, *refs):
    ins, outs = refs[:n_in], refs[n_in:]
    size = outs[0].shape[0]
    step = min(size, 64)
    for k, out in enumerate(outs):
        for r in range(0, size, step):
            total = ins[0][k * size + r : k * size + r + step, :].astype(F32)
            for ref in ins[1:]:
                total = total + ref[k * size + r : k * size + r + step, :].astype(F32)
            out[r : r + step, :] = total.astype(out.dtype)


def add_split(parts, n_out, own=BF16, sent=BF16):
    rows = parts[0].shape[0] // n_out
    shapes = [jax.ShapeDtypeStruct((rows, D), sent if k else own) for k in range(n_out)]
    return call(
        functools.partial(add_split_kernel, len(parts), n_out),
        shapes,
        0,
        len(parts),
        flops=len(parts) * n_out * rows * D,
        bytes_accessed=3 * len(parts) * n_out * rows * D,
    )(*parts)


def split3(x):
    hi = x.astype(BF16).astype(F32)
    mid = (x - hi).astype(BF16).astype(F32)
    return hi, mid, x - hi - mid


def sum_with_means_kernel(*refs):
    parts, out_ref = refs[:-1], refs[-1]
    rows = parts[0].shape[0]
    means = []
    for r in range(0, rows, H):
        total = parts[0][r : r + H, :].astype(F32)
        for ref in parts[1:]:
            total = total + ref[r : r + H, :].astype(F32)
        out_ref[r : r + H, :] = total.astype(BF16)
        mean = jnp.sum(total * total, axis=1, keepdims=True) * (1.0 / D)
        means.append(jnp.transpose(jnp.broadcast_to(mean, (H, H)))[0:1, :])
    means.append(jnp.zeros((8 - len(means), H), F32))
    hi, mid, lo = split3(jnp.concatenate(means, axis=0))
    top = jnp.concatenate([hi, mid], axis=1)
    bottom = jnp.concatenate([lo, jnp.zeros_like(lo)], axis=1)
    out_ref[rows : rows + 16, :] = jnp.concatenate([top, bottom], axis=0).astype(BF16)


def sum_with_means(parts):
    rows = parts[0].shape[0]
    return call(
        sum_with_means_kernel,
        jax.ShapeDtypeStruct((rows + 16, D), BF16),
        0,
        len(parts),
        flops=len(parts) * rows * D,
        bytes_accessed=3 * len(parts) * rows * D,
    )(*parts)


def means_of(piece, start, row):
    tile = piece[start : start + 16, :].astype(F32)
    return tile[row : row + 1, :H] + tile[row : row + 1, H:] + tile[8 + row : 9 + row, :H]


def update_kernel(counts, place_ref, *refs):
    tables = len(counts)
    n_in = 2 * tables + sum(counts)
    ins, outs = refs[:n_in], refs[n_in : n_in + 2 * tables]
    in_sem, out_sem, *bufs = refs[n_in + 2 * tables :]
    held, bufs = bufs[:tables], bufs[tables:]
    fetches = []
    for t, n in enumerate(counts):
        rows_ref = ins[2 * t + sum(counts[:t])]
        size = rows_ref.shape[0] // n
        for k in range(n):
            i = lax.bitwise_xor(k, place_ref[t])
            rows = pl.ds(pl.multiple_of(i * size, size), size)
            fetch = pltpu.make_async_copy(
                rows_ref.at[rows, :], held[t].at[rows, :], in_sem.at[len(fetches)]
            )
            fetch.start()
            fetches.append(fetch)
    copies = []
    for t, n in enumerate(counts):
        rows_ref, acc_ref, *rest = ins
        pieces, ins = rest[:n], rest[n:]
        new_ref, new_acc_ref = outs[2 * t : 2 * t + 2]
        size = rows_ref.shape[0] // n
        for k, piece in enumerate(pieces):
            i = lax.bitwise_xor(k, place_ref[t])
            fetches[len(copies)].wait()
            for r in range(0, size, H):
                g = piece[r : r + H, :].astype(F32)
                at = pl.ds(i * (size // H) + r // H, 1)
                acc = acc_ref[at, :] + means_of(piece, size, r // H)
                new_acc_ref[at, :] = acc
                scale = jnp.transpose(jnp.broadcast_to(RATE / jnp.sqrt(acc), (H, H)))
                rows = pl.ds(pl.multiple_of(i * size + r, H), H)
                bufs[t][rows, :H] = held[t][rows, :H] - g[:, :H] * scale
                bufs[t][rows, H:] = held[t][rows, H:] - g[:, H:] * scale
            rows = pl.ds(pl.multiple_of(i * size, size), size)
            copy = pltpu.make_async_copy(
                bufs[t].at[rows, :], new_ref.at[rows, :], out_sem.at[len(copies)]
            )
            copy.start()
            copies.append(copy)
    for copy in copies:
        copy.wait()


def update(place, *tables):
    counts = tuple(len(pieces) for _, _, pieces in tables)
    operands, shapes, bufs, specs = [], [], [], []
    for rows, acc, pieces in tables:
        n = rows.shape[0]
        operands += [rows, acc.reshape(n // H, H), *pieces]
        specs += [pl.BlockSpec(memory_space=pl.ANY)] + [vmem()] * (1 + len(pieces))
        shapes += [
            jax.ShapeDtypeStruct((n, D), F32),
            jax.ShapeDtypeStruct((n // H, H), F32),
        ]
        bufs.append(pltpu.VMEM((n, D), F32))
    outs = pl.pallas_call(
        functools.partial(update_kernel, counts),
        out_shape=shapes,
        in_specs=[smem()] + specs,
        out_specs=[pl.BlockSpec(memory_space=pl.ANY), vmem()] * len(tables),
        scratch_shapes=[pltpu.SemaphoreType.DMA((sum(counts),))] * 2 + bufs * 2,
        cost_estimate=pl.CostEstimate(
            flops=16 * ENT * D, bytes_accessed=20 * ENT * D, transcendentals=2 * ENT
        ),
        compiler_params=pltpu.CompilerParams(vmem_limit_bytes=UPDATE_VMEM_LIMIT),
    )(place, *operands)
    return [out.reshape(-1) if out.shape[1] == H else out for out in outs]


def sum_rows_kernel(parts_ref, out_ref):
    total = parts_ref[0].astype(F32)
    for k in range(1, parts_ref.shape[0]):
        total = total + parts_ref[k].astype(F32)
    out_ref[...] = jnp.broadcast_to(total, out_ref.shape)


def sum_rows(parts):
    return call(
        sum_rows_kernel,
        jax.ShapeDtypeStruct(parts.shape, F32),
        0,
        1,
        flops=parts.size,
        bytes_accessed=6 * parts.size,
    )(parts)


def spread(parts):
    groups = [[2 * k + hi for k in range(32)] for hi in range(2)]
    return lax.all_to_all(parts, "blk", 0, 0, axis_index_groups=groups, tiled=True)


def swap(x, mask):
    return lax.ppermute(x, AXES, [(i, i ^ mask) for i in range(256)])


def shift(x, distance, mask):
    route = [(((i // 4 - distance) % 64) * 4 + ((i % 4) ^ mask), i) for i in range(256)]
    return lax.ppermute(x, AXES, route)


CORE, XL = 1, 2
X_MASKS = (2, 4, 6)


def shards(
    entities, entity_acc, relations, relation_acc, src_ids, rel_ids, dst_ids, neg_ids, counts
):
    blk, rep = lax.axis_index("blk"), lax.axis_index("rep")
    core, xl = rep % 2, rep // 2
    x = (blk % 2) * 2 + xl

    low = entities.astype(BF16)
    quarter = lax.dynamic_slice_in_dim(entities, core * 1024 + (1 - xl) * 512, 512, 0)
    near_first = shift(quarter.astype(BF16), -1, XL)

    ids = jnp.concatenate(
        [
            src_ids,
            rel_ids,
            dst_ids ^ (core * 1024 + xl * 512),
            rel_ids ^ (core * 1024 + x * 256),
            src_ids ^ (core * 1024 + xl * 512),
            jnp.zeros((3, EDGES), jnp.int32),
        ],
        axis=0,
    )
    negs = (neg_ids ^ (core * 1024 + xl * 512)).reshape(4, NEG)
    head, rel_rows, prod, cnt = call(
        gather_kernel,
        [
            jax.ShapeDtypeStruct((EDGES, D), BF16),
            jax.ShapeDtypeStruct((EDGES, D), F32),
            jax.ShapeDtypeStruct((EDGES, D), F32),
            jax.ShapeDtypeStruct((4, ENT // H, H), F32),
        ],
        0,
        4,
        [pltpu.VMEM((NREL, D), BF16)] * 3,
        flops=4 * 2 * EDGES * ENT * D,
        bytes_accessed=1 << 22,
    )(ids, negs, low, relations)

    kept = jax.ShapeDtypeStruct((ENT // 2, D), F32)
    sent = jax.ShapeDtypeStruct((ENT // 2, D), BF16)
    slots = jax.ShapeDtypeStruct((EDGES, D), F32)
    slots_low = jax.ShapeDtypeStruct((EDGES, D), BF16)
    weights = jax.ShapeDtypeStruct((EDGES, ENT // 2), BF16)
    near_first, head = lax.optimization_barrier((near_first, head))
    near_second = swap(near_first, XL)
    far_first = swap(near_first, CORE)
    cc_first, tails, neg = call(
        first_score_kernel,
        [weights, slots, slots],
        0,
        5,
        flops=3 * EDGES * ENT * D,
        bytes_accessed=1 << 22,
    )(ids, near_first, far_first, prod, cnt)
    near_second, tails = lax.optimization_barrier((near_second, tails))
    far_second = swap(near_second, CORE)
    src_keep, src_send, dst_keep, dst_send, gr = call(
        score_kernel,
        [kept, sent, kept, sent, slots_low],
        1,
        10,
        [
            pltpu.VMEM((EDGES, ENT // 2), BF16),
            pltpu.VMEM((D, EDGES), BF16),
            pltpu.VMEM((EDGES, D), BF16),
            pltpu.VMEM((EDGES, D), BF16),
        ],
        flops=9 * EDGES * ENT * D,
        bytes_accessed=1 << 23,
    )(counts, ids, near_second, far_second, head, rel_rows, prod, cnt, tails, neg, cc_first)
    src_recv = swap(src_send, CORE)
    dst_recv = swap(dst_send, CORE)
    rel_keep, rel_send = call(
        relation_kernel,
        [kept, sent],
        0,
        2,
        flops=2 * EDGES * NREL * D,
        bytes_accessed=1 << 21,
    )(ids, gr)

    rel_recv = swap(rel_send, CORE)
    src_own, src_away = add_split([src_keep, src_recv], 2, own=F32)
    dst_away, dst_own = add_split([dst_keep, dst_recv], 2)
    parts = add_split([rel_keep, rel_recv], 4, own=F32)
    recv = [swap(part, mask) for part, mask in zip(parts[1:], X_MASKS)]
    recv, dst_away, src_away = lax.optimization_barrier((recv, dst_away, src_away))
    dst_other = swap(dst_away, XL)
    src_other = swap(src_away, XL)
    (mine,) = add_split([parts[0], *recv], 1)

    landed = spread(mine.reshape(32, 8, D))
    (dst_sum,) = add_split([dst_own, dst_other], 1)
    dst_total = shift(dst_sum, 1, XL)
    ent_own = sum_with_means([src_own, src_other, dst_total])
    landed, _, src_other = lax.optimization_barrier((landed, dst_sum, src_other))
    summed = sum_rows(landed)
    ent_xl = swap(ent_own, XL)
    total, ent_xl = lax.optimization_barrier((spread(summed), ent_xl))
    ent_core = [swap(ent_own, CORE), swap(ent_xl, CORE)]
    quarter = sum_with_means([total.reshape(256, D)])
    recv = [swap(quarter, mask) for mask in X_MASKS]
    pieces = [quarter, *recv]
    pieces = pieces + [swap(piece, CORE) for piece in pieces]
    place = jnp.stack([core * 2 + xl, core * 4 + x])
    return tuple(
        update(
            place,
            (entities, entity_acc, [ent_own, ent_xl, *ent_core]),
            (relations, relation_acc, pieces),
        )
    )


def solution(mesh):
    in_specs = (
        P("blk", None),
        P("blk"),
        P(),
        P(),
        P("blk", "rep"),
        P("blk", "rep"),
        P("blk", "rep"),
        P("blk", "rep"),
        P("blk", "rep"),
    )
    out_specs = (P("blk", None), P("blk"), P(), P())
    return jax.shard_map(shards, mesh=mesh, in_specs=in_specs, out_specs=out_specs, check_vma=False)
```

```python
import functools

import jax
import jax.numpy as jnp
from jax import lax
from jax.experimental import pallas as pl
from jax.experimental.pallas import tpu as pltpu
from jax.sharding import PartitionSpec as P

F32 = jnp.float32
BF16 = jnp.bfloat16
D = 256
H = 128
ENT = 2048
EDGES = 1024
GROUP = 256
NEG = 1024
NREL = 2048
RATE = 0.1
AXES = ("blk", "rep")
VMEM_LIMIT = 32 * 1024 * 1024
UPDATE_VMEM_LIMIT = 51 * 1024 * 1024
CHUNK = 256
UNROLL = 4


def vmem():
    return pl.BlockSpec(memory_space=pltpu.VMEM)


def smem():
    return pl.BlockSpec(memory_space=pltpu.SMEM)


def call(kernel, out_shape, n_smem, n_vmem, scratch=(), flops=0, bytes_accessed=0):
    return pl.pallas_call(
        kernel,
        out_shape=out_shape,
        in_specs=[smem()] * n_smem + [vmem()] * n_vmem,
        out_specs=jax.tree.map(lambda _: vmem(), out_shape),
        scratch_shapes=list(scratch),
        cost_estimate=pl.CostEstimate(
            flops=flops, bytes_accessed=bytes_accessed, transcendentals=0
        ),
        compiler_params=pltpu.CompilerParams(vmem_limit_bytes=VMEM_LIMIT),
    )


def columns(row):
    n = row.shape[1]
    parts = [
        jnp.transpose(jnp.broadcast_to(row[:, i : i + H], (H, H))) for i in range(0, n, H)
    ]
    return parts[0] if len(parts) == 1 else jnp.concatenate(parts, axis=0)


def one_hot_rows(col, n, base=0):
    e = col.shape[0]
    lane = lax.broadcasted_iota(jnp.int32, (e, H), 1)
    parts = [jnp.where(col == lane + (base + j), 1.0, 0.0).astype(BF16) for j in range(0, n, H)]
    return jnp.concatenate(parts, axis=1)


def one_hot_cols(row, n, base):
    e = row.shape[1]
    sub = lax.broadcasted_iota(jnp.int32, (n, e), 0) + base
    return jnp.where(jnp.broadcast_to(row, (n, e)) == sub, 1.0, 0.0).astype(BF16)


def dot(a, b):
    return jnp.dot(a, b, preferred_element_type=F32)


def dot_nt(a, b):
    return lax.dot_general(a, b, (((1,), (1,)), ((), ())), preferred_element_type=F32)


def gather_kernel(ids_ref, negs_ref, low_ref, rel_ref, head_ref, relrow_ref, prod_ref, cnt_ref, hi_ref, mid_ref, lo_ref):
    for r in range(0, NREL, 256):
        x = rel_ref[r : r + 256, :]
        for ref in (hi_ref, mid_ref, lo_ref):
            part = x.astype(BF16)
            ref[r : r + 256, :] = part
            x = x - part.astype(F32)

    def group(g, _):
        rows = pl.ds(pl.multiple_of(g * GROUP, GROUP), GROUP)
        src = columns(ids_ref[0:1, rows])
        heads = dot(one_hot_rows(src, ENT), low_ref[...])
        pick = one_hot_rows(columns(ids_ref[1:2, rows]), NREL)
        rel = dot(pick, hi_ref[...]) + dot(pick, mid_ref[...]) + dot(pick, lo_ref[...])
        hr, hi, rr, ri = heads[:, :H], heads[:, H:], rel[:, :H], rel[:, H:]
        head_ref[rows, :] = heads.astype(BF16)
        relrow_ref[rows, :] = rel
        prod_ref[rows, :H] = hr * rr - hi * ri
        prod_ref[rows, H:] = hr * ri + hi * rr
        negs = negs_ref[pl.ds(g, 1), :]
        high = one_hot_cols(lax.shift_right_logical(negs, 7), ENT // H, 0)
        low = one_hot_cols(lax.bitwise_and(negs, H - 1), H, 0)
        cnt_ref[g] = dot_nt(high, low) * (1.0 / NEG)
        return 0

    lax.fori_loop(0, EDGES // GROUP, group, 0, unroll=UNROLL)


def against(part, ids_ref, near_ref, far_ref, prod_ref, cnt_ref, cc_ref, rows, g):
    size = near_ref.shape[0]
    dst = columns(ids_ref[2:3, rows])
    low = prod_ref[rows, :].astype(BF16)
    tails = neg = None
    for j, table in ((0, near_ref), (1, far_ref)):
        base = j * (ENT // 2) + part * size
        tail = dot(one_hot_rows(dst, size, base), table[...])
        scores = dot_nt(low, table[...])
        for i in range(size // H):
            w = cnt_ref[g, base // H + i : base // H + i + 1, :]
            cc_ref[rows, j * size + i * H : j * size + (i + 1) * H] = (
                jax.nn.sigmoid(scores[:, i * H : (i + 1) * H]) * w
            ).astype(BF16)
        drawn = dot(cc_ref[rows, j * size : (j + 1) * size], table[...])
        tails = tail if tails is None else tails + tail
        neg = drawn if neg is None else neg + drawn
    return tails, neg


def first_score_kernel(ids_ref, near_ref, far_ref, prod_ref, cnt_ref, cc_ref, tails_ref, neg_ref):
    def group(g, _):
        rows = pl.ds(pl.multiple_of(g * GROUP, GROUP), GROUP)
        tails, neg = against(0, ids_ref, near_ref, far_ref, prod_ref, cnt_ref, cc_ref, rows, g)
        tails_ref[rows, :] = tails
        neg_ref[rows, :] = neg
        return 0

    lax.fori_loop(0, EDGES // GROUP, group, 0, unroll=UNROLL)


def score_kernel(
    count_ref,
    ids_ref,
    near_ref,
    far_ref,
    head_ref,
    relrow_ref,
    prod_ref,
    cnt_ref,
    tails_ref,
    neg_ref,
    first_ref,
    src_keep_ref,
    src_send_ref,
    dst_keep_ref,
    dst_send_ref,
    gr_ref,
    cc_ref,
    plt_ref,
    pd_ref,
    gh_ref,
):
    half = ENT // 2
    quarter = half // 2
    count = count_ref[0, 0]

    def group(g, _):
        rows = pl.ds(pl.multiple_of(g * GROUP, GROUP), GROUP)
        tails, neg = against(1, ids_ref, near_ref, far_ref, prod_ref, cnt_ref, cc_ref, rows, g)
        tails = tails + tails_ref[rows, :]
        neg = neg + neg_ref[rows, :]
        prod = prod_ref[rows, :]
        edge = lax.broadcasted_iota(jnp.int32, (GROUP, 1), 0) + g * GROUP
        live = jnp.where(edge < count, 1.0, 0.0).astype(F32)
        positive = jnp.sum(prod * tails, axis=1, keepdims=True)
        pos = -live * jax.nn.sigmoid(-positive)
        grad = pos * tails + live * neg
        rel = relrow_ref[rows, :]
        head = head_ref[rows, :].astype(F32)
        gr, gi = grad[:, :H], grad[:, H:]
        for out, other in ((gh_ref, rel), (gr_ref, head)):
            a, b = other[:, :H], other[:, H:]
            out[rows, :H] = (gr * a + gi * b).astype(BF16)
            out[rows, H:] = (gi * a - gr * b).astype(BF16)
        pd_ref[rows, :] = (pos * prod).astype(BF16)
        plt_ref[:, rows] = jnp.transpose(live * prod).astype(BF16)
        return 0

    lax.fori_loop(0, EDGES // GROUP, group, 0, unroll=UNROLL)

    for part, ref in ((0, first_ref), (1, cc_ref)):
        for i in range(quarter // CHUNK):
            at = part * quarter + i * CHUNK
            rows = slice(at, at + CHUNK)
            for j, src_ref, dst_ref in (
                (0, src_keep_ref, dst_keep_ref),
                (1, src_send_ref, dst_send_ref),
            ):
                src = dot(one_hot_cols(ids_ref[4:5, :], CHUNK, j * half + at), gh_ref[...])
                src_ref[rows, :] = src.astype(src_ref.dtype)
                cols = slice(j * quarter + i * CHUNK, j * quarter + (i + 1) * CHUNK)
                drawn = jnp.transpose(dot(plt_ref[...], ref[:, cols]))
                dst = dot(one_hot_cols(ids_ref[2:3, :], CHUNK, j * half + at), pd_ref[...])
                dst_ref[rows, :] = (drawn + dst).astype(dst_ref.dtype)


def relation_kernel(ids_ref, gr_ref, keep_ref, send_ref):
    half = NREL // 2
    for i in range(half // CHUNK):
        rows = slice(i * CHUNK, (i + 1) * CHUNK)
        keep_ref[rows, :] = dot(one_hot_cols(ids_ref[3:4, :], CHUNK, i * CHUNK), gr_ref[...])
        send_ref[rows, :] = dot(
            one_hot_cols(ids_ref[3:4, :], CHUNK, half + i * CHUNK), gr_ref[...]
        ).astype(BF16)


def add_split_kernel(n_in, n_out, *refs):
    ins, outs = refs[:n_in], refs[n_in:]
    size = outs[0].shape[0]
    step = min(size, 64)
    for k, out in enumerate(outs):
        for r in range(0, size, step):
            total = ins[0][k * size + r : k * size + r + step, :].astype(F32)
            for ref in ins[1:]:
                total = total + ref[k * size + r : k * size + r + step, :].astype(F32)
            out[r : r + step, :] = total.astype(out.dtype)


def add_split(parts, n_out, own=BF16, sent=BF16):
    rows = parts[0].shape[0] // n_out
    shapes = [jax.ShapeDtypeStruct((rows, D), sent if k else own) for k in range(n_out)]
    return call(
        functools.partial(add_split_kernel, len(parts), n_out),
        shapes,
        0,
        len(parts),
        flops=len(parts) * n_out * rows * D,
        bytes_accessed=3 * len(parts) * n_out * rows * D,
    )(*parts)


def split3(x):
    hi = x.astype(BF16).astype(F32)
    mid = (x - hi).astype(BF16).astype(F32)
    return hi, mid, x - hi - mid


def sum_with_means_kernel(*refs):
    parts, out_ref = refs[:-1], refs[-1]
    rows = parts[0].shape[0]
    means = []
    for r in range(0, rows, H):
        total = parts[0][r : r + H, :].astype(F32)
        for ref in parts[1:]:
            total = total + ref[r : r + H, :].astype(F32)
        out_ref[r : r + H, :] = total.astype(BF16)
        mean = jnp.sum(total * total, axis=1, keepdims=True) * (1.0 / D)
        means.append(jnp.transpose(jnp.broadcast_to(mean, (H, H)))[0:1, :])
    means.append(jnp.zeros((8 - len(means), H), F32))
    hi, mid, lo = split3(jnp.concatenate(means, axis=0))
    top = jnp.concatenate([hi, mid], axis=1)
    bottom = jnp.concatenate([lo, jnp.zeros_like(lo)], axis=1)
    out_ref[rows : rows + 16, :] = jnp.concatenate([top, bottom], axis=0).astype(BF16)


def sum_with_means(parts):
    rows = parts[0].shape[0]
    return call(
        sum_with_means_kernel,
        jax.ShapeDtypeStruct((rows + 16, D), BF16),
        0,
        len(parts),
        flops=len(parts) * rows * D,
        bytes_accessed=3 * len(parts) * rows * D,
    )(*parts)


def means_of(piece, start, row):
    tile = piece[start : start + 16, :].astype(F32)
    return tile[row : row + 1, :H] + tile[row : row + 1, H:] + tile[8 + row : 9 + row, :H]


def update_kernel(counts, place_ref, *refs):
    tables = len(counts)
    n_in = 2 * tables + sum(counts)
    ins, outs = refs[:n_in], refs[n_in : n_in + 2 * tables]
    in_sem, out_sem, *bufs = refs[n_in + 2 * tables :]
    held, bufs = bufs[:tables], bufs[tables:]
    fetches = []
    for t, n in enumerate(counts):
        rows_ref = ins[2 * t + sum(counts[:t])]
        size = rows_ref.shape[0] // n
        for k in range(n):
            i = lax.bitwise_xor(k, place_ref[t])
            rows = pl.ds(pl.multiple_of(i * size, size), size)
            fetch = pltpu.make_async_copy(
                rows_ref.at[rows, :], held[t].at[rows, :], in_sem.at[len(fetches)]
            )
            fetch.start()
            fetches.append(fetch)
    copies = []
    for t, n in enumerate(counts):
        rows_ref, acc_ref, *rest = ins
        pieces, ins = rest[:n], rest[n:]
        new_ref, new_acc_ref = outs[2 * t : 2 * t + 2]
        size = rows_ref.shape[0] // n
        for k, piece in enumerate(pieces):
            i = lax.bitwise_xor(k, place_ref[t])
            fetches[len(copies)].wait()
            for r in range(0, size, H):
                g = piece[r : r + H, :].astype(F32)
                at = pl.ds(i * (size // H) + r // H, 1)
                acc = acc_ref[at, :] + means_of(piece, size, r // H)
                new_acc_ref[at, :] = acc
                scale = jnp.transpose(jnp.broadcast_to(RATE / jnp.sqrt(acc), (H, H)))
                rows = pl.ds(pl.multiple_of(i * size + r, H), H)
                bufs[t][rows, :H] = held[t][rows, :H] - g[:, :H] * scale
                bufs[t][rows, H:] = held[t][rows, H:] - g[:, H:] * scale
            rows = pl.ds(pl.multiple_of(i * size, size), size)
            copy = pltpu.make_async_copy(
                bufs[t].at[rows, :], new_ref.at[rows, :], out_sem.at[len(copies)]
            )
            copy.start()
            copies.append(copy)
    for copy in copies:
        copy.wait()


def update(place, *tables):
    counts = tuple(len(pieces) for _, _, pieces in tables)
    operands, shapes, bufs, specs = [], [], [], []
    for rows, acc, pieces in tables:
        n = rows.shape[0]
        operands += [rows, acc.reshape(n // H, H), *pieces]
        specs += [pl.BlockSpec(memory_space=pl.ANY)] + [vmem()] * (1 + len(pieces))
        shapes += [
            jax.ShapeDtypeStruct((n, D), F32),
            jax.ShapeDtypeStruct((n // H, H), F32),
        ]
        bufs.append(pltpu.VMEM((n, D), F32))
    outs = pl.pallas_call(
        functools.partial(update_kernel, counts),
        out_shape=shapes,
        in_specs=[smem()] + specs,
        out_specs=[pl.BlockSpec(memory_space=pl.ANY), vmem()] * len(tables),
        scratch_shapes=[pltpu.SemaphoreType.DMA((sum(counts),))] * 2 + bufs * 2,
        cost_estimate=pl.CostEstimate(
            flops=16 * ENT * D, bytes_accessed=20 * ENT * D, transcendentals=2 * ENT
        ),
        compiler_params=pltpu.CompilerParams(vmem_limit_bytes=UPDATE_VMEM_LIMIT),
    )(place, *operands)
    return [out.reshape(-1) if out.shape[1] == H else out for out in outs]


def sum_rows_kernel(parts_ref, out_ref):
    total = parts_ref[0].astype(F32)
    for k in range(1, parts_ref.shape[0]):
        total = total + parts_ref[k].astype(F32)
    out_ref[...] = jnp.broadcast_to(total, out_ref.shape)


def sum_rows(parts):
    return call(
        sum_rows_kernel,
        jax.ShapeDtypeStruct(parts.shape, F32),
        0,
        1,
        flops=parts.size,
        bytes_accessed=6 * parts.size,
    )(parts)


def spread(parts):
    groups = [[2 * k + hi for k in range(32)] for hi in range(2)]
    return lax.all_to_all(parts, "blk", 0, 0, axis_index_groups=groups, tiled=True)


def swap(x, mask):
    return lax.ppermute(x, AXES, [(i, i ^ mask) for i in range(256)])


def shift(x, distance, mask):
    route = [(((i // 4 - distance) % 64) * 4 + ((i % 4) ^ mask), i) for i in range(256)]
    return lax.ppermute(x, AXES, route)


CORE, XL = 1, 2
X_MASKS = (2, 4, 6)


def shards(
    entities, entity_acc, relations, relation_acc, src_ids, rel_ids, dst_ids, neg_ids, counts
):
    blk, rep = lax.axis_index("blk"), lax.axis_index("rep")
    core, xl = rep % 2, rep // 2
    x = (blk % 2) * 2 + xl

    low = entities.astype(BF16)
    quarter = lax.dynamic_slice_in_dim(entities, core * 1024 + (1 - xl) * 512, 512, 0)
    near_first = shift(quarter.astype(BF16), -1, XL)

    ids = jnp.concatenate(
        [
            src_ids,
            rel_ids,
            dst_ids ^ (core * 1024 + xl * 512),
            rel_ids ^ (core * 1024 + x * 256),
            src_ids ^ (core * 1024 + xl * 512),
            jnp.zeros((3, EDGES), jnp.int32),
        ],
        axis=0,
    )
    negs = (neg_ids ^ (core * 1024 + xl * 512)).reshape(4, NEG)
    head, rel_rows, prod, cnt = call(
        gather_kernel,
        [
            jax.ShapeDtypeStruct((EDGES, D), BF16),
            jax.ShapeDtypeStruct((EDGES, D), F32),
            jax.ShapeDtypeStruct((EDGES, D), F32),
            jax.ShapeDtypeStruct((4, ENT // H, H), F32),
        ],
        0,
        4,
        [pltpu.VMEM((NREL, D), BF16)] * 3,
        flops=4 * 2 * EDGES * ENT * D,
        bytes_accessed=1 << 22,
    )(ids, negs, low, relations)

    kept = jax.ShapeDtypeStruct((ENT // 2, D), F32)
    sent = jax.ShapeDtypeStruct((ENT // 2, D), BF16)
    slots = jax.ShapeDtypeStruct((EDGES, D), F32)
    slots_low = jax.ShapeDtypeStruct((EDGES, D), BF16)
    weights = jax.ShapeDtypeStruct((EDGES, ENT // 2), BF16)
    near_first, head = lax.optimization_barrier((near_first, head))
    near_second = swap(near_first, XL)
    far_first = swap(near_first, CORE)
    cc_first, tails, neg = call(
        first_score_kernel,
        [weights, slots, slots],
        0,
        5,
        flops=3 * EDGES * ENT * D,
        bytes_accessed=1 << 22,
    )(ids, near_first, far_first, prod, cnt)
    near_second, tails = lax.optimization_barrier((near_second, tails))
    far_second = swap(near_second, CORE)
    src_keep, src_send, dst_keep, dst_send, gr = call(
        score_kernel,
        [kept, sent, kept, sent, slots_low],
        1,
        10,
        [
            pltpu.VMEM((EDGES, ENT // 2), BF16),
            pltpu.VMEM((D, EDGES), BF16),
            pltpu.VMEM((EDGES, D), BF16),
            pltpu.VMEM((EDGES, D), BF16),
        ],
        flops=9 * EDGES * ENT * D,
        bytes_accessed=1 << 23,
    )(counts, ids, near_second, far_second, head, rel_rows, prod, cnt, tails, neg, cc_first)
    src_recv = swap(src_send, CORE)
    dst_recv = swap(dst_send, CORE)
    rel_keep, rel_send = call(
        relation_kernel,
        [kept, sent],
        0,
        2,
        flops=2 * EDGES * NREL * D,
        bytes_accessed=1 << 21,
    )(ids, gr)

    rel_recv = swap(rel_send, CORE)
    src_own, src_away = add_split([src_keep, src_recv], 2, own=F32)
    dst_away, dst_own = add_split([dst_keep, dst_recv], 2)
    parts = add_split([rel_keep, rel_recv], 4, own=F32)
    recv = [swap(part, mask) for part, mask in zip(parts[1:], X_MASKS)]
    recv, dst_away, src_away = lax.optimization_barrier((recv, dst_away, src_away))
    dst_other = swap(dst_away, XL)
    src_other = swap(src_away, XL)
    (mine,) = add_split([parts[0], *recv], 1)

    landed = spread(mine.reshape(32, 8, D))
    dst_other, src_other = lax.optimization_barrier((dst_other, src_other))
    (dst_sum,) = add_split([dst_own, dst_other], 1)
    dst_total = shift(dst_sum, 1, XL)
    ent_own = sum_with_means([src_own, src_other, dst_total])
    landed, _, src_other = lax.optimization_barrier((landed, dst_sum, src_other))
    summed = sum_rows(landed)
    ent_xl = swap(ent_own, XL)
    total, ent_xl = lax.optimization_barrier((spread(summed), ent_xl))
    ent_core = [swap(ent_own, CORE), swap(ent_xl, CORE)]
    quarter = sum_with_means([total.reshape(256, D)])
    recv = [swap(quarter, mask) for mask in X_MASKS]
    pieces = [quarter, *recv]
    pieces = pieces + [swap(piece, CORE) for piece in pieces]
    place = jnp.stack([core * 2 + xl, core * 4 + x])
    return tuple(
        update(
            place,
            (entities, entity_acc, [ent_own, ent_xl, *ent_core]),
            (relations, relation_acc, pieces),
        )
    )


def solution(mesh):
    in_specs = (
        P("blk", None),
        P("blk"),
        P(),
        P(),
        P("blk", "rep"),
        P("blk", "rep"),
        P("blk", "rep"),
        P("blk", "rep"),
        P("blk", "rep"),
    )
    out_specs = (P("blk", None), P("blk"), P(), P())
    return jax.shard_map(shards, mesh=mesh, in_specs=in_specs, out_specs=out_specs, check_vma=False)
```

```python
import functools

import jax
import jax.numpy as jnp
from jax import lax
from jax.experimental import pallas as pl
from jax.experimental.pallas import tpu as pltpu
from jax.sharding import PartitionSpec as P

F32 = jnp.float32
BF16 = jnp.bfloat16
D = 256
H = 128
ENT = 2048
EDGES = 1024
GROUP = 256
NEG = 1024
NREL = 2048
RATE = 0.1
AXES = ("blk", "rep")
VMEM_LIMIT = 32 * 1024 * 1024
UPDATE_VMEM_LIMIT = 51 * 1024 * 1024
CHUNK = 256
UNROLL = 4


def vmem():
    return pl.BlockSpec(memory_space=pltpu.VMEM)


def smem():
    return pl.BlockSpec(memory_space=pltpu.SMEM)


def call(kernel, out_shape, n_smem, n_vmem, scratch=(), flops=0, bytes_accessed=0):
    return pl.pallas_call(
        kernel,
        out_shape=out_shape,
        in_specs=[smem()] * n_smem + [vmem()] * n_vmem,
        out_specs=jax.tree.map(lambda _: vmem(), out_shape),
        scratch_shapes=list(scratch),
        cost_estimate=pl.CostEstimate(
            flops=flops, bytes_accessed=bytes_accessed, transcendentals=0
        ),
        compiler_params=pltpu.CompilerParams(vmem_limit_bytes=VMEM_LIMIT),
    )


def columns(row):
    n = row.shape[1]
    parts = [
        jnp.transpose(jnp.broadcast_to(row[:, i : i + H], (H, H))) for i in range(0, n, H)
    ]
    return parts[0] if len(parts) == 1 else jnp.concatenate(parts, axis=0)


def one_hot_rows(col, n, base=0):
    e = col.shape[0]
    lane = lax.broadcasted_iota(jnp.int32, (e, H), 1)
    parts = [jnp.where(col == lane + (base + j), 1.0, 0.0).astype(BF16) for j in range(0, n, H)]
    return jnp.concatenate(parts, axis=1)


def one_hot_cols(row, n, base):
    e = row.shape[1]
    sub = lax.broadcasted_iota(jnp.int32, (n, e), 0) + base
    return jnp.where(jnp.broadcast_to(row, (n, e)) == sub, 1.0, 0.0).astype(BF16)


def dot(a, b):
    return jnp.dot(a, b, preferred_element_type=F32)


def dot_nt(a, b):
    return lax.dot_general(a, b, (((1,), (1,)), ((), ())), preferred_element_type=F32)


def gather_kernel(ids_ref, negs_ref, low_ref, rel_ref, head_ref, relrow_ref, prod_ref, cnt_ref, hi_ref, mid_ref, lo_ref):
    for r in range(0, NREL, 256):
        x = rel_ref[r : r + 256, :]
        for ref in (hi_ref, mid_ref, lo_ref):
            part = x.astype(BF16)
            ref[r : r + 256, :] = part
            x = x - part.astype(F32)

    def group(g, _):
        rows = pl.ds(pl.multiple_of(g * GROUP, GROUP), GROUP)
        src = columns(ids_ref[0:1, rows])
        heads = dot(one_hot_rows(src, ENT), low_ref[...])
        pick = one_hot_rows(columns(ids_ref[1:2, rows]), NREL)
        rel = dot(pick, hi_ref[...]) + dot(pick, mid_ref[...]) + dot(pick, lo_ref[...])
        hr, hi, rr, ri = heads[:, :H], heads[:, H:], rel[:, :H], rel[:, H:]
        head_ref[rows, :] = heads.astype(BF16)
        relrow_ref[rows, :] = rel
        prod_ref[rows, :H] = hr * rr - hi * ri
        prod_ref[rows, H:] = hr * ri + hi * rr
        negs = negs_ref[pl.ds(g, 1), :]
        high = one_hot_cols(lax.shift_right_logical(negs, 7), ENT // H, 0)
        low = one_hot_cols(lax.bitwise_and(negs, H - 1), H, 0)
        cnt_ref[g] = dot_nt(high, low) * (1.0 / NEG)
        return 0

    lax.fori_loop(0, EDGES // GROUP, group, 0, unroll=UNROLL)


def against(part, ids_ref, near_ref, far_ref, prod_ref, cnt_ref, cc_ref, rows, g):
    size = near_ref.shape[0]
    dst = columns(ids_ref[2:3, rows])
    low = prod_ref[rows, :].astype(BF16)
    tails = neg = None
    for j, table in ((0, near_ref), (1, far_ref)):
        base = j * (ENT // 2) + part * size
        tail = dot(one_hot_rows(dst, size, base), table[...])
        scores = dot_nt(low, table[...])
        for i in range(size // H):
            w = cnt_ref[g, base // H + i : base // H + i + 1, :]
            cc_ref[rows, j * size + i * H : j * size + (i + 1) * H] = (
                jax.nn.sigmoid(scores[:, i * H : (i + 1) * H]) * w
            ).astype(BF16)
        drawn = dot(cc_ref[rows, j * size : (j + 1) * size], table[...])
        tails = tail if tails is None else tails + tail
        neg = drawn if neg is None else neg + drawn
    return tails, neg


def first_score_kernel(ids_ref, near_ref, far_ref, prod_ref, cnt_ref, cc_ref, tails_ref, neg_ref):
    def group(g, _):
        rows = pl.ds(pl.multiple_of(g * GROUP, GROUP), GROUP)
        tails, neg = against(0, ids_ref, near_ref, far_ref, prod_ref, cnt_ref, cc_ref, rows, g)
        tails_ref[rows, :] = tails
        neg_ref[rows, :] = neg
        return 0

    lax.fori_loop(0, EDGES // GROUP, group, 0, unroll=UNROLL)


def score_kernel(
    count_ref,
    ids_ref,
    near_ref,
    far_ref,
    head_ref,
    relrow_ref,
    prod_ref,
    cnt_ref,
    tails_ref,
    neg_ref,
    first_ref,
    src_keep_ref,
    src_send_ref,
    dst_keep_ref,
    dst_send_ref,
    gr_ref,
    cc_ref,
    plt_ref,
    pd_ref,
    gh_ref,
):
    half = ENT // 2
    quarter = half // 2
    count = count_ref[0, 0]

    def group(g, _):
        rows = pl.ds(pl.multiple_of(g * GROUP, GROUP), GROUP)
        tails, neg = against(1, ids_ref, near_ref, far_ref, prod_ref, cnt_ref, cc_ref, rows, g)
        tails = tails + tails_ref[rows, :]
        neg = neg + neg_ref[rows, :]
        prod = prod_ref[rows, :]
        edge = lax.broadcasted_iota(jnp.int32, (GROUP, 1), 0) + g * GROUP
        live = jnp.where(edge < count, 1.0, 0.0).astype(F32)
        positive = jnp.sum(prod * tails, axis=1, keepdims=True)
        pos = -live * jax.nn.sigmoid(-positive)
        grad = pos * tails + live * neg
        rel = relrow_ref[rows, :]
        head = head_ref[rows, :].astype(F32)
        gr, gi = grad[:, :H], grad[:, H:]
        for out, other in ((gh_ref, rel), (gr_ref, head)):
            a, b = other[:, :H], other[:, H:]
            out[rows, :H] = (gr * a + gi * b).astype(BF16)
            out[rows, H:] = (gi * a - gr * b).astype(BF16)
        pd_ref[rows, :] = (pos * prod).astype(BF16)
        plt_ref[:, rows] = jnp.transpose(live * prod).astype(BF16)
        return 0

    lax.fori_loop(0, EDGES // GROUP, group, 0, unroll=UNROLL)

    for part, ref in ((0, first_ref), (1, cc_ref)):
        for i in range(quarter // CHUNK):
            at = part * quarter + i * CHUNK
            rows = slice(at, at + CHUNK)
            for j, src_ref, dst_ref in (
                (0, src_keep_ref, dst_keep_ref),
                (1, src_send_ref, dst_send_ref),
            ):
                src = dot(one_hot_cols(ids_ref[4:5, :], CHUNK, j * half + at), gh_ref[...])
                src_ref[rows, :] = src.astype(src_ref.dtype)
                cols = slice(j * quarter + i * CHUNK, j * quarter + (i + 1) * CHUNK)
                drawn = jnp.transpose(dot(plt_ref[...], ref[:, cols]))
                dst = dot(one_hot_cols(ids_ref[2:3, :], CHUNK, j * half + at), pd_ref[...])
                dst_ref[rows, :] = (drawn + dst).astype(dst_ref.dtype)


def relation_kernel(ids_ref, gr_ref, keep_ref, send_ref):
    half = NREL // 2
    for i in range(half // CHUNK):
        rows = slice(i * CHUNK, (i + 1) * CHUNK)
        keep_ref[rows, :] = dot(one_hot_cols(ids_ref[3:4, :], CHUNK, i * CHUNK), gr_ref[...])
        send_ref[rows, :] = dot(
            one_hot_cols(ids_ref[3:4, :], CHUNK, half + i * CHUNK), gr_ref[...]
        ).astype(BF16)


def add_split_kernel(n_in, n_out, *refs):
    ins, outs = refs[:n_in], refs[n_in:]
    size = outs[0].shape[0]
    step = min(size, 64)
    for k, out in enumerate(outs):
        for r in range(0, size, step):
            total = ins[0][k * size + r : k * size + r + step, :].astype(F32)
            for ref in ins[1:]:
                total = total + ref[k * size + r : k * size + r + step, :].astype(F32)
            out[r : r + step, :] = total.astype(out.dtype)


def add_split(parts, n_out, own=BF16, sent=BF16):
    rows = parts[0].shape[0] // n_out
    shapes = [jax.ShapeDtypeStruct((rows, D), sent if k else own) for k in range(n_out)]
    return call(
        functools.partial(add_split_kernel, len(parts), n_out),
        shapes,
        0,
        len(parts),
        flops=len(parts) * n_out * rows * D,
        bytes_accessed=3 * len(parts) * n_out * rows * D,
    )(*parts)


def split3(x):
    hi = x.astype(BF16).astype(F32)
    mid = (x - hi).astype(BF16).astype(F32)
    return hi, mid, x - hi - mid


def sum_with_means_kernel(*refs):
    parts, out_ref = refs[:-1], refs[-1]
    rows = parts[0].shape[0]
    means = []
    for r in range(0, rows, H):
        total = parts[0][r : r + H, :].astype(F32)
        for ref in parts[1:]:
            total = total + ref[r : r + H, :].astype(F32)
        out_ref[r : r + H, :] = total.astype(BF16)
        mean = jnp.sum(total * total, axis=1, keepdims=True) * (1.0 / D)
        means.append(jnp.transpose(jnp.broadcast_to(mean, (H, H)))[0:1, :])
    means.append(jnp.zeros((8 - len(means), H), F32))
    hi, mid, lo = split3(jnp.concatenate(means, axis=0))
    top = jnp.concatenate([hi, mid], axis=1)
    bottom = jnp.concatenate([lo, jnp.zeros_like(lo)], axis=1)
    out_ref[rows : rows + 16, :] = jnp.concatenate([top, bottom], axis=0).astype(BF16)


def sum_with_means(parts):
    rows = parts[0].shape[0]
    return call(
        sum_with_means_kernel,
        jax.ShapeDtypeStruct((rows + 16, D), BF16),
        0,
        len(parts),
        flops=len(parts) * rows * D,
        bytes_accessed=3 * len(parts) * rows * D,
    )(*parts)


def means_of(piece, start, row):
    tile = piece[start : start + 16, :].astype(F32)
    return tile[row : row + 1, :H] + tile[row : row + 1, H:] + tile[8 + row : 9 + row, :H]


def update_kernel(counts, place_ref, *refs):
    tables = len(counts)
    n_in = 2 * tables + sum(counts)
    ins, outs = refs[:n_in], refs[n_in : n_in + 2 * tables]
    in_sem, out_sem, *bufs = refs[n_in + 2 * tables :]
    held, bufs = bufs[:tables], bufs[tables:]
    fetches = []
    for t, n in enumerate(counts):
        rows_ref = ins[2 * t + sum(counts[:t])]
        size = rows_ref.shape[0] // n
        for k in range(n):
            i = lax.bitwise_xor(k, place_ref[t])
            rows = pl.ds(pl.multiple_of(i * size, size), size)
            fetch = pltpu.make_async_copy(
                rows_ref.at[rows, :], held[t].at[rows, :], in_sem.at[len(fetches)]
            )
            fetch.start()
            fetches.append(fetch)
    copies = []
    for t, n in enumerate(counts):
        rows_ref, acc_ref, *rest = ins
        pieces, ins = rest[:n], rest[n:]
        new_ref, new_acc_ref = outs[2 * t : 2 * t + 2]
        size = rows_ref.shape[0] // n
        for k, piece in enumerate(pieces):
            i = lax.bitwise_xor(k, place_ref[t])
            fetches[len(copies)].wait()
            for r in range(0, size, H):
                g = piece[r : r + H, :].astype(F32)
                at = pl.ds(i * (size // H) + r // H, 1)
                acc = acc_ref[at, :] + means_of(piece, size, r // H)
                new_acc_ref[at, :] = acc
                scale = jnp.transpose(jnp.broadcast_to(RATE / jnp.sqrt(acc), (H, H)))
                rows = pl.ds(pl.multiple_of(i * size + r, H), H)
                bufs[t][rows, :H] = held[t][rows, :H] - g[:, :H] * scale
                bufs[t][rows, H:] = held[t][rows, H:] - g[:, H:] * scale
            rows = pl.ds(pl.multiple_of(i * size, size), size)
            copy = pltpu.make_async_copy(
                bufs[t].at[rows, :], new_ref.at[rows, :], out_sem.at[len(copies)]
            )
            copy.start()
            copies.append(copy)
    for copy in copies:
        copy.wait()


def update(place, *tables):
    counts = tuple(len(pieces) for _, _, pieces in tables)
    operands, shapes, bufs, specs = [], [], [], []
    for rows, acc, pieces in tables:
        n = rows.shape[0]
        operands += [rows, acc.reshape(n // H, H), *pieces]
        specs += [pl.BlockSpec(memory_space=pl.ANY)] + [vmem()] * (1 + len(pieces))
        shapes += [
            jax.ShapeDtypeStruct((n, D), F32),
            jax.ShapeDtypeStruct((n // H, H), F32),
        ]
        bufs.append(pltpu.VMEM((n, D), F32))
    outs = pl.pallas_call(
        functools.partial(update_kernel, counts),
        out_shape=shapes,
        in_specs=[smem()] + specs,
        out_specs=[pl.BlockSpec(memory_space=pl.ANY), vmem()] * len(tables),
        scratch_shapes=[pltpu.SemaphoreType.DMA((sum(counts),))] * 2 + bufs * 2,
        cost_estimate=pl.CostEstimate(
            flops=16 * ENT * D, bytes_accessed=20 * ENT * D, transcendentals=2 * ENT
        ),
        compiler_params=pltpu.CompilerParams(vmem_limit_bytes=UPDATE_VMEM_LIMIT),
    )(place, *operands)
    return [out.reshape(-1) if out.shape[1] == H else out for out in outs]


def sum_rows_kernel(parts_ref, out_ref):
    total = parts_ref[0].astype(F32)
    for k in range(1, parts_ref.shape[0]):
        total = total + parts_ref[k].astype(F32)
    out_ref[...] = jnp.broadcast_to(total, out_ref.shape)


def sum_rows(parts):
    return call(
        sum_rows_kernel,
        jax.ShapeDtypeStruct(parts.shape, F32),
        0,
        1,
        flops=parts.size,
        bytes_accessed=6 * parts.size,
    )(parts)


def spread(parts):
    groups = [[2 * k + hi for k in range(32)] for hi in range(2)]
    return lax.all_to_all(parts, "blk", 0, 0, axis_index_groups=groups, tiled=True)


def swap(x, mask):
    return lax.ppermute(x, AXES, [(i, i ^ mask) for i in range(256)])


def shift(x, distance, mask):
    route = [(((i // 4 - distance) % 64) * 4 + ((i % 4) ^ mask), i) for i in range(256)]
    return lax.ppermute(x, AXES, route)


CORE, XL = 1, 2
X_MASKS = (2, 4, 6)


def shards(
    entities, entity_acc, relations, relation_acc, src_ids, rel_ids, dst_ids, neg_ids, counts
):
    blk, rep = lax.axis_index("blk"), lax.axis_index("rep")
    core, xl = rep % 2, rep // 2
    x = (blk % 2) * 2 + xl

    low = entities.astype(BF16)
    quarter = lax.dynamic_slice_in_dim(entities, core * 1024 + (1 - xl) * 512, 512, 0)
    near_first = shift(quarter.astype(BF16), -1, XL)

    ids = jnp.concatenate(
        [
            src_ids,
            rel_ids,
            dst_ids ^ (core * 1024 + xl * 512),
            rel_ids ^ (core * 1024 + x * 256),
            src_ids ^ (core * 1024 + xl * 512),
            jnp.zeros((3, EDGES), jnp.int32),
        ],
        axis=0,
    )
    negs = (neg_ids ^ (core * 1024 + xl * 512)).reshape(4, NEG)
    head, rel_rows, prod, cnt = call(
        gather_kernel,
        [
            jax.ShapeDtypeStruct((EDGES, D), BF16),
            jax.ShapeDtypeStruct((EDGES, D), F32),
            jax.ShapeDtypeStruct((EDGES, D), F32),
            jax.ShapeDtypeStruct((4, ENT // H, H), F32),
        ],
        0,
        4,
        [pltpu.VMEM((NREL, D), BF16)] * 3,
        flops=4 * 2 * EDGES * ENT * D,
        bytes_accessed=1 << 22,
    )(ids, negs, low, relations)

    kept = jax.ShapeDtypeStruct((ENT // 2, D), F32)
    sent = jax.ShapeDtypeStruct((ENT // 2, D), BF16)
    slots = jax.ShapeDtypeStruct((EDGES, D), F32)
    slots_low = jax.ShapeDtypeStruct((EDGES, D), BF16)
    weights = jax.ShapeDtypeStruct((EDGES, ENT // 2), BF16)
    near_first, head = lax.optimization_barrier((near_first, head))
    near_second = swap(near_first, XL)
    far_first = swap(near_first, CORE)
    cc_first, tails, neg = call(
        first_score_kernel,
        [weights, slots, slots],
        0,
        5,
        flops=3 * EDGES * ENT * D,
        bytes_accessed=1 << 22,
    )(ids, near_first, far_first, prod, cnt)
    near_second, tails = lax.optimization_barrier((near_second, tails))
    far_second = swap(near_second, CORE)
    src_keep, src_send, dst_keep, dst_send, gr = call(
        score_kernel,
        [kept, sent, kept, sent, slots_low],
        1,
        10,
        [
            pltpu.VMEM((EDGES, ENT // 2), BF16),
            pltpu.VMEM((D, EDGES), BF16),
            pltpu.VMEM((EDGES, D), BF16),
            pltpu.VMEM((EDGES, D), BF16),
        ],
        flops=9 * EDGES * ENT * D,
        bytes_accessed=1 << 23,
    )(counts, ids, near_second, far_second, head, rel_rows, prod, cnt, tails, neg, cc_first)
    src_recv = swap(src_send, CORE)
    dst_recv = swap(dst_send, CORE)
    rel_keep, rel_send = call(
        relation_kernel,
        [kept, sent],
        0,
        2,
        flops=2 * EDGES * NREL * D,
        bytes_accessed=1 << 21,
    )(ids, gr)

    rel_recv = swap(rel_send, CORE)
    src_own, src_away = add_split([src_keep, src_recv], 2, own=F32)
    dst_away, dst_own = add_split([dst_keep, dst_recv], 2)
    parts = add_split([rel_keep, rel_recv], 4, own=F32)
    recv = [swap(parts[k], X_MASKS[k - 1]) for k in (2, 1, 3)]
    recv, dst_away, src_away = lax.optimization_barrier((recv, dst_away, src_away))
    dst_other = swap(dst_away, XL)
    src_other = swap(src_away, XL)
    (mine,) = add_split([parts[0], *recv], 1)

    landed = spread(mine.reshape(32, 8, D))
    dst_other, src_other = lax.optimization_barrier((dst_other, src_other))
    (dst_sum,) = add_split([dst_own, dst_other], 1)
    dst_total = shift(dst_sum, 1, XL)
    ent_own = sum_with_means([src_own, src_other, dst_total])
    landed, _, src_other = lax.optimization_barrier((landed, dst_sum, src_other))
    summed = sum_rows(landed)
    ent_xl = swap(ent_own, XL)
    total, ent_xl = lax.optimization_barrier((spread(summed), ent_xl))
    ent_core = [swap(ent_own, CORE), swap(ent_xl, CORE)]
    quarter = sum_with_means([total.reshape(256, D)])
    recv = [swap(quarter, mask) for mask in X_MASKS]
    pieces = [quarter, *recv]
    pieces = pieces + [swap(piece, CORE) for piece in pieces]
    place = jnp.stack([core * 2 + xl, core * 4 + x])
    return tuple(
        update(
            place,
            (entities, entity_acc, [ent_own, ent_xl, *ent_core]),
            (relations, relation_acc, pieces),
        )
    )


def solution(mesh):
    in_specs = (
        P("blk", None),
        P("blk"),
        P(),
        P(),
        P("blk", "rep"),
        P("blk", "rep"),
        P("blk", "rep"),
        P("blk", "rep"),
        P("blk", "rep"),
    )
    out_specs = (P("blk", None), P("blk"), P(), P())
    return jax.shard_map(shards, mesh=mesh, in_specs=in_specs, out_specs=out_specs, check_vma=False)
```
